32 devices in a mesh: experts: 4 (over y, x), context: 4 (over z), dp: 2 (over core).
Axes of the slice: x: 2, y: 2, z: 4, core: 2. Of those that a mesh axis runs over, the one named last changes fastest.
Arguments:
- inputs: bfloat16 [2, 8, 1024, 768], P(None, ('experts', 'dp'), 'context'), may hold values from -6 to 6
- cotangent: bfloat16 [2, 8, 1024, 768], P(None, ('experts', 'dp'), 'context'), may hold values from -6 to 6
- qkv_weight: bfloat16 [3, 768, 768], P(None, ('context', 'dp')), may hold values from -0.21875 to 0.21875
- out_weight: bfloat16 [768, 768], P(('context', 'dp')), may hold values from -0.875 to 0.875
- norm_gains: float32 [2, 768], P(None, ('context', 'dp')), may hold values from 0.5 to 1.5
- route_weight: bfloat16 [768, 8], P(('context', 'dp')), may hold values from -0.109375 to 0.109375
- const_gate: bfloat16 [768, 4], P(('context', 'dp')), may hold values from -0.21875 to 0.21875
- const_vec: float32 [2, 768], P(None, ('context', 'dp')), may hold values from -6 to 6
- w_gate: bfloat16 [4, 768, 2048], P('experts', None, ('context', 'dp')), may hold values from -0.3125 to 0.3125
- w_up: bfloat16 [4, 768, 2048], P('experts', None, ('context', 'dp')), may hold values from -0.3125 to 0.3125
- w_down: bfloat16 [4, 768, 2048], P('experts', None, ('context', 'dp')), may hold values from -0.375 to 0.375
- prev_logits: float32 [2, 8, 1024, 8], P(None, ('experts', 'dp'), 'context'), may hold values from -3 to 3
- routes: int32 [2, 8, 1024, 2], P(None, ('experts', 'dp'), 'context'), may hold values from 0 to 7, all different within a row; in each aligned block of 256 rows (0 to 255, 256 to 511, ..., all dimensions but the last counted through in order) at most 80 rows name the same one
- segments: int32 [2, 8, 1024], P(None, ('experts', 'dp'), 'context'), may hold values from 0 to 6, as said below
Outputs:
- output: bfloat16 [2, 8, 1024, 768], P(None, ('experts', 'dp'), 'context')
- input_grad: float32 [2, 8, 1024, 768], P(None, ('experts', 'dp'), 'context')
- logit_grad: float32 [2, 8, 1024, 8], P(None, ('experts', 'dp'), 'context')
- qkv_grad: float32 [3, 768, 768], P(None, ('context', 'dp'))
- out_proj_grad: float32 [768, 768], P(('context', 'dp'))
- gain_grad: float32 [2, 768], P(None, ('context', 'dp'))
- route_grad: float32 [768, 8], P(('context', 'dp'))
- const_gate_grad: float32 [768, 4], P(('context', 'dp'))
- const_vec_grad: float32 [2, 768], P(None, ('context', 'dp'))
- gate_grad: float32 [4, 768, 2048], P('experts', None, ('context', 'dp'))
- up_grad: float32 [4, 768, 2048], P('experts', None, ('context', 'dp'))
- down_grad: float32 [4, 768, 2048], P('experts', None, ('context', 'dp'))
The draws below stay inside these ranges and needn't reach their ends.
Inputs may be any that keep to these rules, and one draw needn't show every extreme that they name: `routes`: each row names two different experts; within the 256 positions of one sequence block, no expert is named more than 80 times. `segments`: never fall along a sequence.
All inputs are finite; a program needn't handle non-finite values.
Results may differ from the reference program's by a relative error of at most 0.039.
Values may be sent and summed in bfloat16 or wider, within the bound.
No kernel may reach another device: no remote copies, remote signals or barrier semaphores. Data moves between devices by JAX's collectives and lax.ppermute only.
A program may use at most 192 MiB of HBM per device.

```python
import math
import jax
import jax.numpy as jnp
import numpy as np
from jax import lax

D = 768
HEAD_DIM = 64
FF = 2048
MICRO = 2
EXPERTS = 4
ROUTED = 8
SEQ_LEN = 1024
TOK_DEV = 256
CAP = 80
SEQS = 8


def draw_segments(key, part):
    key = jax.random.fold_in(key, 7)
    keys_split = jax.random.split(key, 4)
    shape_head = (MICRO, SEQS, 1)
    start_cut = jax.random.randint(keys_split[0], shape_head, 1, TOK_DEV)
    end_cut = SEQ_LEN - jax.random.randint(keys_split[1], shape_head, 1, TOK_DEV)
    early_cuts = jax.random.randint(keys_split[2], (MICRO, SEQS, 2), 1, start_cut + 1)
    late_cuts = jax.random.randint(keys_split[3], (MICRO, SEQS, 2), end_cut, SEQ_LEN)
    all_cuts = jnp.concatenate([start_cut, end_cut, early_cuts, late_cuts], axis=-1)
    positions = jnp.arange(SEQ_LEN, dtype=jnp.int32)
    return jnp.sum((positions[None, None, :, None] >= all_cuts[:, :, None, :]).astype(jnp.int32), axis=-1)


def levels(key, extent, shards, smallest, largest):
    gain, own = 1.0, jax.random.fold_in(key, 6)
    for position, shards_of in shards:
        steps = jnp.exp(jax.random.uniform(jax.random.fold_in(own, position), (shards_of,), jnp.float32, smallest / len(shards), largest / len(shards)))
        gain = gain * jnp.repeat(steps, extent[position] // shards_of).reshape([-1 if axis == position else 1 for axis in range(len(extent))])
    return gain


def shared_out(rng, own, number, rows, number_of, top, bound, skew):
    order = jax.random.permutation(rng, number_of)
    packed, common = shares(number_of, rows * top, bound, skew, True), shares(number_of, rows * top, bound, skew, False)
    places = jnp.arange(number_of)

    def named(sizes, offset_by):
        used = int((sizes > 0).sum())
        fixed = max(1, used // 4)
        passed = fixed + (places - fixed + offset_by * (used - fixed)) % max(1, number_of - fixed)
        return jnp.zeros((number_of,), jnp.int32).at[order[jnp.where(places < fixed, places, passed)]].set(jnp.asarray(sizes, jnp.int32))

    sizes = jnp.where(number % 4 == 0, named(packed, number // 4), named(common, number - number // 4 - 1))
    mixed = jax.random.permutation(jax.random.fold_in(own, 3), number_of)
    donor, receiver = mixed[0:number_of // 2 * 2:2], mixed[1:number_of // 2 * 2:2]
    slack = jnp.minimum(sizes[donor] - 1, bound - sizes[receiver]) // 2
    slack = jnp.where((donor == order[0]) | (receiver == order[0]) | (sizes[receiver] == 0), 0, jnp.maximum(slack, 0))
    passed = jax.random.randint(jax.random.fold_in(own, 4), (number_of // 2,), 0, 1 << 20) % (slack + 1)
    sizes = sizes.at[donor].add(-passed).at[receiver].add(passed)
    labels = jnp.searchsorted(jnp.cumsum(sizes), jnp.arange(rows * top), side="right").astype(jnp.int32)
    table = labels.reshape(top, rows).T
    table = table[jax.random.permutation(jax.random.fold_in(own, 1), rows)]
    offset_by = jax.random.randint(jax.random.fold_in(own, 2), (rows, 1), 0, top)
    return jnp.take_along_axis(table, (jnp.arange(top)[None, :] + offset_by) % top, axis=1)


def shares(number_of, total, limit, slope, full):
    portions = [(1 << 20) // math.isqrt(standing ** slope) + 1 for standing in range(1, number_of + 1)]
    largest = limit if full else min(limit, max(-(-total // number_of), total * portions[0] // sum(portions)))
    least = 1 if total - largest >= number_of - 1 else 0
    counts, surplus = [largest] + [least] * (number_of - 1), total - largest - least * (number_of - 1)
    while surplus > 0:
        movable = [i for i in range(1, number_of) if counts[i] < largest] or [i for i in range(1, number_of) if counts[i] < limit]
        mass, remaining = sum([portions[i] for i in movable]), surplus
        for i in movable:
            more = min(limit - counts[i], max(1, remaining * portions[i] // mass), surplus)
            counts[i] = counts[i] + more
            surplus = surplus - more
    return np.array(counts)


def normal_values(rng, extent, width, most, cuts=(), kind=jnp.bfloat16):
    drawn = jax.random.normal(rng, extent, jnp.float32) * width
    if len(cuts) > 0:
        drawn = levels(rng, extent, cuts, -0.22, 0.18) * drawn
    return jnp.clip(drawn, min=-most, max=most).astype(kind)


def setup_inputs(seed: int = 0) -> dict:
    seeds = jax.random.split(jax.random.key(seed), 15)
    inputs = normal_values(seeds[0], (MICRO, SEQS, SEQ_LEN, D), 1.0, 6.0, ((1, 8), (2, 4)))
    cotangent = normal_values(seeds[1], (MICRO, SEQS, SEQ_LEN, D), 1.0, 6.0, ((1, 8), (2, 4)))
    qkv_weight = normal_values(seeds[2], (3, D, D), D ** -0.5, 0.21875, ((1, 8),))
    out_weight = normal_values(seeds[3], (D, D), (D // 16) ** -0.5, 0.875, ((0, 8),))
    norm_gains = jnp.clip(1.0 + 0.1 * jax.random.normal(seeds[4], (2, D), jnp.float32), 0.5, 1.5)
    route_weight = normal_values(seeds[5], (D, ROUTED), (4 * D) ** -0.5, 0.109375, ((0, 8),))
    const_gate = normal_values(seeds[6], (D, 4), D ** -0.5, 0.21875, ((0, 8),))
    const_vec = normal_values(seeds[7], (2, D), 1.0, 6.0, ((1, 8),), jnp.float32)
    w_gate = normal_values(seeds[8], (EXPERTS, D, FF), (D // 2) ** -0.5, 0.3125, ((0, 4), (2, 8)))
    w_up = normal_values(seeds[9], (EXPERTS, D, FF), (D // 2) ** -0.5, 0.3125, ((0, 4), (2, 8)))
    w_down = normal_values(seeds[10], (EXPERTS, D, FF), (FF // 8) ** -0.5, 0.375, ((0, 4), (2, 8)))
    prev_logits = normal_values(seeds[11], (MICRO, SEQS, SEQ_LEN, ROUTED), 0.5, 3.0, ((1, 8), (2, 4)), jnp.float32)
    routes_keys = jax.random.split(jax.random.fold_in(seeds[12], 1), MICRO * SEQS * SEQ_LEN // TOK_DEV)
    routes_turns = jax.random.permutation(jax.random.fold_in(seeds[12], 3), MICRO * SEQS * SEQ_LEN // TOK_DEV)
    routes = jax.vmap(lambda own, number: shared_out(jax.random.fold_in(seeds[12], 2), own, number, TOK_DEV, ROUTED, 2, CAP, 1))(routes_keys, routes_turns).reshape((MICRO, SEQS, SEQ_LEN, 2))
    segments = draw_segments(jax.random.fold_in(seeds[14], 71), 0)
    return {"inputs": inputs, "cotangent": cotangent, "qkv_weight": qkv_weight, "out_weight": out_weight, "norm_gains": norm_gains, "route_weight": route_weight, "const_gate": const_gate, "const_vec": const_vec, "w_gate": w_gate, "w_up": w_up, "w_down": w_down, "prev_logits": prev_logits, "routes": routes, "segments": segments}


EPSILON = 1e-05
MASKED = -1e+30

@jax.custom_vjp
def low(v):
    return lax.optimization_barrier(v.astype(jnp.bfloat16)).astype(jnp.float32)

@jax.custom_vjp
def low_back(v):
    return v

def low_keep(v):
    return (low(v), None)

def low_pass(kept, grad):
    return (grad,)

def back_keep(v):
    return (v, None)

def back_low(kept, grad):
    return (low(grad),)
low.defvjp(low_keep, low_pass)
low_back.defvjp(back_keep, back_low)

def matmul(left_matrix, right_matrix):
    return jnp.dot(left_matrix, right_matrix, precision=lax.Precision.HIGHEST, preferred_element_type=jnp.float32)

def rms_norm(values, gain_vec):
    return values * lax.rsqrt(lax.optimization_barrier(jnp.mean(values * values, axis=-1, keepdims=True)) + EPSILON) * gain_vec

def softmax_last(logits):
    shifted = jnp.exp(logits - lax.optimization_barrier(jnp.max(logits, axis=-1, keepdims=True)))
    return shifted / lax.optimization_barrier(jnp.sum(shifted, axis=-1, keepdims=True))

def rotate(values, positions, direction):
    half_dim = values.shape[-1] // 2
    inverse = 10000.0 ** (-jnp.arange(half_dim, dtype=jnp.float32) / half_dim)
    angles = positions.astype(jnp.float32)[:, None] * inverse[None, :]
    cosine = jnp.cos(angles)[:, None, :]
    sine_part = jnp.sin(angles)[:, None, :]
    first_half = values[..., :half_dim]
    second = values[..., half_dim:]
    return jnp.concatenate([first_half * cosine - direction * second * sine_part, second * cosine + direction * first_half * sine_part], axis=-1)

def attend_sequence(operands):
    queries, key_rows, value_rows, segment = operands
    length = queries.shape[0]
    head_count = queries.shape[1]
    block_rows = math.gcd(length, 512)
    block_count = length // block_rows
    score_scale = queries.shape[-1] ** (-0.5)
    key_positions = jnp.arange(length, dtype=jnp.int32)

    @jax.checkpoint
    def one_block(block_parts):
        query_block, segment_block, position_block = block_parts
        scores = jnp.einsum('qhd,khd->hqk', query_block, key_rows, precision=lax.Precision.HIGHEST) * score_scale
        scores = low_back(scores)
        allowed = (segment_block[:, None] == segment[None, :]) & (key_positions[None, :] <= position_block[:, None])
        scores = jnp.where(allowed[None], scores, MASKED)
        weights = low(softmax_last(scores))
        return jnp.einsum('hqk,khd->qhd', weights, value_rows, precision=lax.Precision.HIGHEST)
    outputs = lax.map(one_block, (queries.reshape(block_count, block_rows, head_count, queries.shape[-1]), segment.reshape(block_count, block_rows), key_positions.reshape(block_count, block_rows)))
    return outputs.reshape(queries.shape)

def forward(inputs, qkv_weight, out_weight, norm_gains, route_weight, const_gate, const_vec, w_gate, w_up, w_down, prev_logits, routes, segments):
    micro_count, seq_count, length, model_width = inputs.shape
    head_count = model_width // HEAD_DIM
    tokens = micro_count * seq_count * length
    flat_rows = inputs.reshape(tokens, model_width)
    normed_in = low(rms_norm(flat_rows, norm_gains[0]))
    projected = jnp.einsum('nd,cde->cne', normed_in, qkv_weight, precision=lax.Precision.HIGHEST)
    positions = jnp.arange(length, dtype=jnp.int32)
    head_shape = (micro_count * seq_count, length, head_count, HEAD_DIM)
    queries = low(rotate(low_back(projected[0]).reshape(head_shape), positions, 1.0))
    key_rows = low(rotate(low_back(projected[1]).reshape(head_shape), positions, 1.0))
    value_rows = low(low_back(projected[2])).reshape(head_shape)
    attended = lax.map(jax.checkpoint(attend_sequence), (queries, key_rows, value_rows, segments.reshape(micro_count * seq_count, length)))
    attended = low(low_back(attended.reshape(tokens, model_width)))
    hidden = flat_rows + low_back(matmul(attended, out_weight))
    normed = rms_norm(hidden, norm_gains[1])
    normed_low = low(normed)
    logits = matmul(normed_low, route_weight) + prev_logits.reshape(tokens, prev_logits.shape[-1])
    probabilities = softmax_last(logits)
    route_flat = routes.reshape(tokens, 2)
    gate_values = jnp.take_along_axis(probabilities, route_flat, axis=-1)
    experts = w_gate.shape[0]
    route_ids = route_flat.reshape(-1)
    routed_ffn = route_ids < experts
    onehot = (route_ids[:, None] == jnp.arange(experts, dtype=jnp.int32)[None, :]).astype(jnp.int32)
    slot_index = lax.optimization_barrier(jnp.sum((jnp.cumsum(onehot, axis=0) - onehot) * onehot, axis=-1))
    buffer = tokens // TOK_DEV * CAP
    slot_table = jnp.full((experts, buffer), tokens, jnp.int32).at[jnp.where(routed_ffn, route_ids, experts), slot_index].set(jnp.arange(2 * tokens, dtype=jnp.int32) // 2, mode='drop')
    padded = jnp.concatenate([normed_low, jnp.zeros((1, model_width), jnp.float32)], axis=0)

    def run_expert(block_parts):
        row_index, gate_matrix, up_matrix, down_matrix = block_parts
        entry_rows = low_back(padded[row_index])
        gate_act = low_back(matmul(entry_rows, gate_matrix))
        up_act = low_back(matmul(entry_rows, up_matrix))
        inner_act = low(jax.nn.silu(gate_act) * up_act)
        return low(low_back(matmul(inner_act, down_matrix.T)))
    returned = lax.map(jax.checkpoint(run_expert), (slot_table, w_gate, w_up, w_down)).reshape(experts * buffer, model_width)
    pick_index = jnp.where(routed_ffn, route_ids * buffer + slot_index, 0)
    expert_out = jnp.where(routed_ffn[:, None], returned[pick_index], 0.0).reshape(tokens, 2, model_width)
    const_mix = softmax_last(matmul(normed_low, const_gate).reshape(tokens, 2, 2))
    const_out = const_mix[:, :, 0:1] * normed[:, None, :] + const_mix[:, :, 1:2] * const_vec[None, :, :]
    copy_mask = (route_flat == experts + 1).astype(jnp.float32)
    const_pick = (route_flat[:, :, None] == experts + 2 + jnp.arange(2, dtype=jnp.int32)[None, None, :]).astype(jnp.float32)
    branch = expert_out + copy_mask[:, :, None] * normed[:, None, :] + jnp.einsum('njc,ncd->njd', const_pick, const_out, precision=lax.Precision.HIGHEST)
    output = hidden + lax.optimization_barrier(jnp.sum(gate_values[:, :, None] * branch, axis=1))
    return output.reshape(inputs.shape)

def reference(inputs, cotangent, qkv_weight, out_weight, norm_gains, route_weight, const_gate, const_vec, w_gate, w_up, w_down, prev_logits, routes, segments):

    def wrapped(inputs_f, qkv_f, out_f, gains_f, route_f, mixer_f, vec_f, gate_f, up_f, down_f, logits_f):
        return forward(inputs_f, qkv_f, out_f, gains_f, route_f, mixer_f, vec_f, gate_f, up_f, down_f, logits_f, routes, segments)
    output, pullback = jax.vjp(wrapped, inputs.astype(jnp.float32), qkv_weight.astype(jnp.float32), out_weight.astype(jnp.float32), norm_gains.astype(jnp.float32), route_weight.astype(jnp.float32), const_gate.astype(jnp.float32), const_vec.astype(jnp.float32), w_gate.astype(jnp.float32), w_up.astype(jnp.float32), w_down.astype(jnp.float32), prev_logits.astype(jnp.float32))
    gradients = pullback(cotangent.astype(jnp.float32))
    return (output.astype(jnp.bfloat16), gradients[0], gradients[10], gradients[1], gradients[2], gradients[3], gradients[4], gradients[5], gradients[6], gradients[7], gradients[8], gradients[9])
```

```python
import functools
import math

import jax
import jax.numpy as jnp
import numpy as np
from jax import lax
from jax.experimental import pallas as pl
from jax.experimental.pallas import tpu as pltpu
from jax.sharding import PartitionSpec as P

HEAD_DIM = 64
FF = 2048


EPSILON = 1e-05
MASKED = -1e30


def rotate(values, positions, direction):
    half_dim = values.shape[-1] // 2
    inverse = 10000.0 ** (-jnp.arange(half_dim, dtype=jnp.float32) / half_dim)
    angles = positions.astype(jnp.float32)[:, None] * inverse[None, :]
    cosine = jnp.cos(angles)[:, None, :]
    sine_part = jnp.sin(angles)[:, None, :]
    first_half = values[..., :half_dim]
    second = values[..., half_dim:]
    return jnp.concatenate(
        [
            first_half * cosine - direction * second * sine_part,
            second * cosine + direction * first_half * sine_part,
        ],
        axis=-1,
    )


def softmax_last(logits):
    shifted = jnp.exp(logits - jnp.max(logits, axis=-1, keepdims=True))
    return shifted / jnp.sum(shifted, axis=-1, keepdims=True)


def norm_scale(values):
    return lax.rsqrt(jnp.mean(values * values, axis=-1, keepdims=True) + EPSILON)


def norm_back(grad_in, values, factor, gain_vec):
    scaled = grad_in * gain_vec
    grad_gain = jnp.sum(grad_in * values * factor, axis=0)
    grad_values = factor * scaled - values * factor * factor * factor * jnp.mean(
        scaled * values, axis=-1, keepdims=True
    )
    return (grad_values, grad_gain)


def masked_scores(
    queries, key_rows, query_segments, key_segments, query_positions, key_positions, score_scale
):
    scores = (
        jnp.einsum("qhd,khd->hqk", queries, key_rows, preferred_element_type=jnp.float32)
        * score_scale
    )
    allowed = (query_segments[:, None] == key_segments[None, :]) & (
        key_positions[None, :] <= query_positions[:, None]
    )
    return (jnp.where(allowed[None], scores, MASKED), allowed)


def general_local(
    inputs,
    cotangent,
    qkv_weight,
    out_weight,
    norm_gains,
    route_weight,
    const_gate,
    const_vec,
    w_gate,
    w_up,
    w_down,
    prev_logits,
    routes,
    segments,
):
    micro_count = inputs.shape[0]
    row_count = inputs.shape[2]
    model_width = inputs.shape[3]
    head_count = model_width // HEAD_DIM
    score_scale = HEAD_DIM ** (-0.5)
    local_experts = w_gate.shape[0]
    experts = local_experts * lax.axis_size("experts")
    capacity = row_count * 5 // 16
    routed = prev_logits.shape[3]
    assigned = 2 * row_count
    head_shape = (row_count, head_count, HEAD_DIM)
    positions = lax.axis_index("context") * row_count + jnp.arange(row_count, dtype=jnp.int32)
    grad_qkv = jnp.zeros((3, model_width, model_width), jnp.float32)
    grad_out = jnp.zeros((model_width, model_width), jnp.float32)
    gain_first = jnp.zeros((model_width,), jnp.float32)
    gain_second = jnp.zeros((model_width,), jnp.float32)
    grad_vec = jnp.zeros((2, model_width), jnp.float32)
    grad_route = jnp.zeros((model_width, routed), jnp.float32)
    grad_mixer = jnp.zeros((model_width, 4), jnp.float32)
    grad_gate = jnp.zeros((local_experts, model_width, FF), jnp.float32)
    grad_up = jnp.zeros((local_experts, model_width, FF), jnp.float32)
    grad_down = jnp.zeros((local_experts, model_width, FF), jnp.float32)
    output_rows = []
    input_rows = []
    logit_rows = []
    for batch_index in range(micro_count):
        qkv_full, out_full, gains, vectors, route_full, mixer_full = (
            lax.all_gather(qkv_weight, ("context", "dp"), axis=1, tiled=True),
            lax.all_gather(out_weight, ("context", "dp"), axis=0, tiled=True),
            lax.all_gather(
                norm_gains.astype(jnp.bfloat16), ("context", "dp"), axis=1, tiled=True
            ).astype(norm_gains.dtype),
            lax.all_gather(
                const_vec.astype(jnp.bfloat16), ("context", "dp"), axis=1, tiled=True
            ).astype(const_vec.dtype),
            lax.all_gather(route_weight, ("context", "dp"), axis=0, tiled=True),
            lax.all_gather(const_gate, ("context", "dp"), axis=0, tiled=True),
        )
        gate_full, up_full, down_full = (
            lax.all_gather(w_gate, ("context", "dp"), axis=2, tiled=True),
            lax.all_gather(w_up, ("context", "dp"), axis=2, tiled=True),
            lax.all_gather(w_down, ("context", "dp"), axis=2, tiled=True),
        )
        token_rows = inputs[batch_index, 0].astype(jnp.float32)
        seg_rows = segments[batch_index, 0]
        route_rows = routes[batch_index, 0]
        grad_rows = cotangent[batch_index, 0].astype(jnp.float32)
        scale_first = norm_scale(token_rows)
        normed_in = (token_rows * scale_first * gains[0]).astype(jnp.bfloat16)
        projected = jnp.einsum(
            "qd,cde->cqe", normed_in, qkv_full, preferred_element_type=jnp.float32
        )
        queries = rotate(projected[0].reshape(head_shape), positions, 1.0).astype(jnp.bfloat16)
        rotated_keys = rotate(projected[1].reshape(head_shape), positions, 1.0).astype(jnp.bfloat16)
        values = projected[2].reshape(head_shape).astype(jnp.bfloat16)
        row_peak = jnp.full((head_count, row_count), MASKED, jnp.float32)
        key_block = lax.all_gather(rotated_keys, "context", axis=0, tiled=True)
        value_block = lax.all_gather(values, "context", axis=0, tiled=True)
        segment_block = lax.all_gather(seg_rows, "context", axis=0, tiled=True)
        key_positions = jnp.arange(key_block.shape[0], dtype=jnp.int32)
        scores, allowed = masked_scores(
            queries, key_block, seg_rows, segment_block, positions, key_positions, score_scale
        )
        new_peak = jnp.maximum(row_peak, jnp.max(scores, axis=-1))
        expo = jnp.where(allowed[None], jnp.exp(scores - new_peak[:, :, None]), 0.0)
        weighted = jnp.einsum(
            "hqk,khd->hqd",
            expo.astype(jnp.bfloat16),
            value_block,
            preferred_element_type=jnp.float32,
        )
        row_peak, row_total, weighted = (new_peak, jnp.sum(expo, axis=-1), weighted)
        log_total = row_peak + jnp.log(row_total)
        attn_heads = jnp.transpose(weighted / row_total[:, :, None], (1, 0, 2))
        attended = attn_heads.reshape(row_count, model_width).astype(jnp.bfloat16)
        hidden = token_rows + jnp.dot(attended, out_full, preferred_element_type=jnp.float32)
        scale_second = norm_scale(hidden)
        normed = hidden * scale_second * gains[1]
        normed_low = normed.astype(jnp.bfloat16)
        logits = (
            jnp.dot(normed_low, route_full, preferred_element_type=jnp.float32)
            + prev_logits[batch_index, 0]
        )
        probabilities = softmax_last(logits)
        gate_values = jnp.take_along_axis(probabilities, route_rows, axis=-1)
        route_ids = route_rows.reshape(-1)
        routed_ffn = route_ids < experts
        onehot = (route_ids[:, None] == jnp.arange(experts, dtype=jnp.int32)[None, :]).astype(
            jnp.int32
        )
        slot_index = jnp.sum((jnp.cumsum(onehot, axis=0) - onehot) * onehot, axis=-1)
        slot_table = (
            jnp.full((experts, capacity), assigned, jnp.int32)
            .at[jnp.where(routed_ffn, route_ids, experts), slot_index]
            .set(jnp.arange(assigned, dtype=jnp.int32), mode="drop")
        )
        token_of = jnp.where(slot_table < assigned, slot_table // 2, row_count)
        pad_rows = jnp.concatenate([normed_low, jnp.zeros((1, model_width), jnp.bfloat16)], axis=0)
        received = lax.all_to_all(
            pad_rows[token_of], "experts", split_axis=0, concat_axis=1, tiled=True
        )
        gate_act = jnp.einsum(
            "erd,edf->erf", received, gate_full, preferred_element_type=jnp.float32
        )
        up_act = jnp.einsum("erd,edf->erf", received, up_full, preferred_element_type=jnp.float32)
        sigma = jax.nn.sigmoid(gate_act)
        silu_act = gate_act * sigma
        inner_low = (silu_act * up_act).astype(jnp.bfloat16)
        expert_low = jnp.einsum(
            "erf,edf->erd", inner_low, down_full, preferred_element_type=jnp.float32
        ).astype(jnp.bfloat16)
        returned = lax.all_to_all(
            expert_low, "experts", split_axis=1, concat_axis=0, tiled=True
        ).reshape(experts * capacity, model_width)
        pick_index = jnp.where(routed_ffn, route_ids * capacity + slot_index, 0)
        expert_out = jnp.where(
            routed_ffn[:, None], returned[pick_index].astype(jnp.float32), 0.0
        ).reshape(row_count, 2, model_width)
        const_mix = softmax_last(
            jnp.dot(normed_low, mixer_full, preferred_element_type=jnp.float32).reshape(
                row_count, 2, 2
            )
        )
        const_out = (
            const_mix[:, :, 0:1] * normed[:, None, :] + const_mix[:, :, 1:2] * vectors[None, :, :]
        )
        copy_mask = (route_rows == experts + 1).astype(jnp.float32)
        const_pick = (
            route_rows[:, :, None] == experts + 2 + jnp.arange(2, dtype=jnp.int32)[None, None, :]
        ).astype(jnp.float32)
        branch = (
            expert_out
            + copy_mask[:, :, None] * normed[:, None, :]
            + jnp.einsum("qjc,qcd->qjd", const_pick, const_out, precision=lax.Precision.HIGHEST)
        )
        output_rows.append(
            (hidden + jnp.sum(gate_values[:, :, None] * branch, axis=1)).astype(jnp.bfloat16)
        )
        grad_branch = gate_values[:, :, None] * grad_rows[:, None, :]
        grad_gates = jnp.sum(grad_rows[:, None, :] * branch, axis=-1)
        grad_probs = jnp.sum(
            (route_rows[:, :, None] == jnp.arange(routed, dtype=jnp.int32)[None, None, :]).astype(
                jnp.float32
            )
            * grad_gates[:, :, None],
            axis=1,
        )
        grad_logits = probabilities * (
            grad_probs - jnp.sum(probabilities * grad_probs, axis=-1, keepdims=True)
        )
        logit_rows.append(grad_logits)
        normed_wide = normed_low.astype(jnp.float32)
        grad_route = grad_route + jnp.dot(
            normed_wide.T, grad_logits, precision=lax.Precision.HIGHEST
        )
        grad_normed = jnp.dot(
            grad_logits, route_full.astype(jnp.float32).T, precision=lax.Precision.HIGHEST
        )
        grad_normed = grad_normed + jnp.sum(copy_mask[:, :, None] * grad_branch, axis=1)
        grad_const = jnp.einsum(
            "qjc,qjd->qcd", const_pick, grad_branch, precision=lax.Precision.HIGHEST
        )
        grad_mix = jnp.stack(
            [
                jnp.sum(grad_const * normed[:, None, :], axis=-1),
                jnp.sum(grad_const * vectors[None, :, :], axis=-1),
            ],
            axis=-1,
        )
        grad_mix_logits = (
            const_mix * (grad_mix - jnp.sum(const_mix * grad_mix, axis=-1, keepdims=True))
        ).reshape(row_count, 4)
        grad_mixer = grad_mixer + jnp.dot(
            normed_wide.T, grad_mix_logits, precision=lax.Precision.HIGHEST
        )
        grad_normed = grad_normed + jnp.dot(
            grad_mix_logits, mixer_full.astype(jnp.float32).T, precision=lax.Precision.HIGHEST
        )
        grad_normed = grad_normed + jnp.sum(const_mix[:, :, 0:1] * grad_const, axis=1)
        grad_vec = grad_vec + jnp.sum(const_mix[:, :, 1:2] * grad_const, axis=0)
        grad_slots = jnp.where(
            routed_ffn[:, None], grad_branch.reshape(assigned, model_width), 0.0
        ).astype(jnp.bfloat16)
        grad_pad = jnp.concatenate([grad_slots, jnp.zeros((1, model_width), jnp.bfloat16)], axis=0)
        grad_received = lax.all_to_all(
            grad_pad[slot_table], "experts", split_axis=0, concat_axis=1, tiled=True
        )
        grad_inner = jnp.einsum(
            "erd,edf->erf", grad_received, down_full, preferred_element_type=jnp.float32
        )
        grad_down = grad_down + jnp.einsum(
            "erd,erf->edf", grad_received, inner_low, preferred_element_type=jnp.float32
        )
        grad_gate_low = (grad_inner * up_act * sigma * (1.0 + gate_act * (1.0 - sigma))).astype(
            jnp.bfloat16
        )
        grad_up_low = (grad_inner * silu_act).astype(jnp.bfloat16)
        grad_gate = grad_gate + jnp.einsum(
            "erd,erf->edf", received, grad_gate_low, preferred_element_type=jnp.float32
        )
        grad_up = grad_up + jnp.einsum(
            "erd,erf->edf", received, grad_up_low, preferred_element_type=jnp.float32
        )
        grad_entry = (
            jnp.einsum("erf,edf->erd", grad_gate_low, gate_full, preferred_element_type=jnp.float32)
            + jnp.einsum("erf,edf->erd", grad_up_low, up_full, preferred_element_type=jnp.float32)
        ).astype(jnp.bfloat16)
        grad_back = lax.all_to_all(
            grad_entry, "experts", split_axis=1, concat_axis=0, tiled=True
        ).reshape(experts * capacity, model_width)
        grad_normed = grad_normed + jnp.sum(
            jnp.where(routed_ffn[:, None], grad_back[pick_index].astype(jnp.float32), 0.0).reshape(
                row_count, 2, model_width
            ),
            axis=1,
        )
        grad_hidden_norm, gain_term = norm_back(grad_normed, hidden, scale_second, gains[1])
        gain_second = gain_second + gain_term
        grad_hidden = grad_rows + grad_hidden_norm
        grad_attn_low = grad_hidden.astype(jnp.bfloat16)
        grad_out = grad_out + jnp.dot(attended.T, grad_attn_low, preferred_element_type=jnp.float32)
        grad_attended = (
            jnp.dot(grad_attn_low, out_full.T, preferred_element_type=jnp.float32)
            .astype(jnp.bfloat16)
            .reshape(head_shape)
        )
        delta = jnp.sum(grad_attended.astype(jnp.float32) * attn_heads, axis=-1).T
        zero_heads = jnp.zeros(head_shape, jnp.float32)
        key_all, value_all, segment_all = (
            lax.all_gather(rotated_keys, "context", axis=0, tiled=True),
            lax.all_gather(values, "context", axis=0, tiled=True),
            lax.all_gather(seg_rows, "context", axis=0, tiled=True),
        )
        total_keys = key_all.shape[0]
        group_count = math.gcd(total_keys // row_count, max(1, 512 // row_count))
        block_rows = row_count * group_count
        block_count = total_keys // block_rows

        def back_block(grad_query, block_parts):
            key_block, value_block, segment_block, block_start = block_parts
            key_positions = block_start + jnp.arange(block_rows, dtype=jnp.int32)
            scores, allowed = masked_scores(
                queries, key_block, seg_rows, segment_block, positions, key_positions, score_scale
            )
            probability = jnp.where(allowed[None], jnp.exp(scores - log_total[:, :, None]), 0.0)
            grad_prob = jnp.einsum(
                "qhd,khd->hqk", grad_attended, value_block, preferred_element_type=jnp.float32
            )
            grad_score = (probability * (grad_prob - delta[:, :, None])).astype(jnp.bfloat16)
            grad_query = (
                grad_query
                + jnp.einsum(
                    "hqk,khd->qhd", grad_score, key_block, preferred_element_type=jnp.float32
                )
                * score_scale
            )
            grad_key = (
                jnp.einsum("hqk,qhd->khd", grad_score, queries, preferred_element_type=jnp.float32)
                * score_scale
            )
            grad_value = jnp.einsum(
                "hqk,qhd->khd",
                probability.astype(jnp.bfloat16),
                grad_attended,
                preferred_element_type=jnp.float32,
            )
            return (grad_query, (grad_key, grad_value))

        block_starts = jnp.arange(block_count, dtype=jnp.int32) * block_rows
        grad_query, (key_terms, value_terms) = lax.scan(
            back_block,
            zero_heads,
            (
                key_all.reshape(block_count, block_rows, head_count, HEAD_DIM),
                value_all.reshape(block_count, block_rows, head_count, HEAD_DIM),
                segment_all.reshape(block_count, block_rows),
                block_starts,
            ),
        )
        grad_key, grad_value = (
            lax.psum_scatter(
                key_terms.reshape(total_keys, head_count, HEAD_DIM).astype(jnp.bfloat16),
                "context",
                scatter_dimension=0,
                tiled=True,
            ).astype(jnp.float32),
            lax.psum_scatter(
                value_terms.reshape(total_keys, head_count, HEAD_DIM).astype(jnp.bfloat16),
                "context",
                scatter_dimension=0,
                tiled=True,
            ).astype(jnp.float32),
        )
        grad_projected = jnp.stack(
            [
                rotate(grad_query, positions, -1.0).reshape(row_count, model_width),
                rotate(grad_key, positions, -1.0).reshape(row_count, model_width),
                grad_value.reshape(row_count, model_width),
            ]
        ).astype(jnp.bfloat16)
        grad_qkv = grad_qkv + jnp.einsum(
            "qd,cqe->cde", normed_in, grad_projected, preferred_element_type=jnp.float32
        )
        grad_normed_in = jnp.einsum(
            "cqe,cde->qd", grad_projected, qkv_full, preferred_element_type=jnp.float32
        )
        grad_token_norm, gain_term = norm_back(grad_normed_in, token_rows, scale_first, gains[0])
        gain_first = gain_first + gain_term
        input_rows.append(grad_hidden + grad_token_norm)
    grad_gain = jnp.stack([gain_first, gain_second])
    (
        grad_qkv,
        grad_out,
        grad_gain,
        grad_vec,
        grad_route,
        grad_mixer,
        grad_gate,
        grad_up,
        grad_down,
    ) = (
        lax.psum_scatter(
            grad_qkv.astype(jnp.bfloat16), ("context", "dp"), scatter_dimension=1, tiled=True
        ).astype(jnp.float32),
        lax.psum_scatter(
            grad_out.astype(jnp.bfloat16), ("context", "dp"), scatter_dimension=0, tiled=True
        ).astype(jnp.float32),
        lax.psum_scatter(
            grad_gain.astype(jnp.bfloat16), ("context", "dp"), scatter_dimension=1, tiled=True
        ).astype(jnp.float32),
        lax.psum_scatter(
            grad_vec.astype(jnp.bfloat16), ("context", "dp"), scatter_dimension=1, tiled=True
        ).astype(jnp.float32),
        lax.psum_scatter(
            grad_route.astype(jnp.bfloat16), ("context", "dp"), scatter_dimension=0, tiled=True
        ).astype(jnp.float32),
        lax.psum_scatter(
            grad_mixer.astype(jnp.bfloat16), ("context", "dp"), scatter_dimension=0, tiled=True
        ).astype(jnp.float32),
        lax.psum_scatter(
            grad_gate.astype(jnp.bfloat16), ("context", "dp"), scatter_dimension=2, tiled=True
        ).astype(jnp.float32),
        lax.psum_scatter(
            grad_up.astype(jnp.bfloat16), ("context", "dp"), scatter_dimension=2, tiled=True
        ).astype(jnp.float32),
        lax.psum_scatter(
            grad_down.astype(jnp.bfloat16), ("context", "dp"), scatter_dimension=2, tiled=True
        ).astype(jnp.float32),
    )
    grad_qkv, grad_out, grad_gain, grad_vec, grad_route, grad_mixer = (
        lax.psum(grad_qkv.astype(jnp.bfloat16), "experts").astype(jnp.float32),
        lax.psum(grad_out.astype(jnp.bfloat16), "experts").astype(jnp.float32),
        lax.psum(grad_gain.astype(jnp.bfloat16), "experts").astype(jnp.float32),
        lax.psum(grad_vec.astype(jnp.bfloat16), "experts").astype(jnp.float32),
        lax.psum(grad_route.astype(jnp.bfloat16), "experts").astype(jnp.float32),
        lax.psum(grad_mixer.astype(jnp.bfloat16), "experts").astype(jnp.float32),
    )
    output = jnp.stack(output_rows)[:, None]
    input_grad = jnp.stack(input_rows)[:, None]
    logit_grad = jnp.stack(logit_rows)[:, None]
    return (
        output,
        input_grad,
        logit_grad,
        grad_qkv,
        grad_out,
        grad_gain,
        grad_route,
        grad_mixer,
        grad_vec,
        grad_gate,
        grad_up,
        grad_down,
    )


BF = jnp.bfloat16
F32 = jnp.float32
BLOCK = 256
RING = 4
PIECES = tuple((k, own) for k in range(RING) for own in (True, False))
VMEM_BYTES = 60 * 2**20


def dot(left, right, left_dim, right_dim):
    return lax.dot_general(
        left, right, (((left_dim,), (right_dim,)), ((), ())), preferred_element_type=F32
    )


def iota(shape, dim):
    return lax.broadcasted_iota(jnp.int32, shape, dim)


def split3(values):
    high = values.astype(BF).astype(F32)
    rest = values - high
    middle = rest.astype(BF).astype(F32)
    return (high, middle, rest - middle)


def split2(values):
    high = values.astype(BF)
    return (high, (values - high.astype(F32)).astype(BF))


def rows_of(parts, count):
    width = parts[0].shape[1]
    index = iota((count, width), 0)
    total = jnp.zeros((count, width), F32)
    for place, part in enumerate(parts):
        total = jnp.where(index == place, jnp.broadcast_to(part, (count, width)), total)
    return total


def column_of(row, width=128):
    stacked = rows_of(split3(row), 16).astype(BF)
    return dot(stacked, jnp.ones((16, width), BF), 0, 0)


def wide(column, copies):
    return jnp.concatenate([column] * copies, axis=1)


def kernel_call(body, idx, args, outs, flops, grid=None, in_specs=None, out_specs=None, scratch=()):
    moved = sum(a.size * a.dtype.itemsize for a in args)
    moved += sum(math.prod(s) * jnp.dtype(d).itemsize for s, d in outs)
    whole = pl.BlockSpec(memory_space=pltpu.VMEM)
    extra = {} if grid is None else {"grid": grid}
    return pl.pallas_call(
        body,
        out_shape=[jax.ShapeDtypeStruct(s, d) for s, d in outs],
        in_specs=[pl.BlockSpec(memory_space=pltpu.SMEM)]
        + (in_specs if in_specs is not None else [whole] * len(args)),
        out_specs=out_specs if out_specs is not None else [whole] * len(outs),
        scratch_shapes=list(scratch),
        compiler_params=pltpu.CompilerParams(vmem_limit_bytes=VMEM_BYTES),
        cost_estimate=pl.CostEstimate(flops=flops, bytes_accessed=moved, transcendentals=0),
        **extra,
    )(idx, *args)


def rope_tables(length):
    half = HEAD_DIM // 2
    inverse = (10000.0 ** (-np.arange(half, dtype=np.float32) / half)).astype(np.float32)
    angles = (np.arange(length, dtype=np.float32)[:, None] * inverse[None, :]).astype(np.float64)
    cosine, sine = np.cos(angles), np.sin(angles)
    cosine = np.concatenate([cosine] * 4, axis=1).astype(np.float32)
    sine = np.concatenate([-sine, sine] * 2, axis=1).astype(np.float32)
    return cosine, sine


def turn(values, cosine, sine, direction):
    width = values.shape[1]
    copies = width // cosine.shape[1]
    ahead = pltpu.roll(values, width - HEAD_DIM // 2, 1)
    behind = pltpu.roll(values, HEAD_DIM // 2, 1)
    first = (iota(values.shape, 1) & (HEAD_DIM - 1)) < HEAD_DIM // 2
    partner = jnp.where(first, ahead, behind)
    return values * wide(cosine, copies) + direction * (partner * wide(sine, copies))


def project_kernel(idx, xa, xb, ya, yb, params, cosine, sine, *refs):
    pieces, (q_ref, k_ref, v_ref, normed_ref, x_ref, w_ref) = refs[:8], refs[8:]
    z, core, flip = idx[1], idx[2], idx[3]
    depth, width = pieces[0].shape[1], pieces[0].shape[2]
    for (k, own), piece in zip(PIECES, pieces):
        shard = lax.rem(z + k, RING) * 2 + (core if own else 1 - core)
        rows = pl.ds(pl.multiple_of(shard * depth, 16), depth)
        for j in range(3):
            w_ref[rows, j * width : (j + 1) * width] = piece[j]
    for ref, half, slot in ((xa, core, 0), (xb, core, 1), (ya, 1 - core, 0), (yb, 1 - core, 1)):
        block = 2 * half + (flip if slot == 0 else 1 - flip)
        x_ref[pl.ds(pl.multiple_of(block * BLOCK, BLOCK), BLOCK), :] = ref[...]
    gain = params[14:15, :]

    def step(i, carry):
        rows = pl.ds(pl.multiple_of(i * BLOCK, BLOCK), BLOCK)
        x = x_ref[rows, :].astype(F32)
        normed = (x * norm_scale(x) * gain).astype(BF)
        normed_ref[rows, :] = normed
        cos_rows, sin_rows = cosine[rows, :], sine[rows, :]
        queries = turn(dot(normed, w_ref[:, :width], 1, 0), cos_rows, sin_rows, 1.0)
        q_ref[rows, :] = (queries * HEAD_DIM**-0.5).astype(BF)
        keys = turn(dot(normed, w_ref[:, width : 2 * width], 1, 0), cos_rows, sin_rows, 1.0)
        k_ref[rows, :] = keys.astype(BF)
        v_ref[rows, :] = dot(normed, w_ref[:, 2 * width :], 1, 0).astype(BF)
        return carry

    lax.fori_loop(0, x_ref.shape[0] // BLOCK, step, 0)


def mask_of(seg_row, seg_col, i):
    n = (i + 1) * BLOCK
    mine = seg_row[:1, i * BLOCK : n]
    key_index, query_index = iota((BLOCK, BLOCK), 0), iota((BLOCK, BLOCK), 1)
    last = (seg_col[i * BLOCK : n, :1] == mine) & (key_index <= query_index)
    bias = jnp.where(last, 0.0, MASKED)
    if i > 0:
        before = jnp.where(seg_col[: i * BLOCK, :1] == mine, 0.0, MASKED)
        bias = jnp.concatenate([before, bias], axis=0)
    return bias


def attend_kernel(idx, q_ref, k_ref, v_ref, seg_row, seg_col, keep_ref, send_ref, lse_ref):
    core, flip = idx[2], idx[3]
    low_lanes = iota((BLOCK, 2 * HEAD_DIM), 1) < HEAD_DIM
    for i in range(q_ref.shape[0] // BLOCK):
        n = (i + 1) * BLOCK
        queries = q_ref[i * BLOCK : n, :]
        keys, values = k_ref[:n, :], v_ref[:n, :]
        bias = mask_of(seg_row, seg_col, i)
        outs = []
        for head in range(2):
            mine = low_lanes if head == 0 else ~low_lanes
            scores = dot(keys, jnp.where(mine, queries, 0), 1, 1) + bias
            peak = jnp.max(scores, axis=0, keepdims=True)
            weights = jnp.exp(scores - peak)
            total = jnp.sum(weights, axis=0, keepdims=True)
            out = dot(values, weights.astype(BF), 0, 0)
            outs.append(out[head * HEAD_DIM : (head + 1) * HEAD_DIM] / total)
            lse_ref[0, head : head + 1, i * BLOCK : n] = peak + jnp.log(total)
        attended = jnp.concatenate(outs, axis=0).T.astype(BF)
        half, slot = i // 2, (i % 2) ^ flip
        rows = pl.ds(pl.multiple_of(slot * BLOCK, BLOCK), BLOCK)

        @pl.when(half == core)
        def _():
            keep_ref[rows, :] = attended

        @pl.when(half != core)
        def _():
            send_ref[rows, :] = attended


def attend_back_kernel(
    idx, q_ref, k_ref, v_ref, own_ref, other_ref, seg_row, seg_col, lse_ref, cosine, sine,
    dq_ref, dk_ref, dv_ref, key_sum, value_sum,
):
    core, flip = idx[2], idx[3]
    low_lanes = iota((BLOCK, 2 * HEAD_DIM), 1) < HEAD_DIM
    key_sum[...] = jnp.zeros(key_sum.shape, F32)
    value_sum[...] = jnp.zeros(value_sum.shape, F32)
    for i in range(q_ref.shape[0] // BLOCK):
        n = (i + 1) * BLOCK
        queries = q_ref[i * BLOCK : n, :]
        keys, values = k_ref[:n, :], v_ref[:n, :]
        bias = mask_of(seg_row, seg_col, i)
        half, slot = i // 2, (i % 2) ^ flip
        rows = pl.ds(pl.multiple_of(slot * BLOCK, BLOCK), BLOCK)
        grads = jnp.where(half == core, own_ref[rows, :], other_ref[rows, :])
        grad_queries = []
        for head in range(2):
            mine = low_lanes if head == 0 else ~low_lanes
            head_queries = jnp.where(mine, queries, 0)
            head_grads = jnp.where(mine, grads, 0)
            scores = dot(keys, head_queries, 1, 1) + bias
            weights = jnp.exp(scores - lse_ref[0, head : head + 1, i * BLOCK : n])
            grad_weights = dot(values, head_grads, 1, 1)
            delta = jnp.sum(weights * grad_weights, axis=0, keepdims=True)
            grad_scores = (weights * (grad_weights - delta)).astype(BF)
            key_sum[:n, :] += dot(grad_scores, head_queries, 1, 0)
            value_sum[:n, :] += dot(weights.astype(BF), head_grads, 1, 0)
            grad_queries.append(dot(grad_scores, keys, 0, 0))
        grad_query = jnp.where(low_lanes, grad_queries[0], grad_queries[1]) * HEAD_DIM**-0.5
        tile = slice(i * BLOCK, n)
        dq_ref[tile, :] = turn(grad_query, cosine[tile, :], sine[tile, :], -1.0).astype(BF)
    for i in range(q_ref.shape[0] // BLOCK):
        tile = slice(i * BLOCK, (i + 1) * BLOCK)
        dk_ref[tile, :] = turn(key_sum[tile, :], cosine[tile, :], sine[tile, :], -1.0).astype(BF)
        dv_ref[tile, :] = value_sum[tile, :].astype(BF)


def routed_rows(small, routed):
    index = iota((routed, small.shape[1]), 0).astype(F32)
    return jnp.where((small[8:9, :] == index) | (small[9:10, :] == index), 1.0, 0.0)


def ranks_of(named):
    tokens = named.shape[1]
    before, here = iota((tokens, tokens), 0), iota((tokens, tokens), 1)
    earlier = (before < here) & (before // BLOCK == here // BLOCK)
    stacked = jnp.concatenate([named, jnp.zeros_like(named)], axis=0).astype(BF)
    return dot(stacked, jnp.where(earlier, 1.0, 0.0).astype(BF), 1, 0)[: named.shape[0]]


def pick_row(values, index):
    return jnp.sum(jnp.where(iota(values.shape, 0) == index, values, 0.0), axis=0, keepdims=True)


def slots_of(named, rank, expert, capacity):
    tokens = named.shape[1]
    place = pick_row(rank, expert)
    place = place + jnp.where(iota((1, tokens), 1) >= BLOCK, float(capacity), 0.0)
    slot = iota((2 * capacity, tokens), 0).astype(F32)
    taken = (slot == place) & (pick_row(named, expert) > 0.5)
    return jnp.where(taken, 1.0, 0.0).astype(BF)


def pair_of(first, second):
    return jnp.concatenate([first[...], second[...]], axis=0)


def grad_slots_kernel(idx, sa, sb, ca, cb, *outs):
    small = jnp.concatenate([sa[...], sb[...]], axis=1)
    named = routed_rows(small, 8)
    rank = ranks_of(named)
    grads = pair_of(ca, cb)
    for k, out in enumerate(outs):
        taken = slots_of(named, rank, idx[0] ^ k, out.shape[0] // 2)
        out[...] = dot(taken, grads, 1, 0).astype(BF)


def route_kernel(idx, keep, recv, xa, xb, params, sa, sb, *refs):
    pieces, (hidden_ref, ow_ref, state_ref), outs = refs[:8], refs[8:11], refs[11:]
    z, core = idx[1], idx[2]
    depth = pieces[0].shape[0]
    for (k, own), piece in zip(PIECES, pieces):
        shard = lax.rem(z + k, RING) * 2 + (core if own else 1 - core)
        ow_ref[pl.ds(pl.multiple_of(shard * depth, 16), depth), :] = piece[...]
    width = keep.shape[1]
    own_rows = pl.ds(pl.multiple_of(core * width, 16), width)
    other_rows = pl.ds(pl.multiple_of((1 - core) * width, 16), width)
    hidden = (
        pair_of(xa, xb).astype(F32)
        + dot(keep[...], ow_ref[own_rows, :], 1, 0)
        + dot(recv[...], ow_ref[other_rows, :], 1, 0)
    )
    hidden_ref[...] = hidden
    normed = (hidden * norm_scale(hidden) * params[15:16, :]).astype(BF)
    small = jnp.concatenate([sa[...], sb[...]], axis=1)
    logits = dot(params[...].astype(BF), normed, 1, 1)
    named = routed_rows(small, 8)
    rank = ranks_of(named)
    shifted = logits[:8] + small[:8]
    shifted = jnp.exp(shifted - jnp.max(shifted, axis=0, keepdims=True))
    probabilities = shifted / jnp.sum(shifted, axis=0, keepdims=True)
    mixed = []
    for c in range(2):
        first, second = logits[8 + 2 * c : 9 + 2 * c], logits[9 + 2 * c : 10 + 2 * c]
        peak = jnp.maximum(first, second)
        first, second = jnp.exp(first - peak), jnp.exp(second - peak)
        mixed += [first / (first + second), second / (first + second)]
    state_ref[0:8, :] = probabilities
    state_ref[8:16, :] = rows_of(mixed, 8)
    state_ref[16:24, :] = rank
    slots = outs[0].shape[0] - 16
    for k, out in enumerate(outs):
        expert = idx[0] ^ k
        taken = slots_of(named, rank, expert, slots // 2)
        out[:slots, :] = dot(taken, normed, 1, 0).astype(BF)
        gates = rows_of(split3(pick_row(probabilities, expert)), 16).astype(BF)
        out[slots:, :] = jnp.zeros((16, out.shape[1]), BF)
        out[slots:, :slots] = dot(gates, taken, 1, 1).astype(BF)


def expert_kernel(idx, *refs):
    tokens, grads, weights = refs[:8], refs[8:16], refs[16:24]
    (t_ref, g_ref, inner_ref, gate_ref, up_ref, down_full) = refs[24:30]
    outs = refs[30:38]
    t_all, g_all, scale_all, gate_full, up_full, results = refs[38:]
    core = idx[2]
    j = pl.program_id(0)
    slots = grads[0].shape[0]
    half, chunk = weights[0].shape[1], weights[0].shape[2]

    @pl.when(j == 0)
    def _():
        for k in range(RING):
            columns = slice(k * chunk, (k + 1) * chunk)
            for part in range(2):
                rows = slice(part * half, (part + 1) * half)
                piece = weights[2 * k + part]
                gate_full[rows, columns] = piece[0]
                up_full[rows, columns] = piece[1]
                down_full[rows, columns] = piece[2]
        for p in range(8):
            rows = slice(p * slots, (p + 1) * slots)
            t_all[rows, :] = tokens[p][:slots, :]
            g_all[rows, :] = grads[p][...]
            parts = tokens[p][slots:, :slots]
            scale_all[rows, :] = dot(parts, jnp.ones((16, 128), BF), 0, 0)

    tile = 2 * slots
    rows = pl.ds(pl.multiple_of(j * tile, 16), tile)
    entry, grad = t_all[rows, :], g_all[rows, :]
    scale = scale_all[rows, :]
    model = entry.shape[1]
    t_ref[...] = entry
    g_ref[...] = (grad.astype(F32) * wide(scale, model // 128)).astype(BF)
    gate_act = dot(entry, gate_full[...], 1, 0)
    up_act = dot(entry, up_full[...], 1, 0)
    sigma = jax.nn.sigmoid(gate_act)
    silu_act = gate_act * sigma
    inner = (silu_act * up_act).astype(BF)
    inner_ref[...] = inner
    raw = dot(grad, down_full[...], 1, 0)
    product = split2(inner.astype(F32) * raw)
    grad_inner = raw * wide(scale, raw.shape[1] // 128)
    grad_gate = (grad_inner * up_act * sigma * (1.0 + gate_act * (1.0 - sigma))).astype(BF)
    grad_up = (grad_inner * silu_act).astype(BF)
    gate_ref[...] = grad_gate
    up_ref[...] = grad_up
    entry_grad = dot(grad_gate, gate_full[...], 1, 1) + dot(grad_up, up_full[...], 1, 1)
    ones = jnp.ones((16, raw.shape[1]), BF)
    for part in range(2):
        piece_rows = slice(part * slots, (part + 1) * slots)
        result = results.at[2 * j + part]
        result[:slots, :] = entry_grad[piece_rows].astype(BF)
        sums = dot(ones, product[0][piece_rows], 1, 1) + dot(ones, product[1][piece_rows], 1, 1)
        index = iota(sums.shape, 0)
        high, middle, rest = split3(sums)
        packed = jnp.where(
            index == 4 * core,
            high,
            jnp.where(index == 4 * core + 1, middle, jnp.where(index == 4 * core + 2, rest, 0.0)),
        )
        result[slots:, :] = jnp.zeros((16, model), BF)
        result[slots:, :slots] = packed.astype(BF)

    @pl.when(j == pl.num_programs(0) - 1)
    def _():
        for p in range(8):
            outs[p][...] = results[p]


def expert_out_kernel(idx, inner_ref, down_ref, *outs):
    j = pl.program_id(0)
    slots = outs[0].shape[0]
    out = dot(inner_ref[...], down_ref[...], 1, 1).astype(BF)
    for step in range(4):

        @pl.when(j == step)
        def _(step=step):
            outs[2 * step][...] = out[:slots]
            outs[2 * step + 1][...] = out[slots:]


def expert_grads_kernel(idx, t_ref, g_ref, inner_ref, gate_ref, up_ref, *outs):
    k = pl.program_id(0)
    half = outs[1].shape[1]
    for step in range(RING):

        @pl.when(k == step)
        def _(step=step):
            for place, (left, right) in enumerate(
                ((t_ref, gate_ref), (t_ref, up_ref), (g_ref, inner_ref))
            ):
                grad = dot(left[...], right[...], 0, 0)
                if step == 0:
                    outs[0][place] = grad
                else:
                    outs[2 * step - 1][place] = grad[:half].astype(BF)
                    outs[2 * step][place] = grad[half:].astype(BF)


def slot_table(idx, small, state, capacity):
    named = routed_rows(small, 8)
    rank = state[16:24, :]
    return [slots_of(named, rank, idx[0] ^ k, capacity) for k in range(RING)], named


def branch_weights(state, named):
    gates = state[0:8, :] * named
    consts = [gates[6 + c : 7 + c] for c in range(2)]
    normed_weight = gates[5:6]
    for c in range(2):
        normed_weight = normed_weight + consts[c] * state[8 + 2 * c : 9 + 2 * c, :]
    vector_weights = [consts[c] * state[9 + 2 * c : 10 + 2 * c, :] for c in range(2)]
    return consts, normed_weight, vector_weights


def output_kernel(idx, hidden_ref, state_ref, sa, sb, params, *refs):
    returned, (oa, ob) = refs[:4], refs[4:]
    small = jnp.concatenate([sa[...], sb[...]], axis=1)
    state = state_ref[...]
    tables, named = slot_table(idx, small, state, returned[0].shape[0] // 2)
    hidden = hidden_ref[...]
    normed = hidden * norm_scale(hidden) * params[15:16, :]
    _, normed_weight, vector_weights = branch_weights(state, named)
    output = hidden + wide(column_of(normed_weight), normed.shape[1] // 128) * normed
    vector_rows = rows_of(split3(params[12:13, :])[:2] * 2 + split3(params[13:14, :])[:2] * 2, 16)
    first, second = split3(vector_weights[0])[:2], split3(vector_weights[1])[:2]
    weight_rows = rows_of(
        (first[0], first[0], first[1], first[1], second[0], second[0], second[1], second[1]), 16
    )
    output += dot(weight_rows.astype(BF), vector_rows.astype(BF), 0, 0)
    for k in range(RING):
        gate = pick_row(state[0:8, :], idx[0] ^ k)
        high, low, _ = split3(gate)
        table = tables[k].astype(F32)
        output += dot((table * high).astype(BF), returned[k][...], 0, 0)
        output += dot((table * low).astype(BF), returned[k][...], 0, 0)
    oa[...] = output[:BLOCK].astype(BF)
    ob[...] = output[BLOCK:].astype(BF)


def hidden_back_kernel(idx, hidden_ref, state_ref, sa, sb, ca, cb, params, ow_ref, *refs):
    returned = refs[:4]
    gh_ref, low_ref, own_ref, send_ref, la, lb, small_ref = refs[4:]
    core = idx[2]
    small = jnp.concatenate([sa[...], sb[...]], axis=1)
    state = state_ref[...]
    slots = returned[0].shape[0] - 16
    tables, named = slot_table(idx, small, state, slots // 2)
    probabilities = state[0:8, :]
    hidden = hidden_ref[...]
    factor = norm_scale(hidden)
    scaled_hidden = hidden * factor
    normed = scaled_hidden * params[15:16, :]
    normed_low = normed.astype(BF)
    grads_low = pair_of(ca, cb)
    grads = grads_low.astype(F32)
    ones = jnp.ones((16, hidden.shape[1]), BF)
    high, low = split2(grads * normed)
    on_normed = (dot(ones, high, 1, 1) + dot(ones, low, 1, 1))[0:1]
    first, second = split3(params[12:13, :])[:2], split3(params[13:14, :])[:2]
    on_vectors = dot(rows_of(first + second, 16).astype(BF), grads_low, 1, 1)
    on_vector = (on_vectors[0:1] + on_vectors[1:2], on_vectors[2:3] + on_vectors[3:4])
    consts, normed_weight, vector_weights = branch_weights(state, named)
    index = iota(probabilities.shape, 0)
    grad_probs = jnp.where(index == 5, on_normed, 0.0)
    mix_rows = []
    for c in range(2):
        mix_first, mix_second = state[8 + 2 * c : 9 + 2 * c, :], state[9 + 2 * c : 10 + 2 * c, :]
        dot_c = mix_first * on_normed + mix_second * on_vector[c]
        grad_probs = jnp.where(index == 6 + c, dot_c, grad_probs)
        grad_first, grad_second = consts[c] * on_normed, consts[c] * on_vector[c]
        mean = mix_first * grad_first + mix_second * grad_second
        mix_rows += [mix_first * (grad_first - mean), mix_second * (grad_second - mean)]
    back = jnp.zeros(hidden.shape, F32)
    for k in range(RING):
        packed = returned[k][slots:, :slots]
        found = jnp.sum(dot(packed, tables[k], 1, 0), axis=0, keepdims=True)
        grad_probs = jnp.where(index == (idx[0] ^ k), found, grad_probs)
        back += dot(tables[k], returned[k][:slots, :], 0, 0)
    grad_probs = grad_probs * named
    grad_logits = probabilities * (
        grad_probs - jnp.sum(probabilities * grad_probs, axis=0, keepdims=True)
    )
    la[...] = grad_logits[:, :BLOCK]
    lb[...] = grad_logits[:, BLOCK:]
    router_rows = jnp.concatenate([grad_logits, rows_of(mix_rows, 8)], axis=0)
    rows_high, rows_low = split2(router_rows)
    weights_low = params[...].astype(BF)
    grad_normed = (
        back
        + dot(rows_high, weights_low, 0, 0)
        + dot(rows_low, weights_low, 0, 0)
        + wide(column_of(normed_weight), hidden.shape[1] // 128) * grads
    )
    router_grad = dot(rows_high, normed_low, 1, 0) + dot(rows_low, normed_low, 1, 0)
    first, second = split3(vector_weights[0])[:2], split3(vector_weights[1])[:2]
    vector_grad = dot(rows_of(first + second, 16).astype(BF), grads_low, 1, 0)
    gain_grad = jnp.sum(grad_normed * scaled_hidden, axis=0, keepdims=True)
    small_ref[...] = jnp.where(
        iota(router_grad.shape, 0) < 12,
        router_grad,
        rows_of(
            [jnp.zeros_like(gain_grad)] * 12
            + [vector_grad[0:1] + vector_grad[1:2], vector_grad[2:3] + vector_grad[3:4], gain_grad],
            16,
        ),
    )
    scaled = grad_normed * params[15:16, :]
    mean = jnp.mean(scaled * hidden, axis=-1, keepdims=True)
    grad_hidden = grads + factor * scaled - hidden * (factor * factor * factor * mean)
    gh_ref[...] = grad_hidden
    grad_low = grad_hidden.astype(BF)
    low_ref[...] = grad_low
    width = own_ref.shape[1]
    own_rows = pl.ds(pl.multiple_of(core * width, 16), width)
    other_rows = pl.ds(pl.multiple_of((1 - core) * width, 16), width)
    own_ref[...] = dot(grad_low, ow_ref[own_rows, :], 1, 1).astype(BF)
    send_ref[...] = dot(grad_low, ow_ref[other_rows, :], 1, 1).astype(BF)


def out_grad_kernel(idx, keep, recv, low_ref, small_ref, own_ref, send_ref, full):
    z, core = idx[1], idx[2]
    width, model = keep.shape[1], low_ref.shape[1]
    own_rows = pl.ds(pl.multiple_of(core * width, 16), width)
    other_rows = pl.ds(pl.multiple_of((1 - core) * width, 16), width)
    full[own_rows, :model] = dot(keep[...], low_ref[...], 0, 0).astype(BF)
    full[other_rows, :model] = dot(recv[...], low_ref[...], 0, 0).astype(BF)
    eye = jnp.where(iota((16, 128), 0) == iota((16, 128), 1), 1.0, 0.0).astype(BF)
    full[:, model:] = dot(small_ref[...].astype(BF), eye, 0, 0).astype(BF)
    depth = own_ref.shape[1]
    for k in range(RING):
        shard = lax.rem(z + k, RING) * 2
        own_ref[k] = full[pl.ds(pl.multiple_of((shard + core) * depth, 16), depth), :]
        send_ref[k] = full[pl.ds(pl.multiple_of((shard + 1 - core) * depth, 16), depth), :]


def project_back_kernel(idx, dq, dk, dv, normed_ref, x_ref, w_ref, *refs):
    outs, (keep_ref, send_ref), full = refs[:7], refs[7:9], refs[9]
    z, core, flip = idx[1], idx[2], idx[3]
    width = dq.shape[1]
    gain_sum = jnp.zeros((1, x_ref.shape[1]), F32)
    for i in range(x_ref.shape[0] // BLOCK):
        tile = slice(i * BLOCK, (i + 1) * BLOCK)
        part = (
            dot(dq[tile, :], w_ref[:, :width], 1, 1)
            + dot(dk[tile, :], w_ref[:, width : 2 * width], 1, 1)
            + dot(dv[tile, :], w_ref[:, 2 * width :], 1, 1)
        )
        x = x_ref[tile, :].astype(F32)
        gain_sum += jnp.sum(part * (x * norm_scale(x)), axis=0, keepdims=True)
        half, slot = i // 2, (i % 2) ^ flip
        rows = pl.ds(pl.multiple_of(slot * BLOCK, BLOCK), BLOCK)

        @pl.when(half == core)
        def _(part=part, rows=rows):
            keep_ref[rows, :] = part.astype(BF)

        @pl.when(half != core)
        def _(part=part, rows=rows):
            send_ref[rows, :] = part.astype(BF)

    for j, ref in enumerate((dq, dk, dv)):
        full[:, j * width : (j + 1) * width] = dot(normed_ref[...], ref[...], 0, 0)
    full[:, 3 * width :] = column_of(gain_sum)
    depth = outs[1].shape[0]
    for k in range(RING):
        base = lax.rem(z + k, RING) * 2 * depth
        first = full[pl.ds(pl.multiple_of(base, 16), depth), :]
        second = full[pl.ds(pl.multiple_of(base + depth, 16), depth), :]
        if k == 0:
            outs[0][:depth, :] = first
            outs[0][depth:, :] = second
        else:
            outs[2 * k - 1][...] = first.astype(BF)
            outs[2 * k][...] = second.astype(BF)


def input_back_kernel(idx, keep_ref, recv_ref, gh_ref, xa, xb, params, oa, ob):
    gain = params[14:15, :]
    for slot, (x_ref, out) in enumerate(((xa, oa), (xb, ob))):
        tile = slice(slot * BLOCK, (slot + 1) * BLOCK)
        x = x_ref[...].astype(F32)
        factor = norm_scale(x)
        scaled = (keep_ref[tile, :].astype(F32) + recv_ref[tile, :].astype(F32)) * gain
        mean = jnp.mean(scaled * x, axis=-1, keepdims=True)
        out[...] = (
            gh_ref[tile, :] + factor * scaled - x * (factor * factor * factor * mean)
        ).astype(BF)


def up(values):
    return lax.ppermute(values, "context", [(i, (i + 1) % RING) for i in range(RING)])


def down(values):
    return lax.ppermute(values, "context", [(i, (i - 1) % RING) for i in range(RING)])


def across(values):
    return lax.ppermute(values, "dp", [(0, 1), (1, 0)])


def over(values, k):
    return lax.ppermute(values, "experts", [(i, i ^ k) for i in range(RING)])


def ring_gather(first, second):
    from_below, from_above = (up(first), up(second)), (down(first), down(second))
    opposite = (up(from_below[0]), down(from_above[1]))
    return [(first, second), from_above, opposite, from_below]


def ring_sum(own, pieces):
    (above_1, above_2), (far_1, far_2), (below_1, below_2) = pieces
    far_up, far_down = up(far_2), down(far_1)
    got_1, got_2 = up(above_1), down(below_2)
    more_2 = up((above_2.astype(F32) + far_up.astype(F32)).astype(BF))
    more_1 = down((below_1.astype(F32) + far_down.astype(F32)).astype(BF))
    return (
        own[0] + got_1.astype(F32) + more_1.astype(F32),
        own[1] + got_2.astype(F32) + more_2.astype(F32),
    )


def plane_sum(first, second):
    a, b = first.astype(BF), second.astype(BF)
    a, b = (a.astype(F32) + over(a, 1).astype(F32)), (b.astype(F32) + over(b, 2).astype(F32))
    a_low, b_low = a.astype(BF), b.astype(BF)
    return a + over(a_low, 2).astype(F32), b + over(b_low, 1).astype(F32)


def chip_local(
    inputs, cotangent, qkv_weight, out_weight, norm_gains, route_weight, const_gate, const_vec,
    w_gate, w_up, w_down, prev_logits, routes, segments,
):
    e, z, core = lax.axis_index("experts"), lax.axis_index("context"), lax.axis_index("dp")
    flip = z // 2
    idx = jnp.stack([e, z, core, flip]).astype(jnp.int32)
    odd = lax.rem(z, 2)
    rows, model = inputs.shape[2], inputs.shape[3]
    length = rows * RING
    half_model = model // 2
    capacity = rows * 5 // 16
    slots = 2 * capacity

    def place(z_index, d, which):
        micro = z_index % 2 if which == 0 else 1 - z_index % 2
        return (2 * micro + d) * 2 + z_index // 2

    routes_of = [
        [(zi * 2 + d, place(zi, d, which)) for zi in range(RING) for d in range(2)]
        for which in range(2)
    ]

    def leave(values):
        return [
            lax.ppermute(
                lax.dynamic_index_in_dim(values, odd if which == 0 else 1 - odd, 0, False),
                ("context", "dp"),
                routes_of[which],
            )
            for which in range(2)
        ]

    def come_home(first, second):
        got = [
            lax.ppermute(v, ("context", "dp"), [(b, a) for a, b in routes_of[which]])
            for which, v in enumerate((first, second))
        ]
        return jnp.where(odd == 0, jnp.stack(got), jnp.stack(got[::-1]))

    xa, xb = leave(inputs[:, 0])
    small = jnp.concatenate(
        [
            jnp.swapaxes(prev_logits[:, 0], 1, 2),
            jnp.swapaxes(routes[:, 0], 1, 2).astype(F32),
            segments.astype(F32),
            jnp.zeros((2, 5, rows), F32),
        ],
        axis=1,
    )
    sa, sb = leave(small)
    ya, yb = across(xa), across(xb)
    ta, tb = across(sa), across(sb)
    seg = jnp.stack([sa[10], sb[10], ta[10], tb[10]]).reshape(2, 2, rows)
    seg = jnp.where(core == 0, seg, seg[::-1])
    seg = jnp.where(flip == 0, seg, seg[:, ::-1]).reshape(1, length)
    seg_row, seg_col = jnp.broadcast_to(seg, (8, length)), seg.reshape(length, 1)

    params = jnp.concatenate(
        [route_weight.astype(F32).T, const_gate.astype(F32).T, const_vec, norm_gains], axis=0
    )
    other = across(params)
    pair = jnp.where(core == 0, jnp.stack([params, other]), jnp.stack([other, params]))
    ring = jnp.stack([pair, down(pair), up(up(pair)), up(pair)])
    ring = lax.dynamic_slice_in_dim(jnp.concatenate([ring, ring]), RING - z, RING, 0)
    params = jnp.transpose(ring, (2, 0, 1, 3)).reshape(16, model)

    own_half = lax.dynamic_slice_in_dim(qkv_weight, core * half_model, half_model, 2)
    other_half = lax.dynamic_slice_in_dim(qkv_weight, (1 - core) * half_model, half_model, 2)
    qkv_pieces = [p for pieces in ring_gather(own_half, across(other_half)) for p in pieces]
    below, above = up(out_weight), down(out_weight)
    out_ring = [out_weight, above, up(below), below]
    out_pieces = [p for piece in out_ring for p in (piece, across(piece))]

    late = (cotangent[:, 0], w_gate[0], w_up[0], w_down[0])
    late, _ = lax.optimization_barrier((late, (xa, xb)))
    cot, gate_w, up_w, down_w = late
    ca, cb = leave(cot)
    mid = model // 2
    first = jnp.stack([gate_w[:mid], up_w[:mid], down_w[:mid]])
    second = jnp.stack([gate_w[mid:], up_w[mid:], down_w[mid:]])
    expert_pieces = [p for pieces in ring_gather(first, second) for p in pieces]

    cosine, sine = (jnp.asarray(t) for t in rope_tables(length))
    q, k, v, normed_in, x_all, w_all = kernel_call(
        project_kernel,
        idx,
        [xa, xb, ya, yb, params, cosine, sine, *qkv_pieces],
        [((length, half_model), BF)] * 3
        + [((length, model), BF)] * 2
        + [((model, 3 * half_model), BF)],
        flops=2 * length * model * 3 * half_model,
    )
    pairs = half_model // (2 * HEAD_DIM)
    lanes = 2 * HEAD_DIM
    by_pair = pl.BlockSpec((length, lanes), lambda h: (0, h))
    half_by_pair = pl.BlockSpec((length // 2, lanes), lambda h: (0, h))
    all_of = pl.BlockSpec(memory_space=pltpu.VMEM)
    lse_spec = pl.BlockSpec((1, 8, length), lambda h: (h, 0, 0))
    keep, send, lse = kernel_call(
        attend_kernel,
        idx,
        [q, k, v, seg_row, seg_col],
        [((length // 2, half_model), BF)] * 2 + [((pairs, 8, length), F32)],
        flops=4 * length * length * half_model,
        grid=(pairs,),
        in_specs=[by_pair] * 3 + [all_of] * 2,
        out_specs=[half_by_pair] * 2 + [lse_spec],
    )
    recv = across(send)

    g_slots = kernel_call(
        grad_slots_kernel,
        idx,
        [sa, sb, ca, cb],
        [((slots, model), BF)] * RING,
        flops=2 * RING * slots * 2 * rows * model,
    )
    g_mine = [g_slots[0]] + [over(g_slots[i], i) for i in range(1, RING)]
    g_theirs = [across(g) for g in g_mine]
    hidden, ow_all, state, *sent = kernel_call(
        route_kernel,
        idx,
        [keep, recv, xa, xb, params, sa, sb, *out_pieces],
        [((2 * rows, model), F32), ((model, model), BF), ((24, 2 * rows), F32)]
        + [((slots + 16, model), BF)] * RING,
        flops=2 * 2 * rows * model * model + 2 * RING * slots * 2 * rows * model,
    )
    t_mine = [sent[0]] + [over(sent[i], i) for i in range(1, RING)]
    t_theirs = [across(t) for t in t_mine]

    count = 8 * slots
    hidden_units = RING * w_gate.shape[2]
    tile_of = lambda n: pl.BlockSpec((2 * slots, n), lambda j: (j, 0))
    t_all, g_all, inner, gate_g, up_g, down_all, *entry = kernel_call(
        expert_kernel,
        idx,
        [*t_mine, *t_theirs, *g_mine, *g_theirs, *expert_pieces],
        [((count, model), BF)] * 2
        + [((count, hidden_units), BF)] * 3
        + [((model, hidden_units), BF)]
        + [((slots + 16, model), BF)] * 8,
        flops=10 * count * model * hidden_units,
        grid=(4,),
        in_specs=[all_of] * 24,
        out_specs=[tile_of(model)] * 2 + [tile_of(hidden_units)] * 3 + [all_of] * 9,
        scratch=[
            pltpu.VMEM((count, model), BF),
            pltpu.VMEM((count, model), BF),
            pltpu.VMEM((count, 128), F32),
            pltpu.VMEM((model, hidden_units), BF),
            pltpu.VMEM((model, hidden_units), BF),
            pltpu.VMEM((8, slots + 16, model), BF),
        ],
    )

    def give_back(parts):
        sums = [
            (parts[i].astype(F32) + across(parts[RING + i]).astype(F32)).astype(BF)
            for i in range(RING)
        ]
        return [sums[0]] + [over(sums[i], i) for i in range(1, RING)]

    entry_back = give_back(entry)
    out_parts = kernel_call(
        expert_out_kernel,
        idx,
        [inner, down_all],
        [((slots, model), BF)] * 8,
        flops=2 * count * model * hidden_units,
        grid=(4,),
        in_specs=[tile_of(hidden_units), all_of],
        out_specs=[all_of] * 8,
    )
    out_back = give_back(out_parts)
    chunk_of = pl.BlockSpec((count, w_gate.shape[2]), lambda j: (0, j))
    own_grad, *far_grads = kernel_call(
        expert_grads_kernel,
        idx,
        [t_all, g_all, inner, gate_g, up_g],
        [((3, model, w_gate.shape[2]), F32)] + [((3, mid, w_gate.shape[2]), BF)] * 6,
        flops=6 * count * model * hidden_units,
        grid=(RING,),
        in_specs=[all_of] * 2 + [chunk_of] * 3,
        out_specs=[all_of] * 7,
    )
    grad_first, grad_second = ring_sum(
        (own_grad[:, :mid], own_grad[:, mid:]),
        [(far_grads[2 * i], far_grads[2 * i + 1]) for i in range(3)],
    )
    expert_grads = jnp.concatenate([grad_first, grad_second], axis=1)

    grad_hidden, grad_low, ga_own, ga_send, la, lb, small_grad = kernel_call(
        hidden_back_kernel,
        idx,
        [hidden, state, sa, sb, ca, cb, params, ow_all, *entry_back],
        [((2 * rows, model), F32), ((2 * rows, model), BF)]
        + [((2 * rows, half_model), BF)] * 2
        + [((8, rows), F32)] * 2
        + [((16, model), F32)],
        flops=2 * 2 * rows * model * model + 2 * RING * slots * 2 * rows * model,
    )
    ga_other = across(ga_send)
    logit_grad = jnp.swapaxes(come_home(la, lb), 1, 2)[:, None]
    oa, ob = kernel_call(
        output_kernel,
        idx,
        [hidden, state, sa, sb, params, *out_back],
        [((rows, model), BF)] * 2,
        flops=4 * RING * slots * 2 * rows * model,
    )
    output = come_home(oa, ob)[:, None]
    og_own, og_send = kernel_call(
        out_grad_kernel,
        idx,
        [keep, recv, grad_low, small_grad],
        [((RING, model // 8, model + 128), BF)] * 2,
        flops=2 * 2 * rows * model * model,
        scratch=[pltpu.VMEM((model, model + 128), BF)],
    )
    og_sum = og_own.astype(F32) + across(og_send).astype(F32)
    og_low = og_sum.astype(BF)
    cut = model // 16
    out_grad = ring_sum(
        (og_sum[0, :cut], og_sum[0, cut:]),
        [(og_low[i, :cut], og_low[i, cut:]) for i in range(1, RING)],
    )
    out_grad = jnp.concatenate(plane_sum(*out_grad), axis=0)
    small_grad = out_grad[:, model : model + 16].T
    grad_out = out_grad[:, :model]

    dq, dk, dv = kernel_call(
        attend_back_kernel,
        idx,
        [q, k, v, ga_own, ga_other, seg_row, seg_col, lse, cosine, sine],
        [((length, half_model), BF)] * 3,
        flops=10 * length * length * half_model,
        grid=(pairs,),
        in_specs=[by_pair] * 3 + [half_by_pair] * 2 + [all_of] * 2 + [lse_spec] + [all_of] * 2,
        out_specs=[by_pair] * 3,
        scratch=[pltpu.VMEM((length, lanes), F32)] * 2,
    )
    depth = model // 8
    columns = 3 * half_model + 128
    qkv_own, *rest = kernel_call(
        project_back_kernel,
        idx,
        [dq, dk, dv, normed_in, x_all, w_all],
        [((2 * depth, columns), F32)]
        + [((depth, columns), BF)] * 6
        + [((2 * rows, model), BF)] * 2,
        flops=4 * length * model * 3 * half_model,
        scratch=[pltpu.VMEM((model, columns), F32)],
    )
    far, gn_keep, gn_send = rest[:6], rest[6], rest[7]
    ia, ib = kernel_call(
        input_back_kernel,
        idx,
        [gn_keep, across(gn_send), grad_hidden, xa, xb, params],
        [((rows, model), BF)] * 2,
        flops=0,
    )
    input_grad = come_home(ia, ib).astype(F32)[:, None]
    first, second = ring_sum(
        (qkv_own[:depth], qkv_own[depth:]), [(far[2 * i], far[2 * i + 1]) for i in range(3)]
    )
    mine = jnp.where(core == 0, first, second)
    theirs = across(jnp.where(core == 0, second, first).astype(BF)).astype(F32)
    mine, theirs = plane_sum(mine, theirs)
    left, right = jnp.where(core == 0, mine, theirs), jnp.where(core == 0, theirs, mine)
    grad_qkv = jnp.stack(
        [
            jnp.concatenate(
                [
                    left[:, j * half_model : (j + 1) * half_model],
                    right[:, j * half_model : (j + 1) * half_model],
                ],
                axis=1,
            )
            for j in range(3)
        ]
    )
    gain_first = mine[:, 3 * half_model] + theirs[:, 3 * half_model]
    grad_gain = jnp.stack([gain_first, small_grad[14]])
    return (
        output,
        input_grad,
        logit_grad,
        grad_qkv,
        grad_out,
        grad_gain,
        small_grad[:8].T,
        small_grad[8:12].T,
        small_grad[12:14],
        expert_grads[0][None],
        expert_grads[1][None],
        expert_grads[2][None],
    )


def whole_sequence_fits(mesh):
    return (mesh.shape["experts"], mesh.shape["context"], mesh.shape["dp"]) == (4, 4, 2)


def solution(mesh):
    local = chip_local if whole_sequence_fits(mesh) else general_local
    in_specs = (
        P(None, ("experts", "dp"), "context", None),
        P(None, ("experts", "dp"), "context", None),
        P(None, ("context", "dp"), None),
        P(("context", "dp"), None),
        P(None, ("context", "dp")),
        P(("context", "dp"), None),
        P(("context", "dp"), None),
        P(None, ("context", "dp")),
        P("experts", None, ("context", "dp")),
        P("experts", None, ("context", "dp")),
        P("experts", None, ("context", "dp")),
        P(None, ("experts", "dp"), "context", None),
        P(None, ("experts", "dp"), "context", None),
        P(None, ("experts", "dp"), "context"),
    )
    out_specs = (
        P(None, ("experts", "dp"), "context", None),
        P(None, ("experts", "dp"), "context", None),
        P(None, ("experts", "dp"), "context", None),
        P(None, ("context", "dp"), None),
        P(("context", "dp"), None),
        P(None, ("context", "dp")),
        P(("context", "dp"), None),
        P(("context", "dp"), None),
        P(None, ("context", "dp")),
        P("experts", None, ("context", "dp")),
        P("experts", None, ("context", "dp")),
        P("experts", None, ("context", "dp")),
    )
    return jax.shard_map(local, mesh=mesh, in_specs=in_specs, out_specs=out_specs, check_vma=False)
```

```python
import functools
import functools
import math

import jax
import jax.numpy as jnp
import numpy as np
from jax import lax
from jax.experimental import pallas as pl
from jax.experimental.pallas import tpu as pltpu
from jax.sharding import PartitionSpec as P

HEAD_DIM = 64
FF = 2048


EPSILON = 1e-05
MASKED = -1e30


def rotate(values, positions, direction):
    half_dim = values.shape[-1] // 2
    inverse = 10000.0 ** (-jnp.arange(half_dim, dtype=jnp.float32) / half_dim)
    angles = positions.astype(jnp.float32)[:, None] * inverse[None, :]
    cosine = jnp.cos(angles)[:, None, :]
    sine_part = jnp.sin(angles)[:, None, :]
    first_half = values[..., :half_dim]
    second = values[..., half_dim:]
    return jnp.concatenate(
        [
            first_half * cosine - direction * second * sine_part,
            second * cosine + direction * first_half * sine_part,
        ],
        axis=-1,
    )


def softmax_last(logits):
    shifted = jnp.exp(logits - jnp.max(logits, axis=-1, keepdims=True))
    return shifted / jnp.sum(shifted, axis=-1, keepdims=True)


def norm_scale(values):
    return lax.rsqrt(jnp.mean(values * values, axis=-1, keepdims=True) + EPSILON)


def norm_back(grad_in, values, factor, gain_vec):
    scaled = grad_in * gain_vec
    grad_gain = jnp.sum(grad_in * values * factor, axis=0)
    grad_values = factor * scaled - values * factor * factor * factor * jnp.mean(
        scaled * values, axis=-1, keepdims=True
    )
    return (grad_values, grad_gain)


def masked_scores(
    queries, key_rows, query_segments, key_segments, query_positions, key_positions, score_scale
):
    scores = (
        jnp.einsum("qhd,khd->hqk", queries, key_rows, preferred_element_type=jnp.float32)
        * score_scale
    )
    allowed = (query_segments[:, None] == key_segments[None, :]) & (
        key_positions[None, :] <= query_positions[:, None]
    )
    return (jnp.where(allowed[None], scores, MASKED), allowed)


def general_local(
    inputs,
    cotangent,
    qkv_weight,
    out_weight,
    norm_gains,
    route_weight,
    const_gate,
    const_vec,
    w_gate,
    w_up,
    w_down,
    prev_logits,
    routes,
    segments,
):
    micro_count = inputs.shape[0]
    row_count = inputs.shape[2]
    model_width = inputs.shape[3]
    head_count = model_width // HEAD_DIM
    score_scale = HEAD_DIM ** (-0.5)
    local_experts = w_gate.shape[0]
    experts = local_experts * lax.axis_size("experts")
    capacity = row_count * 5 // 16
    routed = prev_logits.shape[3]
    assigned = 2 * row_count
    head_shape = (row_count, head_count, HEAD_DIM)
    positions = lax.axis_index("context") * row_count + jnp.arange(row_count, dtype=jnp.int32)
    grad_qkv = jnp.zeros((3, model_width, model_width), jnp.float32)
    grad_out = jnp.zeros((model_width, model_width), jnp.float32)
    gain_first = jnp.zeros((model_width,), jnp.float32)
    gain_second = jnp.zeros((model_width,), jnp.float32)
    grad_vec = jnp.zeros((2, model_width), jnp.float32)
    grad_route = jnp.zeros((model_width, routed), jnp.float32)
    grad_mixer = jnp.zeros((model_width, 4), jnp.float32)
    grad_gate = jnp.zeros((local_experts, model_width, FF), jnp.float32)
    grad_up = jnp.zeros((local_experts, model_width, FF), jnp.float32)
    grad_down = jnp.zeros((local_experts, model_width, FF), jnp.float32)
    output_rows = []
    input_rows = []
    logit_rows = []
    for batch_index in range(micro_count):
        qkv_full, out_full, gains, vectors, route_full, mixer_full = (
            lax.all_gather(qkv_weight, ("context", "dp"), axis=1, tiled=True),
            lax.all_gather(out_weight, ("context", "dp"), axis=0, tiled=True),
            lax.all_gather(
                norm_gains.astype(jnp.bfloat16), ("context", "dp"), axis=1, tiled=True
            ).astype(norm_gains.dtype),
            lax.all_gather(
                const_vec.astype(jnp.bfloat16), ("context", "dp"), axis=1, tiled=True
            ).astype(const_vec.dtype),
            lax.all_gather(route_weight, ("context", "dp"), axis=0, tiled=True),
            lax.all_gather(const_gate, ("context", "dp"), axis=0, tiled=True),
        )
        gate_full, up_full, down_full = (
            lax.all_gather(w_gate, ("context", "dp"), axis=2, tiled=True),
            lax.all_gather(w_up, ("context", "dp"), axis=2, tiled=True),
            lax.all_gather(w_down, ("context", "dp"), axis=2, tiled=True),
        )
        token_rows = inputs[batch_index, 0].astype(jnp.float32)
        seg_rows = segments[batch_index, 0]
        route_rows = routes[batch_index, 0]
        grad_rows = cotangent[batch_index, 0].astype(jnp.float32)
        scale_first = norm_scale(token_rows)
        normed_in = (token_rows * scale_first * gains[0]).astype(jnp.bfloat16)
        projected = jnp.einsum(
            "qd,cde->cqe", normed_in, qkv_full, preferred_element_type=jnp.float32
        )
        queries = rotate(projected[0].reshape(head_shape), positions, 1.0).astype(jnp.bfloat16)
        rotated_keys = rotate(projected[1].reshape(head_shape), positions, 1.0).astype(jnp.bfloat16)
        values = projected[2].reshape(head_shape).astype(jnp.bfloat16)
        row_peak = jnp.full((head_count, row_count), MASKED, jnp.float32)
        key_block = lax.all_gather(rotated_keys, "context", axis=0, tiled=True)
        value_block = lax.all_gather(values, "context", axis=0, tiled=True)
        segment_block = lax.all_gather(seg_rows, "context", axis=0, tiled=True)
        key_positions = jnp.arange(key_block.shape[0], dtype=jnp.int32)
        scores, allowed = masked_scores(
            queries, key_block, seg_rows, segment_block, positions, key_positions, score_scale
        )
        new_peak = jnp.maximum(row_peak, jnp.max(scores, axis=-1))
        expo = jnp.where(allowed[None], jnp.exp(scores - new_peak[:, :, None]), 0.0)
        weighted = jnp.einsum(
            "hqk,khd->hqd",
            expo.astype(jnp.bfloat16),
            value_block,
            preferred_element_type=jnp.float32,
        )
        row_peak, row_total, weighted = (new_peak, jnp.sum(expo, axis=-1), weighted)
        log_total = row_peak + jnp.log(row_total)
        attn_heads = jnp.transpose(weighted / row_total[:, :, None], (1, 0, 2))
        attended = attn_heads.reshape(row_count, model_width).astype(jnp.bfloat16)
        hidden = token_rows + jnp.dot(attended, out_full, preferred_element_type=jnp.float32)
        scale_second = norm_scale(hidden)
        normed = hidden * scale_second * gains[1]
        normed_low = normed.astype(jnp.bfloat16)
        logits = (
            jnp.dot(normed_low, route_full, preferred_element_type=jnp.float32)
            + prev_logits[batch_index, 0]
        )
        probabilities = softmax_last(logits)
        gate_values = jnp.take_along_axis(probabilities, route_rows, axis=-1)
        route_ids = route_rows.reshape(-1)
        routed_ffn = route_ids < experts
        onehot = (route_ids[:, None] == jnp.arange(experts, dtype=jnp.int32)[None, :]).astype(
            jnp.int32
        )
        slot_index = jnp.sum((jnp.cumsum(onehot, axis=0) - onehot) * onehot, axis=-1)
        slot_table = (
            jnp.full((experts, capacity), assigned, jnp.int32)
            .at[jnp.where(routed_ffn, route_ids, experts), slot_index]
            .set(jnp.arange(assigned, dtype=jnp.int32), mode="drop")
        )
        token_of = jnp.where(slot_table < assigned, slot_table // 2, row_count)
        pad_rows = jnp.concatenate([normed_low, jnp.zeros((1, model_width), jnp.bfloat16)], axis=0)
        received = lax.all_to_all(
            pad_rows[token_of], "experts", split_axis=0, concat_axis=1, tiled=True
        )
        gate_act = jnp.einsum(
            "erd,edf->erf", received, gate_full, preferred_element_type=jnp.float32
        )
        up_act = jnp.einsum("erd,edf->erf", received, up_full, preferred_element_type=jnp.float32)
        sigma = jax.nn.sigmoid(gate_act)
        silu_act = gate_act * sigma
        inner_low = (silu_act * up_act).astype(jnp.bfloat16)
        expert_low = jnp.einsum(
            "erf,edf->erd", inner_low, down_full, preferred_element_type=jnp.float32
        ).astype(jnp.bfloat16)
        returned = lax.all_to_all(
            expert_low, "experts", split_axis=1, concat_axis=0, tiled=True
        ).reshape(experts * capacity, model_width)
        pick_index = jnp.where(routed_ffn, route_ids * capacity + slot_index, 0)
        expert_out = jnp.where(
            routed_ffn[:, None], returned[pick_index].astype(jnp.float32), 0.0
        ).reshape(row_count, 2, model_width)
        const_mix = softmax_last(
            jnp.dot(normed_low, mixer_full, preferred_element_type=jnp.float32).reshape(
                row_count, 2, 2
            )
        )
        const_out = (
            const_mix[:, :, 0:1] * normed[:, None, :] + const_mix[:, :, 1:2] * vectors[None, :, :]
        )
        copy_mask = (route_rows == experts + 1).astype(jnp.float32)
        const_pick = (
            route_rows[:, :, None] == experts + 2 + jnp.arange(2, dtype=jnp.int32)[None, None, :]
        ).astype(jnp.float32)
        branch = (
            expert_out
            + copy_mask[:, :, None] * normed[:, None, :]
            + jnp.einsum("qjc,qcd->qjd", const_pick, const_out, precision=lax.Precision.HIGHEST)
        )
        output_rows.append(
            (hidden + jnp.sum(gate_values[:, :, None] * branch, axis=1)).astype(jnp.bfloat16)
        )
        grad_branch = gate_values[:, :, None] * grad_rows[:, None, :]
        grad_gates = jnp.sum(grad_rows[:, None, :] * branch, axis=-1)
        grad_probs = jnp.sum(
            (route_rows[:, :, None] == jnp.arange(routed, dtype=jnp.int32)[None, None, :]).astype(
                jnp.float32
            )
            * grad_gates[:, :, None],
            axis=1,
        )
        grad_logits = probabilities * (
            grad_probs - jnp.sum(probabilities * grad_probs, axis=-1, keepdims=True)
        )
        logit_rows.append(grad_logits)
        normed_wide = normed_low.astype(jnp.float32)
        grad_route = grad_route + jnp.dot(
            normed_wide.T, grad_logits, precision=lax.Precision.HIGHEST
        )
        grad_normed = jnp.dot(
            grad_logits, route_full.astype(jnp.float32).T, precision=lax.Precision.HIGHEST
        )
        grad_normed = grad_normed + jnp.sum(copy_mask[:, :, None] * grad_branch, axis=1)
        grad_const = jnp.einsum(
            "qjc,qjd->qcd", const_pick, grad_branch, precision=lax.Precision.HIGHEST
        )
        grad_mix = jnp.stack(
            [
                jnp.sum(grad_const * normed[:, None, :], axis=-1),
                jnp.sum(grad_const * vectors[None, :, :], axis=-1),
            ],
            axis=-1,
        )
        grad_mix_logits = (
            const_mix * (grad_mix - jnp.sum(const_mix * grad_mix, axis=-1, keepdims=True))
        ).reshape(row_count, 4)
        grad_mixer = grad_mixer + jnp.dot(
            normed_wide.T, grad_mix_logits, precision=lax.Precision.HIGHEST
        )
        grad_normed = grad_normed + jnp.dot(
            grad_mix_logits, mixer_full.astype(jnp.float32).T, precision=lax.Precision.HIGHEST
        )
        grad_normed = grad_normed + jnp.sum(const_mix[:, :, 0:1] * grad_const, axis=1)
        grad_vec = grad_vec + jnp.sum(const_mix[:, :, 1:2] * grad_const, axis=0)
        grad_slots = jnp.where(
            routed_ffn[:, None], grad_branch.reshape(assigned, model_width), 0.0
        ).astype(jnp.bfloat16)
        grad_pad = jnp.concatenate([grad_slots, jnp.zeros((1, model_width), jnp.bfloat16)], axis=0)
        grad_received = lax.all_to_all(
            grad_pad[slot_table], "experts", split_axis=0, concat_axis=1, tiled=True
        )
        grad_inner = jnp.einsum(
            "erd,edf->erf", grad_received, down_full, preferred_element_type=jnp.float32
        )
        grad_down = grad_down + jnp.einsum(
            "erd,erf->edf", grad_received, inner_low, preferred_element_type=jnp.float32
        )
        grad_gate_low = (grad_inner * up_act * sigma * (1.0 + gate_act * (1.0 - sigma))).astype(
            jnp.bfloat16
        )
        grad_up_low = (grad_inner * silu_act).astype(jnp.bfloat16)
        grad_gate = grad_gate + jnp.einsum(
            "erd,erf->edf", received, grad_gate_low, preferred_element_type=jnp.float32
        )
        grad_up = grad_up + jnp.einsum(
            "erd,erf->edf", received, grad_up_low, preferred_element_type=jnp.float32
        )
        grad_entry = (
            jnp.einsum("erf,edf->erd", grad_gate_low, gate_full, preferred_element_type=jnp.float32)
            + jnp.einsum("erf,edf->erd", grad_up_low, up_full, preferred_element_type=jnp.float32)
        ).astype(jnp.bfloat16)
        grad_back = lax.all_to_all(
            grad_entry, "experts", split_axis=1, concat_axis=0, tiled=True
        ).reshape(experts * capacity, model_width)
        grad_normed = grad_normed + jnp.sum(
            jnp.where(routed_ffn[:, None], grad_back[pick_index].astype(jnp.float32), 0.0).reshape(
                row_count, 2, model_width
            ),
            axis=1,
        )
        grad_hidden_norm, gain_term = norm_back(grad_normed, hidden, scale_second, gains[1])
        gain_second = gain_second + gain_term
        grad_hidden = grad_rows + grad_hidden_norm
        grad_attn_low = grad_hidden.astype(jnp.bfloat16)
        grad_out = grad_out + jnp.dot(attended.T, grad_attn_low, preferred_element_type=jnp.float32)
        grad_attended = (
            jnp.dot(grad_attn_low, out_full.T, preferred_element_type=jnp.float32)
            .astype(jnp.bfloat16)
            .reshape(head_shape)
        )
        delta = jnp.sum(grad_attended.astype(jnp.float32) * attn_heads, axis=-1).T
        zero_heads = jnp.zeros(head_shape, jnp.float32)
        key_all, value_all, segment_all = (
            lax.all_gather(rotated_keys, "context", axis=0, tiled=True),
            lax.all_gather(values, "context", axis=0, tiled=True),
            lax.all_gather(seg_rows, "context", axis=0, tiled=True),
        )
        total_keys = key_all.shape[0]
        group_count = math.gcd(total_keys // row_count, max(1, 512 // row_count))
        block_rows = row_count * group_count
        block_count = total_keys // block_rows

        def back_block(grad_query, block_parts):
            key_block, value_block, segment_block, block_start = block_parts
            key_positions = block_start + jnp.arange(block_rows, dtype=jnp.int32)
            scores, allowed = masked_scores(
                queries, key_block, seg_rows, segment_block, positions, key_positions, score_scale
            )
            probability = jnp.where(allowed[None], jnp.exp(scores - log_total[:, :, None]), 0.0)
            grad_prob = jnp.einsum(
                "qhd,khd->hqk", grad_attended, value_block, preferred_element_type=jnp.float32
            )
            grad_score = (probability * (grad_prob - delta[:, :, None])).astype(jnp.bfloat16)
            grad_query = (
                grad_query
                + jnp.einsum(
                    "hqk,khd->qhd", grad_score, key_block, preferred_element_type=jnp.float32
                )
                * score_scale
            )
            grad_key = (
                jnp.einsum("hqk,qhd->khd", grad_score, queries, preferred_element_type=jnp.float32)
                * score_scale
            )
            grad_value = jnp.einsum(
                "hqk,qhd->khd",
                probability.astype(jnp.bfloat16),
                grad_attended,
                preferred_element_type=jnp.float32,
            )
            return (grad_query, (grad_key, grad_value))

        block_starts = jnp.arange(block_count, dtype=jnp.int32) * block_rows
        grad_query, (key_terms, value_terms) = lax.scan(
            back_block,
            zero_heads,
            (
                key_all.reshape(block_count, block_rows, head_count, HEAD_DIM),
                value_all.reshape(block_count, block_rows, head_count, HEAD_DIM),
                segment_all.reshape(block_count, block_rows),
                block_starts,
            ),
        )
        grad_key, grad_value = (
            lax.psum_scatter(
                key_terms.reshape(total_keys, head_count, HEAD_DIM).astype(jnp.bfloat16),
                "context",
                scatter_dimension=0,
                tiled=True,
            ).astype(jnp.float32),
            lax.psum_scatter(
                value_terms.reshape(total_keys, head_count, HEAD_DIM).astype(jnp.bfloat16),
                "context",
                scatter_dimension=0,
                tiled=True,
            ).astype(jnp.float32),
        )
        grad_projected = jnp.stack(
            [
                rotate(grad_query, positions, -1.0).reshape(row_count, model_width),
                rotate(grad_key, positions, -1.0).reshape(row_count, model_width),
                grad_value.reshape(row_count, model_width),
            ]
        ).astype(jnp.bfloat16)
        grad_qkv = grad_qkv + jnp.einsum(
            "qd,cqe->cde", normed_in, grad_projected, preferred_element_type=jnp.float32
        )
        grad_normed_in = jnp.einsum(
            "cqe,cde->qd", grad_projected, qkv_full, preferred_element_type=jnp.float32
        )
        grad_token_norm, gain_term = norm_back(grad_normed_in, token_rows, scale_first, gains[0])
        gain_first = gain_first + gain_term
        input_rows.append(grad_hidden + grad_token_norm)
    grad_gain = jnp.stack([gain_first, gain_second])
    (
        grad_qkv,
        grad_out,
        grad_gain,
        grad_vec,
        grad_route,
        grad_mixer,
        grad_gate,
        grad_up,
        grad_down,
    ) = (
        lax.psum_scatter(
            grad_qkv.astype(jnp.bfloat16), ("context", "dp"), scatter_dimension=1, tiled=True
        ).astype(jnp.float32),
        lax.psum_scatter(
            grad_out.astype(jnp.bfloat16), ("context", "dp"), scatter_dimension=0, tiled=True
        ).astype(jnp.float32),
        lax.psum_scatter(
            grad_gain.astype(jnp.bfloat16), ("context", "dp"), scatter_dimension=1, tiled=True
        ).astype(jnp.float32),
        lax.psum_scatter(
            grad_vec.astype(jnp.bfloat16), ("context", "dp"), scatter_dimension=1, tiled=True
        ).astype(jnp.float32),
        lax.psum_scatter(
            grad_route.astype(jnp.bfloat16), ("context", "dp"), scatter_dimension=0, tiled=True
        ).astype(jnp.float32),
        lax.psum_scatter(
            grad_mixer.astype(jnp.bfloat16), ("context", "dp"), scatter_dimension=0, tiled=True
        ).astype(jnp.float32),
        lax.psum_scatter(
            grad_gate.astype(jnp.bfloat16), ("context", "dp"), scatter_dimension=2, tiled=True
        ).astype(jnp.float32),
        lax.psum_scatter(
            grad_up.astype(jnp.bfloat16), ("context", "dp"), scatter_dimension=2, tiled=True
        ).astype(jnp.float32),
        lax.psum_scatter(
            grad_down.astype(jnp.bfloat16), ("context", "dp"), scatter_dimension=2, tiled=True
        ).astype(jnp.float32),
    )
    grad_qkv, grad_out, grad_gain, grad_vec, grad_route, grad_mixer = (
        lax.psum(grad_qkv.astype(jnp.bfloat16), "experts").astype(jnp.float32),
        lax.psum(grad_out.astype(jnp.bfloat16), "experts").astype(jnp.float32),
        lax.psum(grad_gain.astype(jnp.bfloat16), "experts").astype(jnp.float32),
        lax.psum(grad_vec.astype(jnp.bfloat16), "experts").astype(jnp.float32),
        lax.psum(grad_route.astype(jnp.bfloat16), "experts").astype(jnp.float32),
        lax.psum(grad_mixer.astype(jnp.bfloat16), "experts").astype(jnp.float32),
    )
    output = jnp.stack(output_rows)[:, None]
    input_grad = jnp.stack(input_rows)[:, None]
    logit_grad = jnp.stack(logit_rows)[:, None]
    return (
        output,
        input_grad,
        logit_grad,
        grad_qkv,
        grad_out,
        grad_gain,
        grad_route,
        grad_mixer,
        grad_vec,
        grad_gate,
        grad_up,
        grad_down,
    )


BF = jnp.bfloat16
F32 = jnp.float32
BLOCK = 256
RING = 4
VMEM_BYTES = 60 * 2**20


def dot(left, right, left_dim, right_dim):
    return lax.dot_general(
        left, right, (((left_dim,), (right_dim,)), ((), ())), preferred_element_type=F32
    )


def iota(shape, dim):
    return lax.broadcasted_iota(jnp.int32, shape, dim)


def split3(values):
    high = values.astype(BF).astype(F32)
    rest = values - high
    middle = rest.astype(BF).astype(F32)
    return (high, middle, rest - middle)


def split2(values):
    high = values.astype(BF)
    return (high, (values - high.astype(F32)).astype(BF))


def rows_of(parts, count):
    width = parts[0].shape[1]
    index = iota((count, width), 0)
    total = jnp.zeros((count, width), F32)
    for place, part in enumerate(parts):
        total = jnp.where(index == place, jnp.broadcast_to(part, (count, width)), total)
    return total


def column_of(row, width=128):
    stacked = rows_of(split3(row), 16).astype(BF)
    return dot(stacked, jnp.ones((16, width), BF), 0, 0)


def wide(column, copies):
    return jnp.concatenate([column] * copies, axis=1)


def kernel_call(
    body, idx, args, outs, flops, grid=None, in_specs=None, out_specs=None, scratch=(), share=1
):
    moved = sum(a.size * a.dtype.itemsize for a in args)
    moved += sum(math.prod(s) * jnp.dtype(d).itemsize for s, d in outs)
    whole = pl.BlockSpec(memory_space=pltpu.VMEM)
    extra = {} if grid is None else {"grid": grid}
    return pl.pallas_call(
        body,
        out_shape=[jax.ShapeDtypeStruct(s, d) for s, d in outs],
        in_specs=[pl.BlockSpec(memory_space=pltpu.SMEM)]
        + (in_specs if in_specs is not None else [whole] * len(args)),
        out_specs=out_specs if out_specs is not None else [whole] * len(outs),
        scratch_shapes=list(scratch),
        compiler_params=pltpu.CompilerParams(vmem_limit_bytes=VMEM_BYTES),
        cost_estimate=pl.CostEstimate(
            flops=flops // share, bytes_accessed=moved // share, transcendentals=0
        ),
        **extra,
    )(idx, *args)


def rope_tables(length):
    half = HEAD_DIM // 2
    inverse = (10000.0 ** (-np.arange(half, dtype=np.float32) / half)).astype(np.float32)
    angles = (np.arange(length, dtype=np.float32)[:, None] * inverse[None, :]).astype(np.float64)
    cosine, sine = np.cos(angles), np.sin(angles)
    cosine = np.concatenate([cosine] * 4, axis=1).astype(np.float32)
    sine = np.concatenate([-sine, sine] * 2, axis=1).astype(np.float32)
    return cosine, sine


def turn(values, cosine, sine, direction):
    width = values.shape[1]
    copies = width // cosine.shape[1]
    ahead = pltpu.roll(values, width - HEAD_DIM // 2, 1)
    behind = pltpu.roll(values, HEAD_DIM // 2, 1)
    first = (iota(values.shape, 1) & (HEAD_DIM - 1)) < HEAD_DIM // 2
    partner = jnp.where(first, ahead, behind)
    return values * wide(cosine, copies) + direction * (partner * wide(sine, copies))


def project_kernel(idx, xa, xb, theirs, columns, w_ref, cosine, sine, *outs):
    q_ref, k_ref, v_ref, normed_ref, params_ref, seg_row, seg_col, x_ref = outs
    core, flip = idx[2], idx[3]
    row, column = iota((16, 128), 0), iota((16, 128), 1)
    spread = (row == column) | ((row >= 12) & ((column == row + 4) | (column == row + 8)))
    params_ref[...] = dot(jnp.where(spread, 1.0, 0.0).astype(BF), columns[...], 1, 1)
    sources = (
        (xa, core, 0),
        (xb, core, 1),
        (theirs.at[0], 1 - core, 0),
        (theirs.at[1], 1 - core, 1),
    )
    for ref, half, slot in sources:
        block = 2 * half + (flip if slot == 0 else 1 - flip)
        rows = pl.ds(pl.multiple_of(block * BLOCK, BLOCK), BLOCK)
        x_ref[rows, :] = ref[:BLOCK, :]
        segment = ref[ref.shape[0] - 16 :, :BLOCK].astype(F32)[10:11]
        seg_row[:, rows] = jnp.broadcast_to(segment, (8, BLOCK))
        seg_col[rows, :] = column_of(segment)
    gain = params_ref[14:15, :]

    def step(i, carry):
        rows = pl.ds(pl.multiple_of(i * BLOCK, BLOCK), BLOCK)
        x = x_ref[rows, :].astype(F32)
        normed = (x * norm_scale(x) * gain).astype(BF)
        normed_ref[rows, :] = normed
        cos_rows, sin_rows = cosine[rows, :], sine[rows, :]
        queries = turn(dot(normed, w_ref[0], 1, 0), cos_rows, sin_rows, 1.0)
        q_ref[rows, :] = (queries * HEAD_DIM**-0.5).astype(BF)
        keys = turn(dot(normed, w_ref[1], 1, 0), cos_rows, sin_rows, 1.0)
        k_ref[rows, :] = keys.astype(BF)
        v_ref[rows, :] = dot(normed, w_ref[2], 1, 0).astype(BF)
        return carry

    lax.fori_loop(0, x_ref.shape[0] // BLOCK, step, 0)


def mask_of(seg_row, seg_col, i):
    n = (i + 1) * BLOCK
    mine = seg_row[:1, i * BLOCK : n]
    key_index, query_index = iota((BLOCK, BLOCK), 0), iota((BLOCK, BLOCK), 1)
    last = (seg_col[i * BLOCK : n, :1] == mine) & (key_index <= query_index)
    bias = jnp.where(last, 0.0, MASKED)
    if i > 0:
        before = jnp.where(seg_col[: i * BLOCK, :1] == mine, 0.0, MASKED)
        bias = jnp.concatenate([before, bias], axis=0)
    return bias


def attend_kernel(idx, q_ref, k_ref, v_ref, seg_row, seg_col, keep_ref, send_ref, lse_ref):
    core, flip = idx[2], idx[3]
    low_lanes = iota((BLOCK, 2 * HEAD_DIM), 1) < HEAD_DIM
    for i in range(q_ref.shape[0] // BLOCK):
        n = (i + 1) * BLOCK
        queries = q_ref[i * BLOCK : n, :]
        keys, values = k_ref[:n, :], v_ref[:n, :]
        bias = mask_of(seg_row, seg_col, i)
        outs = []
        for head in range(2):
            mine = low_lanes if head == 0 else ~low_lanes
            scores = dot(keys, jnp.where(mine, queries, 0), 1, 1) + bias
            peak = jnp.max(scores, axis=0, keepdims=True)
            weights = jnp.exp(scores - peak)
            total = jnp.sum(weights, axis=0, keepdims=True)
            out = dot(values, weights.astype(BF), 0, 0)
            outs.append(out[head * HEAD_DIM : (head + 1) * HEAD_DIM] / total)
            lse_ref[0, head : head + 1, i * BLOCK : n] = peak + jnp.log(total)
        attended = jnp.concatenate(outs, axis=0).T.astype(BF)
        half, slot = i // 2, (i % 2) ^ flip
        rows = pl.ds(pl.multiple_of(slot * BLOCK, BLOCK), BLOCK)

        @pl.when(half == core)
        def _():
            keep_ref[rows, :] = attended

        @pl.when(half != core)
        def _():
            send_ref[rows, :] = attended


def pair_back_kernel(
    first, idx, q_ref, k_ref, v_ref, own_ref, other_ref, seg_row, seg_col, lse_ref, cosine, sine,
    normed_ref, og_ref, og_recv, *refs,
):
    if first:
        small_ref, grads_ref, shared, key_sum, value_sum = refs
    else:
        grads_ref, shared, key_sum, value_sum = refs
    core, flip = idx[2], idx[3]
    lanes = 2 * HEAD_DIM
    low_lanes = iota((BLOCK, lanes), 1) < HEAD_DIM
    key_sum[...] = jnp.zeros(key_sum.shape, F32)
    value_sum[...] = jnp.zeros(value_sum.shape, F32)
    for i in range(q_ref.shape[0] // BLOCK):
        n = (i + 1) * BLOCK
        queries = q_ref[i * BLOCK : n, :]
        keys, values = k_ref[:n, :], v_ref[:n, :]
        bias = mask_of(seg_row, seg_col, i)
        half, slot = i // 2, (i % 2) ^ flip
        rows = pl.ds(pl.multiple_of(slot * BLOCK, BLOCK), BLOCK)
        grads = jnp.where(half == core, own_ref[rows, :], other_ref[rows, :])
        grad_queries = []
        for head in range(2):
            mine = low_lanes if head == 0 else ~low_lanes
            head_queries = jnp.where(mine, queries, 0)
            head_grads = jnp.where(mine, grads, 0)
            scores = dot(keys, head_queries, 1, 1) + bias
            weights = jnp.exp(scores - lse_ref[0, head : head + 1, i * BLOCK : n])
            grad_weights = dot(values, head_grads, 1, 1)
            delta = jnp.sum(weights * grad_weights, axis=0, keepdims=True)
            grad_scores = (weights * (grad_weights - delta)).astype(BF)
            key_sum[:n, :] += dot(grad_scores, head_queries, 1, 0)
            value_sum[:n, :] += dot(weights.astype(BF), head_grads, 1, 0)
            grad_queries.append(dot(grad_scores, keys, 0, 0))
        grad_query = jnp.where(low_lanes, grad_queries[0], grad_queries[1]) * HEAD_DIM**-0.5
        tile = slice(i * BLOCK, n)
        turned = turn(grad_query, cosine[tile, :], sine[tile, :], -1.0)
        grads_ref[tile, :lanes] = turned.astype(BF)
    for i in range(q_ref.shape[0] // BLOCK):
        tile = slice(i * BLOCK, (i + 1) * BLOCK)
        turned = turn(key_sum[tile, :], cosine[tile, :], sine[tile, :], -1.0)
        grads_ref[tile, lanes : 2 * lanes] = turned.astype(BF)
        grads_ref[tile, 2 * lanes :] = value_sum[tile, :].astype(BF)
    model = normed_ref.shape[1]
    depth = model // RING
    weight_grads = dot(normed_ref[...], grads_ref[...], 0, 0)
    out_grads = og_ref[...].astype(F32) + og_recv[...].astype(F32)
    for z in range(RING):
        rows = slice(z * depth, (z + 1) * depth)
        for j in range(3):
            piece = weight_grads[rows, j * lanes : (j + 1) * lanes]
            shared[j, z, :depth, :] = piece.astype(BF)
        shared[3, z, :depth, :] = out_grads[rows].astype(BF)
        if first:
            shard = depth // 2
            for j in range(2):
                lane = iota((model, lanes), 1)
                pick = iota((model, lanes), 0) == lane + (z * depth + j * shard)
                pick = jnp.where(pick & (lane < shard), 1.0, 0.0).astype(BF)
                picked = dot(small_ref[...].astype(BF), pick, 1, 0)
                shared[j, z, depth:, :] = picked.astype(BF)
            for j in range(2, RING):
                shared[j, z, depth:, :] = jnp.zeros((16, lanes), BF)


def routed_rows(small, routed):
    index = iota((routed, small.shape[1]), 0).astype(F32)
    return jnp.where((small[8:9, :] == index) | (small[9:10, :] == index), 1.0, 0.0)


def ranks_of(named):
    tokens = named.shape[1]
    before, here = iota((tokens, tokens), 0), iota((tokens, tokens), 1)
    earlier = (before < here) & (before // BLOCK == here // BLOCK)
    stacked = jnp.concatenate([named, jnp.zeros_like(named)], axis=0).astype(BF)
    return dot(stacked, jnp.where(earlier, 1.0, 0.0).astype(BF), 1, 0)[: named.shape[0]]


def pick_row(values, index):
    return jnp.sum(jnp.where(iota(values.shape, 0) == index, values, 0.0), axis=0, keepdims=True)


def slots_of(named, rank, expert, capacity):
    tokens = named.shape[1]
    place = pick_row(rank, expert)
    place = place + jnp.where(iota((1, tokens), 1) >= BLOCK, float(capacity), 0.0)
    slot = iota((2 * capacity, tokens), 0).astype(F32)
    taken = (slot == place) & (pick_row(named, expert) > 0.5)
    return jnp.where(taken, 1.0, 0.0).astype(BF)


def pair_of(first, second):
    return jnp.concatenate([first[:BLOCK, :], second[:BLOCK, :]], axis=0)


def small_of(xa, xb):
    blocks = []
    for packed in (xa, xb):
        values = packed[BLOCK:, :].astype(F32)
        width = values.shape[1] // 3
        logits = values[:8, :width] + values[:8, width : 2 * width] + values[:8, 2 * width :]
        blocks.append(jnp.concatenate([logits, values[8:, :width]], axis=0))
    return jnp.concatenate(blocks, axis=1)


def grad_slots_kernel(idx, xa, xb, ca, cb, out):
    named = routed_rows(small_of(xa, xb), 8)
    rank = ranks_of(named)
    grads = pair_of(ca, cb)
    for expert in range(out.shape[0]):
        taken = slots_of(named, rank, expert, out.shape[1] // 2)
        out[expert] = dot(taken, grads, 1, 0).astype(BF)


def route_kernel(idx, keep, recv, xa, xb, params, mine, theirs, *outs):
    hidden_ref, ow_ref, state_ref, out = outs
    core = idx[2]
    width = keep.shape[1]
    own = pl.ds(pl.multiple_of(core * width, 128), width)
    other = pl.ds(pl.multiple_of((1 - core) * width, 128), width)
    ow_ref[:, own] = mine[...]
    ow_ref[:, other] = theirs[...]
    hidden = (
        pair_of(xa, xb).astype(F32)
        + dot(keep[...], ow_ref[own, :], 1, 0)
        + dot(recv[...], ow_ref[other, :], 1, 0)
    )
    hidden_ref[...] = hidden
    normed = (hidden * norm_scale(hidden) * params[15:16, :]).astype(BF)
    small = small_of(xa, xb)
    logits = dot(params[...].astype(BF), normed, 1, 1)
    named = routed_rows(small, 8)
    rank = ranks_of(named)
    shifted = logits[:8] + small[:8]
    shifted = jnp.exp(shifted - jnp.max(shifted, axis=0, keepdims=True))
    probabilities = shifted / jnp.sum(shifted, axis=0, keepdims=True)
    mixed = []
    for c in range(2):
        first, second = logits[8 + 2 * c : 9 + 2 * c], logits[9 + 2 * c : 10 + 2 * c]
        peak = jnp.maximum(first, second)
        first, second = jnp.exp(first - peak), jnp.exp(second - peak)
        mixed += [first / (first + second), second / (first + second)]
    state_ref[0:8, :] = probabilities
    state_ref[8:16, :] = rows_of(mixed, 8)
    state_ref[16:24, :] = rank
    slots = out.shape[1] - 16
    for expert in range(out.shape[0]):
        taken = slots_of(named, rank, expert, slots // 2)
        out[expert, :slots, :] = dot(taken, normed, 1, 0).astype(BF)
        gates = rows_of(split3(pick_row(probabilities, expert)), 16).astype(BF)
        out[expert, slots:, :] = jnp.zeros((16, out.shape[2]), BF)
        out[expert, slots:, :slots] = dot(gates, taken, 1, 1).astype(BF)


def expert_kernel(idx, t_own, t_other, g_own, g_other, weights, *refs):
    (t_ref, g_ref, inner_ref, gate_ref, up_ref, down_full, keep, send) = refs[:8]
    t_all, g_all, scale_all, gate_full, up_full = refs[8:]
    core = idx[2]
    j = pl.program_id(0)
    slots = g_own.shape[1]
    chunk = weights.shape[3]

    @pl.when(j == 0)
    def _():
        for k in range(RING):
            columns = slice(k * chunk, (k + 1) * chunk)
            gate_full[:, columns] = weights[k, 0]
            up_full[:, columns] = weights[k, 1]
            down_full[:, columns] = weights[k, 2]
        for p in range(8):
            tokens, grads = (t_own, g_own) if p < RING else (t_other, g_other)
            rows = slice(p * slots, (p + 1) * slots)
            t_all[rows, :] = tokens[p % RING, :slots, :]
            g_all[rows, :] = grads[p % RING]
            parts = tokens[p % RING, slots:, :slots]
            scale_all[rows, :] = dot(parts, jnp.ones((16, 128), BF), 0, 0)

    tile = 2 * slots
    rows = pl.ds(pl.multiple_of(j * tile, 16), tile)
    entry, grad = t_all[rows, :], g_all[rows, :]
    scale = scale_all[rows, :]
    model = entry.shape[1]
    t_ref[...] = entry
    g_ref[...] = (grad.astype(F32) * wide(scale, model // 128)).astype(BF)
    gate_act = dot(entry, gate_full[...], 1, 0)
    up_act = dot(entry, up_full[...], 1, 0)
    sigma = jax.nn.sigmoid(gate_act)
    silu_act = gate_act * sigma
    inner = (silu_act * up_act).astype(BF)
    inner_ref[...] = inner
    raw = dot(grad, down_full[...], 1, 0)
    product = split2(inner.astype(F32) * raw)
    grad_inner = raw * wide(scale, raw.shape[1] // 128)
    grad_gate = (grad_inner * up_act * sigma * (1.0 + gate_act * (1.0 - sigma))).astype(BF)
    grad_up = (grad_inner * silu_act).astype(BF)
    gate_ref[...] = grad_gate
    up_ref[...] = grad_up
    entry_grad = dot(grad_gate, gate_full[...], 1, 1) + dot(grad_up, up_full[...], 1, 1)
    ones = jnp.ones((16, raw.shape[1]), BF)
    for part in range(2):
        piece_rows = slice(part * slots, (part + 1) * slots)
        sums = dot(ones, product[0][piece_rows], 1, 1) + dot(ones, product[1][piece_rows], 1, 1)
        index = iota(sums.shape, 0)
        high, middle, rest = split3(sums)
        packed = jnp.where(
            index == 4 * core,
            high,
            jnp.where(index == 4 * core + 1, middle, jnp.where(index == 4 * core + 2, rest, 0.0)),
        ).astype(BF)
        rows_out = entry_grad[piece_rows].astype(BF)
        place = lax.rem(2 * j + part, RING)

        def put(out, place=place, rows_out=rows_out, packed=packed):
            out[place, :slots, :] = rows_out
            out[place, slots:, :] = jnp.zeros((16, model), BF)
            out[place, slots:, :slots] = packed

        @pl.when(j < 2)
        def _(put=put):
            put(keep)

        @pl.when(j >= 2)
        def _(put=put):
            put(send)


def expert_out_kernel(idx, inner_ref, down_ref, keep, send):
    j = pl.program_id(0)
    slots = keep.shape[1]
    out = dot(inner_ref[...], down_ref[...], 1, 1).astype(BF)
    for part in range(2):
        place = lax.rem(2 * j + part, RING)
        piece = out[part * slots : (part + 1) * slots]

        @pl.when(j < 2)
        def _(place=place, piece=piece):
            keep[place] = piece

        @pl.when(j >= 2)
        def _(place=place, piece=piece):
            send[place] = piece


def expert_grads_kernel(idx, t_ref, g_ref, inner_ref, gate_ref, up_ref, out):
    for place, (left, right) in enumerate(((t_ref, gate_ref), (t_ref, up_ref), (g_ref, inner_ref))):
        out[0, place] = dot(left[...], right[...], 0, 0).astype(BF)


def slot_table(small, state, capacity):
    named = routed_rows(small, 8)
    rank = state[16:24, :]
    return [slots_of(named, rank, expert, capacity) for expert in range(RING)], named


def branch_weights(state, named):
    gates = state[0:8, :] * named
    consts = [gates[6 + c : 7 + c] for c in range(2)]
    normed_weight = gates[5:6]
    for c in range(2):
        normed_weight = normed_weight + consts[c] * state[8 + 2 * c : 9 + 2 * c, :]
    vector_weights = [consts[c] * state[9 + 2 * c : 10 + 2 * c, :] for c in range(2)]
    return consts, normed_weight, vector_weights


def output_kernel(idx, hidden_ref, state_ref, xa, xb, params, returned, logits_ref, oa, ob):
    state = state_ref[...]
    tables, named = slot_table(small_of(xa, xb), state, returned.shape[1] // 2)
    hidden = hidden_ref[...]
    normed = hidden * norm_scale(hidden) * params[15:16, :]
    _, normed_weight, vector_weights = branch_weights(state, named)
    output = hidden + wide(column_of(normed_weight), normed.shape[1] // 128) * normed
    vector_rows = rows_of(split3(params[12:13, :])[:2] * 2 + split3(params[13:14, :])[:2] * 2, 16)
    first, second = split3(vector_weights[0])[:2], split3(vector_weights[1])[:2]
    weight_rows = rows_of(
        (first[0], first[0], first[1], first[1], second[0], second[0], second[1], second[1]), 16
    )
    output += dot(weight_rows.astype(BF), vector_rows.astype(BF), 0, 0)
    for k in range(RING):
        gate = state[k : k + 1, :]
        high, low, _ = split3(gate)
        table = tables[k].astype(F32)
        output += dot((table * high).astype(BF), returned[k], 0, 0)
        output += dot((table * low).astype(BF), returned[k], 0, 0)
    for slot, out in enumerate((oa, ob)):
        out[:BLOCK, :] = output[slot * BLOCK : (slot + 1) * BLOCK].astype(BF)
        parts = split3(logits_ref[:, slot * BLOCK : (slot + 1) * BLOCK])
        parts = jnp.concatenate(parts, axis=1)
        out[BLOCK:, :] = jnp.concatenate([parts, jnp.zeros_like(parts)], axis=0).astype(BF)


def hidden_back_kernel(
    idx, hidden_ref, state_ref, xa, xb, ca, cb, params, ow_ref, returned, *outs
):
    gh_ref, low_ref, own_ref, send_ref, logits_ref, small_ref = outs
    core = idx[2]
    state = state_ref[...]
    slots = returned.shape[1] - 16
    tables, named = slot_table(small_of(xa, xb), state, slots // 2)
    probabilities = state[0:8, :]
    hidden = hidden_ref[...]
    factor = norm_scale(hidden)
    scaled_hidden = hidden * factor
    normed = scaled_hidden * params[15:16, :]
    normed_low = normed.astype(BF)
    grads_low = pair_of(ca, cb)
    grads = grads_low.astype(F32)
    ones = jnp.ones((16, hidden.shape[1]), BF)
    high, low = split2(grads * normed)
    on_normed = (dot(ones, high, 1, 1) + dot(ones, low, 1, 1))[0:1]
    first, second = split3(params[12:13, :])[:2], split3(params[13:14, :])[:2]
    on_vectors = dot(rows_of(first + second, 16).astype(BF), grads_low, 1, 1)
    on_vector = (on_vectors[0:1] + on_vectors[1:2], on_vectors[2:3] + on_vectors[3:4])
    consts, normed_weight, vector_weights = branch_weights(state, named)
    index = iota(probabilities.shape, 0)
    grad_probs = jnp.where(index == 5, on_normed, 0.0)
    mix_rows = []
    for c in range(2):
        mix_first, mix_second = state[8 + 2 * c : 9 + 2 * c, :], state[9 + 2 * c : 10 + 2 * c, :]
        dot_c = mix_first * on_normed + mix_second * on_vector[c]
        grad_probs = jnp.where(index == 6 + c, dot_c, grad_probs)
        grad_first, grad_second = consts[c] * on_normed, consts[c] * on_vector[c]
        mean = mix_first * grad_first + mix_second * grad_second
        mix_rows += [mix_first * (grad_first - mean), mix_second * (grad_second - mean)]
    back = jnp.zeros(hidden.shape, F32)
    for k in range(RING):
        packed = returned[k, slots:, :slots]
        found = jnp.sum(dot(packed, tables[k], 1, 0), axis=0, keepdims=True)
        grad_probs = jnp.where(index == k, found, grad_probs)
        back += dot(tables[k], returned[k, :slots, :], 0, 0)
    grad_probs = grad_probs * named
    grad_logits = probabilities * (
        grad_probs - jnp.sum(probabilities * grad_probs, axis=0, keepdims=True)
    )
    logits_ref[...] = grad_logits
    router_rows = jnp.concatenate([grad_logits, rows_of(mix_rows, 8)], axis=0)
    rows_high, rows_low = split2(router_rows)
    weights_low = params[...].astype(BF)
    grad_normed = (
        back
        + dot(rows_high, weights_low, 0, 0)
        + dot(rows_low, weights_low, 0, 0)
        + wide(column_of(normed_weight), hidden.shape[1] // 128) * grads
    )
    router_grad = dot(rows_high, normed_low, 1, 0) + dot(rows_low, normed_low, 1, 0)
    first, second = split3(vector_weights[0])[:2], split3(vector_weights[1])[:2]
    vector_grad = dot(rows_of(first + second, 16).astype(BF), grads_low, 1, 0)
    gain_grad = jnp.sum(grad_normed * scaled_hidden, axis=0, keepdims=True)
    small_ref[...] = jnp.where(
        iota(router_grad.shape, 0) < 12,
        router_grad,
        rows_of(
            [jnp.zeros_like(gain_grad)] * 12
            + [vector_grad[0:1] + vector_grad[1:2], vector_grad[2:3] + vector_grad[3:4], gain_grad],
            16,
        ),
    )
    scaled = grad_normed * params[15:16, :]
    mean = jnp.mean(scaled * hidden, axis=-1, keepdims=True)
    grad_hidden = grads + factor * scaled - hidden * (factor * factor * factor * mean)
    gh_ref[...] = grad_hidden
    grad_low = grad_hidden.astype(BF)
    low_ref[...] = grad_low
    width = own_ref.shape[1]
    own_rows = pl.ds(pl.multiple_of(core * width, 16), width)
    other_rows = pl.ds(pl.multiple_of((1 - core) * width, 16), width)
    own_ref[...] = dot(grad_low, ow_ref[own_rows, :], 1, 1).astype(BF)
    send_ref[...] = dot(grad_low, ow_ref[other_rows, :], 1, 1).astype(BF)


def out_grad_kernel(idx, keep, recv, low_ref, own_ref, send_ref):
    core = idx[2]
    width = keep.shape[1]
    own = pl.ds(pl.multiple_of(core * width, 128), width)
    other = pl.ds(pl.multiple_of((1 - core) * width, 128), width)
    for out, columns in ((own_ref, own), (send_ref, other)):
        grads = low_ref[:, columns]
        out[own, :] = dot(keep[...], grads, 0, 0).astype(BF)
        out[other, :] = dot(recv[...], grads, 0, 0).astype(BF)


def normed_back_kernel(idx, *refs):
    pair_grads, w_ref, keep_ref, send_ref = refs[:-3], refs[-3], refs[-2], refs[-1]
    core, flip = idx[2], idx[3]
    lanes = 2 * HEAD_DIM
    for i in range(pair_grads[0].shape[0] // BLOCK):
        tile = slice(i * BLOCK, (i + 1) * BLOCK)
        total = 0.0
        for j in range(3):
            columns = slice(j * lanes, (j + 1) * lanes)
            grads = jnp.concatenate([ref[tile, columns] for ref in pair_grads], axis=1)
            total = total + dot(grads, w_ref[j], 1, 1)
        half, slot = i // 2, (i % 2) ^ flip
        rows = pl.ds(pl.multiple_of(slot * BLOCK, BLOCK), BLOCK)

        @pl.when(half == core)
        def _(total=total, rows=rows):
            keep_ref[rows, :] = total.astype(BF)

        @pl.when(half != core)
        def _(total=total, rows=rows):
            send_ref[rows, :] = total.astype(BF)


def input_back_kernel(idx, keep_ref, recv_ref, gh_ref, xa, xb, params, oa, ob):
    gain = params[14:15, :]
    for slot, (x_ref, out) in enumerate(((xa, oa), (xb, ob))):
        tile = slice(slot * BLOCK, (slot + 1) * BLOCK)
        x = x_ref[:BLOCK, :].astype(F32)
        factor = norm_scale(x)
        scaled = (keep_ref[tile, :].astype(F32) + recv_ref[tile, :].astype(F32)) * gain
        mean = jnp.mean(scaled * x, axis=-1, keepdims=True)
        out[...] = (
            gh_ref[tile, :] + factor * scaled - x * (factor * factor * factor * mean)
        ).astype(BF)


def across(values):
    return lax.ppermute(values, "dp", [(0, 1), (1, 0)])


def exchange(values, axis):
    return lax.all_to_all(values, axis, 0, 0, tiled=True)


def after(values, *others):
    return lax.optimization_barrier((values, others))[0]


def handed_to_all(values, axis):
    return exchange(jnp.broadcast_to(values[None], (RING, *values.shape)), axis)


def chip_local(
    inputs, cotangent, qkv_weight, out_weight, norm_gains, route_weight, const_gate, const_vec,
    w_gate, w_up, w_down, prev_logits, routes, segments,
):
    e, z, core = lax.axis_index("experts"), lax.axis_index("context"), lax.axis_index("dp")
    flip = z // 2
    idx = jnp.stack([e, z, core, flip]).astype(jnp.int32)
    odd = lax.rem(z, 2)
    rows, model = inputs.shape[2], inputs.shape[3]
    length = rows * RING
    half_model = model // 2
    slots = 2 * (rows * 5 // 16)

    def place(z_index, d, which):
        micro = z_index % 2 if which == 0 else 1 - z_index % 2
        return (2 * micro + d) * 2 + z_index // 2

    routes_of = [
        [(zi * 2 + d, place(zi, d, which)) for zi in range(RING) for d in range(2)]
        for which in range(2)
    ]

    def leave(values):
        return [
            lax.ppermute(
                lax.dynamic_index_in_dim(values, odd if which == 0 else 1 - odd, 0, False),
                ("context", "dp"),
                routes_of[which],
            )
            for which in range(2)
        ]

    def go_home(values, which):
        return lax.ppermute(values, ("context", "dp"), [(b, a) for a, b in routes_of[which]])

    def at_home(*got):
        return jnp.where(odd == 0, jnp.stack(got), jnp.stack(got[::-1]))

    def columns_of(values, side):
        return lax.dynamic_slice_in_dim(values, side * half_model, half_model, values.ndim - 1)

    def in_order(mine, theirs, axis):
        pair = jnp.stack([mine, theirs], axis=axis), jnp.stack([theirs, mine], axis=axis)
        return jnp.where(core == 0, *pair)

    vectors = split3(jnp.concatenate([const_vec, norm_gains], axis=0).T)
    columns = jnp.concatenate(
        [route_weight, const_gate, *(part.astype(BF) for part in vectors)], axis=1
    )
    columns = jnp.pad(columns, ((0, 0), (0, 128 - columns.shape[1])))
    matrix = lax.dynamic_index_in_dim(
        jnp.concatenate([qkv_weight, out_weight[None]], axis=0), e, 0, False
    )
    ring = handed_to_all(jnp.concatenate([matrix, columns], axis=1), "context")
    logit_parts = jnp.concatenate(split3(jnp.swapaxes(prev_logits[:, 0], 1, 2)), axis=2)
    ids = jnp.concatenate([jnp.swapaxes(routes[:, 0], 1, 2), segments], axis=1).astype(F32)
    ids = jnp.pad(ids, ((0, 0), (0, 5), (0, 2 * rows)))
    xa, xb = leave(
        jnp.concatenate([inputs[:, 0], logit_parts.astype(BF), ids.astype(BF)], axis=1)
    )
    ring, xa, xb = lax.optimization_barrier((ring, xa, xb))

    def my_part(side):
        return jnp.concatenate([columns_of(ring[:, :, :model], side), ring[:, :, model:]], axis=2)

    shared = in_order(my_part(core), across(my_part(1 - core)), 1)
    shared = shared.reshape(model, half_model + 128)
    columns = shared[:, half_model:]
    w_all = handed_to_all(shared[:, :half_model], "experts")
    theirs = across(jnp.stack([xa, xb]))

    stacked = jnp.stack([w_gate[0], w_up[0], w_down[0]])
    expert_w = lax.all_gather(after(stacked, ring), "context", axis=0)
    ca, cb = leave(after(cotangent[:, 0], shared))

    cosine, sine = (jnp.asarray(t) for t in rope_tables(length))
    q, k, v, normed_in, params, seg_row, seg_col = kernel_call(
        project_kernel,
        idx,
        [xa, xb, theirs, columns, w_all, cosine, sine],
        [((length, half_model), BF)] * 3
        + [((length, model), BF)]
        + [((16, model), F32), ((8, length), F32), ((length, 128), F32)],
        flops=2 * length * model * 3 * half_model,
        share=100,
        scratch=[pltpu.VMEM((length, model), BF)],
    )
    pairs = half_model // (2 * HEAD_DIM)
    lanes = 2 * HEAD_DIM
    by_pair = pl.BlockSpec((length, lanes), lambda h: (0, h))
    half_by_pair = pl.BlockSpec((length // 2, lanes), lambda h: (0, h))
    all_of = pl.BlockSpec(memory_space=pltpu.VMEM)
    lse_spec = pl.BlockSpec((1, 8, length), lambda h: (h, 0, 0))
    keep, send, lse = kernel_call(
        attend_kernel,
        idx,
        [q, k, v, seg_row, seg_col],
        [((length // 2, half_model), BF)] * 2 + [((pairs, 8, length), F32)],
        flops=4 * length * length * half_model,
        share=100,
        grid=(pairs,),
        in_specs=[by_pair] * 3 + [all_of] * 2,
        out_specs=[half_by_pair] * 2 + [lse_spec],
    )
    ca, cb = after((ca, cb), keep)
    (g_slots,) = kernel_call(
        grad_slots_kernel,
        idx,
        [xa, xb, ca, cb],
        [((RING, slots, model), BF)],
        flops=2 * RING * slots * 2 * rows * model,
    )
    g_mine = exchange(g_slots, "experts")
    recv = after(across(send), g_slots)

    hidden, ow_all, state, sent = kernel_call(
        route_kernel,
        idx,
        [keep, recv, xa, xb, params, w_all[3], across(w_all[3])],
        [((2 * rows, model), F32), ((model, model), BF), ((24, 2 * rows), F32)]
        + [((RING, slots + 16, model), BF)],
        flops=2 * 2 * rows * model * model + 2 * RING * slots * 2 * rows * model,
    )
    t_mine = exchange(after(sent, g_mine), "experts")
    g_theirs = across(g_mine)
    t_theirs = across(t_mine)

    count = 8 * slots
    chunk = w_gate.shape[2]
    hidden_units = RING * chunk
    tile_of = lambda n: pl.BlockSpec((2 * slots, n), lambda j: (j, 0))
    t_all, g_all, inner, gate_g, up_g, down_all, entry_keep, entry_send = kernel_call(
        expert_kernel,
        idx,
        [t_mine, t_theirs, g_mine, g_theirs, expert_w],
        [((count, model), BF)] * 2
        + [((count, hidden_units), BF)] * 3
        + [((model, hidden_units), BF)]
        + [((RING, slots + 16, model), BF)] * 2,
        flops=10 * count * model * hidden_units,
        grid=(4,),
        in_specs=[all_of] * 5,
        out_specs=[tile_of(model)] * 2 + [tile_of(hidden_units)] * 3 + [all_of] * 3,
        scratch=[
            pltpu.VMEM((count, model), BF),
            pltpu.VMEM((count, model), BF),
            pltpu.VMEM((count, 128), F32),
            pltpu.VMEM((model, hidden_units), BF),
            pltpu.VMEM((model, hidden_units), BF),
        ],
    )

    def both_cores(kept, received):
        return (kept.astype(F32) + received.astype(F32)).astype(BF)

    chunk_of = pl.BlockSpec((count, chunk), lambda j: (0, j))
    (far_grads,) = kernel_call(
        expert_grads_kernel,
        idx,
        [t_all, g_all, inner, gate_g, up_g],
        [((RING, 3, model, chunk), BF)],
        flops=6 * count * model * hidden_units,
        grid=(RING,),
        in_specs=[all_of] * 2 + [chunk_of] * 3,
        out_specs=[pl.BlockSpec((1, 3, model, chunk), lambda j: (j, 0, 0, 0))],
    )
    entry_sum = both_cores(entry_keep, after(across(entry_send), far_grads))
    entry_back = exchange(entry_sum, "experts")
    out_keep, out_send = kernel_call(
        expert_out_kernel,
        idx,
        [after(inner, entry_sum), down_all],
        [((RING, slots, model), BF)] * 2,
        flops=2 * count * model * hidden_units,
        grid=(4,),
        in_specs=[tile_of(hidden_units), all_of],
        out_specs=[all_of] * 2,
    )
    entry_back, out_send = lax.optimization_barrier((entry_back, out_send))
    expert_grads = lax.psum_scatter(far_grads, "context", scatter_dimension=0).astype(F32)

    grad_hidden, grad_low, ga_own, ga_send, logit_rows, small_grad = kernel_call(
        hidden_back_kernel,
        idx,
        [hidden, state, xa, xb, ca, cb, params, ow_all, entry_back],
        [((2 * rows, model), F32), ((2 * rows, model), BF)]
        + [((2 * rows, half_model), BF)] * 2
        + [((8, 2 * rows), F32), ((16, model), F32)],
        flops=2 * 2 * rows * model * model + 2 * RING * slots * 2 * rows * model,
    )
    ga_other = across(ga_send)
    out_sum = both_cores(out_keep, across(out_send))
    out_back = exchange(after(out_sum, entry_back), "experts")
    og_own, og_send = kernel_call(
        out_grad_kernel,
        idx,
        [keep, recv, grad_low],
        [((model, half_model), BF)] * 2,
        flops=2 * 2 * rows * model * model,
    )
    og_other = across(og_send)
    q = after(q, out_back)
    shared_parts, pair_grads = [], []
    for h in range(pairs):
        at = lambda n, h=h: pl.BlockSpec((n, lanes), lambda i: (0, h))
        extra = 16 if h == 0 else 0
        grads, part = kernel_call(
            functools.partial(pair_back_kernel, h == 0),
            idx,
            [q, k, v, ga_own, ga_other, seg_row, seg_col, lse, cosine, sine, normed_in]
            + [og_own, og_other]
            + ([small_grad] if h == 0 else []),
            [((length, 3 * lanes), BF), ((RING, RING, model // RING + extra, lanes), BF)],
            flops=10 * length * length * lanes + 6 * length * model * lanes,
            grid=(1,),
            in_specs=[at(length)] * 3
            + [at(length // 2)] * 2
            + [all_of] * 2
            + [pl.BlockSpec((1, 8, length), lambda i, h=h: (h, 0, 0))]
            + [all_of] * 3
            + [at(model)] * 2
            + ([all_of] if h == 0 else []),
            out_specs=[all_of] * 2,
            scratch=[pltpu.VMEM((length, lanes), F32)] * 2,
        )
        pair_grads.append(grads)
        shared_parts.append(exchange(part, "experts"))
        if h == 0:
            oa, ob = kernel_call(
                output_kernel,
                idx,
                [after(hidden, part), state, xa, xb, params, out_back, logit_rows],
                [((rows + 16, model), BF)] * 2,
                flops=4 * RING * slots * 2 * rows * model,
            )
            home_a = go_home(oa, 0)
            home_b = go_home(after(ob, home_a), 1)
            home = at_home(home_a, home_b)
            output = home[:, None, :rows]
            logit_grad = home[:, rows : rows + 8].astype(F32).reshape(2, 8, 3, rows).sum(axis=2)
            logit_grad = jnp.swapaxes(logit_grad, 1, 2)[:, None]
            q = after(q, oa)
        if h == 1:
            q = after(q, shared_parts[0], home_a)
        if h == 2:
            w_all = after(w_all, shared_parts[1], home_b)
    depth = model // RING
    gn_keep, gn_send = kernel_call(
        normed_back_kernel,
        idx,
        [*pair_grads, w_all],
        [((2 * rows, model), BF)] * 2,
        flops=2 * length * model * 3 * half_model,
    )

    shared_parts[2] = after(shared_parts[2], gn_send)
    sums = [part.astype(F32).sum(axis=0).astype(BF) for part in shared_parts]
    parts = jnp.concatenate([part[:, :depth] for part in sums], axis=2)
    rest = jnp.pad(sums[0][:, depth:], ((0, 0), (0, 0), (0, half_model - lanes)))
    parts = jnp.concatenate([parts, rest], axis=1)
    ia, ib = kernel_call(
        input_back_kernel,
        idx,
        [gn_keep, across(gn_send), grad_hidden, xa, xb, params],
        [((rows, model), BF)] * 2,
        flops=0,
    )
    input_grad = at_home(go_home(ia, 0), go_home(ib, 1)).astype(F32)[:, None]
    parts = after(exchange(parts, "context"), ia).astype(F32).sum(axis=0)
    shard = depth // 2
    rest = parts[depth:]
    given = jnp.concatenate(
        [lax.dynamic_slice_in_dim(parts, (1 - core) * shard, shard, 0), rest], axis=0
    )
    taken = across(given.astype(BF)).astype(F32)
    grads = in_order(lax.dynamic_slice_in_dim(parts, core * shard, shard, 0), taken[:shard], 1)
    rest = jnp.pad(rest + taken[shard:], ((0, 0), (0, half_model)))
    grads = jnp.concatenate([grads.reshape(shard, model), rest], axis=0).astype(BF)
    grads = handed_to_all(grads, "experts").astype(F32)
    small_grad = lax.dynamic_index_in_dim(grads, core, 0, False)[shard:, :shard]
    qkv_grad = grads[:3, :shard]
    gain_first = (qkv_grad * qkv_weight.astype(F32)).sum(axis=(0, 2)) / norm_gains[0]
    return (
        output,
        input_grad,
        logit_grad,
        qkv_grad,
        grads[3, :shard],
        jnp.stack([gain_first, small_grad[14]]),
        small_grad[:8].T,
        small_grad[8:12].T,
        small_grad[12:14],
        expert_grads[0][None],
        expert_grads[1][None],
        expert_grads[2][None],
    )


def whole_sequence_fits(mesh):
    return (mesh.shape["experts"], mesh.shape["context"], mesh.shape["dp"]) == (4, 4, 2)


def solution(mesh):
    local = chip_local if whole_sequence_fits(mesh) else general_local
    in_specs = (
        P(None, ("experts", "dp"), "context", None),
        P(None, ("experts", "dp"), "context", None),
        P(None, ("context", "dp"), None),
        P(("context", "dp"), None),
        P(None, ("context", "dp")),
        P(("context", "dp"), None),
        P(("context", "dp"), None),
        P(None, ("context", "dp")),
        P("experts", None, ("context", "dp")),
        P("experts", None, ("context", "dp")),
        P("experts", None, ("context", "dp")),
        P(None, ("experts", "dp"), "context", None),
        P(None, ("experts", "dp"), "context", None),
        P(None, ("experts", "dp"), "context"),
    )
    out_specs = (
        P(None, ("experts", "dp"), "context", None),
        P(None, ("experts", "dp"), "context", None),
        P(None, ("experts", "dp"), "context", None),
        P(None, ("context", "dp"), None),
        P(("context", "dp"), None),
        P(None, ("context", "dp")),
        P(("context", "dp"), None),
        P(("context", "dp"), None),
        P(None, ("context", "dp")),
        P("experts", None, ("context", "dp")),
        P("experts", None, ("context", "dp")),
        P("experts", None, ("context", "dp")),
    )
    return jax.shard_map(local, mesh=mesh, in_specs=in_specs, out_specs=out_specs, check_vma=False)
```

```python
import functools
import functools
import math

import jax
import jax.numpy as jnp
import numpy as np
from jax import lax
from jax.experimental import pallas as pl
from jax.experimental.pallas import tpu as pltpu
from jax.sharding import PartitionSpec as P

HEAD_DIM = 64
FF = 2048


EPSILON = 1e-05
MASKED = -1e30


def rotate(values, positions, direction):
    half_dim = values.shape[-1] // 2
    inverse = 10000.0 ** (-jnp.arange(half_dim, dtype=jnp.float32) / half_dim)
    angles = positions.astype(jnp.float32)[:, None] * inverse[None, :]
    cosine = jnp.cos(angles)[:, None, :]
    sine_part = jnp.sin(angles)[:, None, :]
    first_half = values[..., :half_dim]
    second = values[..., half_dim:]
    return jnp.concatenate(
        [
            first_half * cosine - direction * second * sine_part,
            second * cosine + direction * first_half * sine_part,
        ],
        axis=-1,
    )


def softmax_last(logits):
    shifted = jnp.exp(logits - jnp.max(logits, axis=-1, keepdims=True))
    return shifted / jnp.sum(shifted, axis=-1, keepdims=True)


def norm_scale(values):
    return lax.rsqrt(jnp.mean(values * values, axis=-1, keepdims=True) + EPSILON)


def norm_back(grad_in, values, factor, gain_vec):
    scaled = grad_in * gain_vec
    grad_gain = jnp.sum(grad_in * values * factor, axis=0)
    grad_values = factor * scaled - values * factor * factor * factor * jnp.mean(
        scaled * values, axis=-1, keepdims=True
    )
    return (grad_values, grad_gain)


def masked_scores(
    queries, key_rows, query_segments, key_segments, query_positions, key_positions, score_scale
):
    scores = (
        jnp.einsum("qhd,khd->hqk", queries, key_rows, preferred_element_type=jnp.float32)
        * score_scale
    )
    allowed = (query_segments[:, None] == key_segments[None, :]) & (
        key_positions[None, :] <= query_positions[:, None]
    )
    return (jnp.where(allowed[None], scores, MASKED), allowed)


def general_local(
    inputs,
    cotangent,
    qkv_weight,
    out_weight,
    norm_gains,
    route_weight,
    const_gate,
    const_vec,
    w_gate,
    w_up,
    w_down,
    prev_logits,
    routes,
    segments,
):
    micro_count = inputs.shape[0]
    row_count = inputs.shape[2]
    model_width = inputs.shape[3]
    head_count = model_width // HEAD_DIM
    score_scale = HEAD_DIM ** (-0.5)
    local_experts = w_gate.shape[0]
    experts = local_experts * lax.axis_size("experts")
    capacity = row_count * 5 // 16
    routed = prev_logits.shape[3]
    assigned = 2 * row_count
    head_shape = (row_count, head_count, HEAD_DIM)
    positions = lax.axis_index("context") * row_count + jnp.arange(row_count, dtype=jnp.int32)
    grad_qkv = jnp.zeros((3, model_width, model_width), jnp.float32)
    grad_out = jnp.zeros((model_width, model_width), jnp.float32)
    gain_first = jnp.zeros((model_width,), jnp.float32)
    gain_second = jnp.zeros((model_width,), jnp.float32)
    grad_vec = jnp.zeros((2, model_width), jnp.float32)
    grad_route = jnp.zeros((model_width, routed), jnp.float32)
    grad_mixer = jnp.zeros((model_width, 4), jnp.float32)
    grad_gate = jnp.zeros((local_experts, model_width, FF), jnp.float32)
    grad_up = jnp.zeros((local_experts, model_width, FF), jnp.float32)
    grad_down = jnp.zeros((local_experts, model_width, FF), jnp.float32)
    output_rows = []
    input_rows = []
    logit_rows = []
    for batch_index in range(micro_count):
        qkv_full, out_full, gains, vectors, route_full, mixer_full = (
            lax.all_gather(qkv_weight, ("context", "dp"), axis=1, tiled=True),
            lax.all_gather(out_weight, ("context", "dp"), axis=0, tiled=True),
            lax.all_gather(
                norm_gains.astype(jnp.bfloat16), ("context", "dp"), axis=1, tiled=True
            ).astype(norm_gains.dtype),
            lax.all_gather(
                const_vec.astype(jnp.bfloat16), ("context", "dp"), axis=1, tiled=True
            ).astype(const_vec.dtype),
            lax.all_gather(route_weight, ("context", "dp"), axis=0, tiled=True),
            lax.all_gather(const_gate, ("context", "dp"), axis=0, tiled=True),
        )
        gate_full, up_full, down_full = (
            lax.all_gather(w_gate, ("context", "dp"), axis=2, tiled=True),
            lax.all_gather(w_up, ("context", "dp"), axis=2, tiled=True),
            lax.all_gather(w_down, ("context", "dp"), axis=2, tiled=True),
        )
        token_rows = inputs[batch_index, 0].astype(jnp.float32)
        seg_rows = segments[batch_index, 0]
        route_rows = routes[batch_index, 0]
        grad_rows = cotangent[batch_index, 0].astype(jnp.float32)
        scale_first = norm_scale(token_rows)
        normed_in = (token_rows * scale_first * gains[0]).astype(jnp.bfloat16)
        projected = jnp.einsum(
            "qd,cde->cqe", normed_in, qkv_full, preferred_element_type=jnp.float32
        )
        queries = rotate(projected[0].reshape(head_shape), positions, 1.0).astype(jnp.bfloat16)
        rotated_keys = rotate(projected[1].reshape(head_shape), positions, 1.0).astype(jnp.bfloat16)
        values = projected[2].reshape(head_shape).astype(jnp.bfloat16)
        row_peak = jnp.full((head_count, row_count), MASKED, jnp.float32)
        key_block = lax.all_gather(rotated_keys, "context", axis=0, tiled=True)
        value_block = lax.all_gather(values, "context", axis=0, tiled=True)
        segment_block = lax.all_gather(seg_rows, "context", axis=0, tiled=True)
        key_positions = jnp.arange(key_block.shape[0], dtype=jnp.int32)
        scores, allowed = masked_scores(
            queries, key_block, seg_rows, segment_block, positions, key_positions, score_scale
        )
        new_peak = jnp.maximum(row_peak, jnp.max(scores, axis=-1))
        expo = jnp.where(allowed[None], jnp.exp(scores - new_peak[:, :, None]), 0.0)
        weighted = jnp.einsum(
            "hqk,khd->hqd",
            expo.astype(jnp.bfloat16),
            value_block,
            preferred_element_type=jnp.float32,
        )
        row_peak, row_total, weighted = (new_peak, jnp.sum(expo, axis=-1), weighted)
        log_total = row_peak + jnp.log(row_total)
        attn_heads = jnp.transpose(weighted / row_total[:, :, None], (1, 0, 2))
        attended = attn_heads.reshape(row_count, model_width).astype(jnp.bfloat16)
        hidden = token_rows + jnp.dot(attended, out_full, preferred_element_type=jnp.float32)
        scale_second = norm_scale(hidden)
        normed = hidden * scale_second * gains[1]
        normed_low = normed.astype(jnp.bfloat16)
        logits = (
            jnp.dot(normed_low, route_full, preferred_element_type=jnp.float32)
            + prev_logits[batch_index, 0]
        )
        probabilities = softmax_last(logits)
        gate_values = jnp.take_along_axis(probabilities, route_rows, axis=-1)
        route_ids = route_rows.reshape(-1)
        routed_ffn = route_ids < experts
        onehot = (route_ids[:, None] == jnp.arange(experts, dtype=jnp.int32)[None, :]).astype(
            jnp.int32
        )
        slot_index = jnp.sum((jnp.cumsum(onehot, axis=0) - onehot) * onehot, axis=-1)
        slot_table = (
            jnp.full((experts, capacity), assigned, jnp.int32)
            .at[jnp.where(routed_ffn, route_ids, experts), slot_index]
            .set(jnp.arange(assigned, dtype=jnp.int32), mode="drop")
        )
        token_of = jnp.where(slot_table < assigned, slot_table // 2, row_count)
        pad_rows = jnp.concatenate([normed_low, jnp.zeros((1, model_width), jnp.bfloat16)], axis=0)
        received = lax.all_to_all(
            pad_rows[token_of], "experts", split_axis=0, concat_axis=1, tiled=True
        )
        gate_act = jnp.einsum(
            "erd,edf->erf", received, gate_full, preferred_element_type=jnp.float32
        )
        up_act = jnp.einsum("erd,edf->erf", received, up_full, preferred_element_type=jnp.float32)
        sigma = jax.nn.sigmoid(gate_act)
        silu_act = gate_act * sigma
        inner_low = (silu_act * up_act).astype(jnp.bfloat16)
        expert_low = jnp.einsum(
            "erf,edf->erd", inner_low, down_full, preferred_element_type=jnp.float32
        ).astype(jnp.bfloat16)
        returned = lax.all_to_all(
            expert_low, "experts", split_axis=1, concat_axis=0, tiled=True
        ).reshape(experts * capacity, model_width)
        pick_index = jnp.where(routed_ffn, route_ids * capacity + slot_index, 0)
        expert_out = jnp.where(
            routed_ffn[:, None], returned[pick_index].astype(jnp.float32), 0.0
        ).reshape(row_count, 2, model_width)
        const_mix = softmax_last(
            jnp.dot(normed_low, mixer_full, preferred_element_type=jnp.float32).reshape(
                row_count, 2, 2
            )
        )
        const_out = (
            const_mix[:, :, 0:1] * normed[:, None, :] + const_mix[:, :, 1:2] * vectors[None, :, :]
        )
        copy_mask = (route_rows == experts + 1).astype(jnp.float32)
        const_pick = (
            route_rows[:, :, None] == experts + 2 + jnp.arange(2, dtype=jnp.int32)[None, None, :]
        ).astype(jnp.float32)
        branch = (
            expert_out
            + copy_mask[:, :, None] * normed[:, None, :]
            + jnp.einsum("qjc,qcd->qjd", const_pick, const_out, precision=lax.Precision.HIGHEST)
        )
        output_rows.append(
            (hidden + jnp.sum(gate_values[:, :, None] * branch, axis=1)).astype(jnp.bfloat16)
        )
        grad_branch = gate_values[:, :, None] * grad_rows[:, None, :]
        grad_gates = jnp.sum(grad_rows[:, None, :] * branch, axis=-1)
        grad_probs = jnp.sum(
            (route_rows[:, :, None] == jnp.arange(routed, dtype=jnp.int32)[None, None, :]).astype(
                jnp.float32
            )
            * grad_gates[:, :, None],
            axis=1,
        )
        grad_logits = probabilities * (
            grad_probs - jnp.sum(probabilities * grad_probs, axis=-1, keepdims=True)
        )
        logit_rows.append(grad_logits)
        normed_wide = normed_low.astype(jnp.float32)
        grad_route = grad_route + jnp.dot(
            normed_wide.T, grad_logits, precision=lax.Precision.HIGHEST
        )
        grad_normed = jnp.dot(
            grad_logits, route_full.astype(jnp.float32).T, precision=lax.Precision.HIGHEST
        )
        grad_normed = grad_normed + jnp.sum(copy_mask[:, :, None] * grad_branch, axis=1)
        grad_const = jnp.einsum(
            "qjc,qjd->qcd", const_pick, grad_branch, precision=lax.Precision.HIGHEST
        )
        grad_mix = jnp.stack(
            [
                jnp.sum(grad_const * normed[:, None, :], axis=-1),
                jnp.sum(grad_const * vectors[None, :, :], axis=-1),
            ],
            axis=-1,
        )
        grad_mix_logits = (
            const_mix * (grad_mix - jnp.sum(const_mix * grad_mix, axis=-1, keepdims=True))
        ).reshape(row_count, 4)
        grad_mixer = grad_mixer + jnp.dot(
            normed_wide.T, grad_mix_logits, precision=lax.Precision.HIGHEST
        )
        grad_normed = grad_normed + jnp.dot(
            grad_mix_logits, mixer_full.astype(jnp.float32).T, precision=lax.Precision.HIGHEST
        )
        grad_normed = grad_normed + jnp.sum(const_mix[:, :, 0:1] * grad_const, axis=1)
        grad_vec = grad_vec + jnp.sum(const_mix[:, :, 1:2] * grad_const, axis=0)
        grad_slots = jnp.where(
            routed_ffn[:, None], grad_branch.reshape(assigned, model_width), 0.0
        ).astype(jnp.bfloat16)
        grad_pad = jnp.concatenate([grad_slots, jnp.zeros((1, model_width), jnp.bfloat16)], axis=0)
        grad_received = lax.all_to_all(
            grad_pad[slot_table], "experts", split_axis=0, concat_axis=1, tiled=True
        )
        grad_inner = jnp.einsum(
            "erd,edf->erf", grad_received, down_full, preferred_element_type=jnp.float32
        )
        grad_down = grad_down + jnp.einsum(
            "erd,erf->edf", grad_received, inner_low, preferred_element_type=jnp.float32
        )
        grad_gate_low = (grad_inner * up_act * sigma * (1.0 + gate_act * (1.0 - sigma))).astype(
            jnp.bfloat16
        )
        grad_up_low = (grad_inner * silu_act).astype(jnp.bfloat16)
        grad_gate = grad_gate + jnp.einsum(
            "erd,erf->edf", received, grad_gate_low, preferred_element_type=jnp.float32
        )
        grad_up = grad_up + jnp.einsum(
            "erd,erf->edf", received, grad_up_low, preferred_element_type=jnp.float32
        )
        grad_entry = (
            jnp.einsum("erf,edf->erd", grad_gate_low, gate_full, preferred_element_type=jnp.float32)
            + jnp.einsum("erf,edf->erd", grad_up_low, up_full, preferred_element_type=jnp.float32)
        ).astype(jnp.bfloat16)
        grad_back = lax.all_to_all(
            grad_entry, "experts", split_axis=1, concat_axis=0, tiled=True
        ).reshape(experts * capacity, model_width)
        grad_normed = grad_normed + jnp.sum(
            jnp.where(routed_ffn[:, None], grad_back[pick_index].astype(jnp.float32), 0.0).reshape(
                row_count, 2, model_width
            ),
            axis=1,
        )
        grad_hidden_norm, gain_term = norm_back(grad_normed, hidden, scale_second, gains[1])
        gain_second = gain_second + gain_term
        grad_hidden = grad_rows + grad_hidden_norm
        grad_attn_low = grad_hidden.astype(jnp.bfloat16)
        grad_out = grad_out + jnp.dot(attended.T, grad_attn_low, preferred_element_type=jnp.float32)
        grad_attended = (
            jnp.dot(grad_attn_low, out_full.T, preferred_element_type=jnp.float32)
            .astype(jnp.bfloat16)
            .reshape(head_shape)
        )
        delta = jnp.sum(grad_attended.astype(jnp.float32) * attn_heads, axis=-1).T
        zero_heads = jnp.zeros(head_shape, jnp.float32)
        key_all, value_all, segment_all = (
            lax.all_gather(rotated_keys, "context", axis=0, tiled=True),
            lax.all_gather(values, "context", axis=0, tiled=True),
            lax.all_gather(seg_rows, "context", axis=0, tiled=True),
        )
        total_keys = key_all.shape[0]
        group_count = math.gcd(total_keys // row_count, max(1, 512 // row_count))
        block_rows = row_count * group_count
        block_count = total_keys // block_rows

        def back_block(grad_query, block_parts):
            key_block, value_block, segment_block, block_start = block_parts
            key_positions = block_start + jnp.arange(block_rows, dtype=jnp.int32)
            scores, allowed = masked_scores(
                queries, key_block, seg_rows, segment_block, positions, key_positions, score_scale
            )
            probability = jnp.where(allowed[None], jnp.exp(scores - log_total[:, :, None]), 0.0)
            grad_prob = jnp.einsum(
                "qhd,khd->hqk", grad_attended, value_block, preferred_element_type=jnp.float32
            )
            grad_score = (probability * (grad_prob - delta[:, :, None])).astype(jnp.bfloat16)
            grad_query = (
                grad_query
                + jnp.einsum(
                    "hqk,khd->qhd", grad_score, key_block, preferred_element_type=jnp.float32
                )
                * score_scale
            )
            grad_key = (
                jnp.einsum("hqk,qhd->khd", grad_score, queries, preferred_element_type=jnp.float32)
                * score_scale
            )
            grad_value = jnp.einsum(
                "hqk,qhd->khd",
                probability.astype(jnp.bfloat16),
                grad_attended,
                preferred_element_type=jnp.float32,
            )
            return (grad_query, (grad_key, grad_value))

        block_starts = jnp.arange(block_count, dtype=jnp.int32) * block_rows
        grad_query, (key_terms, value_terms) = lax.scan(
            back_block,
            zero_heads,
            (
                key_all.reshape(block_count, block_rows, head_count, HEAD_DIM),
                value_all.reshape(block_count, block_rows, head_count, HEAD_DIM),
                segment_all.reshape(block_count, block_rows),
                block_starts,
            ),
        )
        grad_key, grad_value = (
            lax.psum_scatter(
                key_terms.reshape(total_keys, head_count, HEAD_DIM).astype(jnp.bfloat16),
                "context",
                scatter_dimension=0,
                tiled=True,
            ).astype(jnp.float32),
            lax.psum_scatter(
                value_terms.reshape(total_keys, head_count, HEAD_DIM).astype(jnp.bfloat16),
                "context",
                scatter_dimension=0,
                tiled=True,
            ).astype(jnp.float32),
        )
        grad_projected = jnp.stack(
            [
                rotate(grad_query, positions, -1.0).reshape(row_count, model_width),
                rotate(grad_key, positions, -1.0).reshape(row_count, model_width),
                grad_value.reshape(row_count, model_width),
            ]
        ).astype(jnp.bfloat16)
        grad_qkv = grad_qkv + jnp.einsum(
            "qd,cqe->cde", normed_in, grad_projected, preferred_element_type=jnp.float32
        )
        grad_normed_in = jnp.einsum(
            "cqe,cde->qd", grad_projected, qkv_full, preferred_element_type=jnp.float32
        )
        grad_token_norm, gain_term = norm_back(grad_normed_in, token_rows, scale_first, gains[0])
        gain_first = gain_first + gain_term
        input_rows.append(grad_hidden + grad_token_norm)
    grad_gain = jnp.stack([gain_first, gain_second])
    (
        grad_qkv,
        grad_out,
        grad_gain,
        grad_vec,
        grad_route,
        grad_mixer,
        grad_gate,
        grad_up,
        grad_down,
    ) = (
        lax.psum_scatter(
            grad_qkv.astype(jnp.bfloat16), ("context", "dp"), scatter_dimension=1, tiled=True
        ).astype(jnp.float32),
        lax.psum_scatter(
            grad_out.astype(jnp.bfloat16), ("context", "dp"), scatter_dimension=0, tiled=True
        ).astype(jnp.float32),
        lax.psum_scatter(
            grad_gain.astype(jnp.bfloat16), ("context", "dp"), scatter_dimension=1, tiled=True
        ).astype(jnp.float32),
        lax.psum_scatter(
            grad_vec.astype(jnp.bfloat16), ("context", "dp"), scatter_dimension=1, tiled=True
        ).astype(jnp.float32),
        lax.psum_scatter(
            grad_route.astype(jnp.bfloat16), ("context", "dp"), scatter_dimension=0, tiled=True
        ).astype(jnp.float32),
        lax.psum_scatter(
            grad_mixer.astype(jnp.bfloat16), ("context", "dp"), scatter_dimension=0, tiled=True
        ).astype(jnp.float32),
        lax.psum_scatter(
            grad_gate.astype(jnp.bfloat16), ("context", "dp"), scatter_dimension=2, tiled=True
        ).astype(jnp.float32),
        lax.psum_scatter(
            grad_up.astype(jnp.bfloat16), ("context", "dp"), scatter_dimension=2, tiled=True
        ).astype(jnp.float32),
        lax.psum_scatter(
            grad_down.astype(jnp.bfloat16), ("context", "dp"), scatter_dimension=2, tiled=True
        ).astype(jnp.float32),
    )
    grad_qkv, grad_out, grad_gain, grad_vec, grad_route, grad_mixer = (
        lax.psum(grad_qkv.astype(jnp.bfloat16), "experts").astype(jnp.float32),
        lax.psum(grad_out.astype(jnp.bfloat16), "experts").astype(jnp.float32),
        lax.psum(grad_gain.astype(jnp.bfloat16), "experts").astype(jnp.float32),
        lax.psum(grad_vec.astype(jnp.bfloat16), "experts").astype(jnp.float32),
        lax.psum(grad_route.astype(jnp.bfloat16), "experts").astype(jnp.float32),
        lax.psum(grad_mixer.astype(jnp.bfloat16), "experts").astype(jnp.float32),
    )
    output = jnp.stack(output_rows)[:, None]
    input_grad = jnp.stack(input_rows)[:, None]
    logit_grad = jnp.stack(logit_rows)[:, None]
    return (
        output,
        input_grad,
        logit_grad,
        grad_qkv,
        grad_out,
        grad_gain,
        grad_route,
        grad_mixer,
        grad_vec,
        grad_gate,
        grad_up,
        grad_down,
    )


BF = jnp.bfloat16
F32 = jnp.float32
BLOCK = 256
RING = 4
VMEM_BYTES = 60 * 2**20


def dot(left, right, left_dim, right_dim):
    return lax.dot_general(
        left, right, (((left_dim,), (right_dim,)), ((), ())), preferred_element_type=F32
    )


def iota(shape, dim):
    return lax.broadcasted_iota(jnp.int32, shape, dim)


def split3(values):
    high = values.astype(BF).astype(F32)
    rest = values - high
    middle = rest.astype(BF).astype(F32)
    return (high, middle, rest - middle)


def split2(values):
    high = values.astype(BF)
    return (high, (values - high.astype(F32)).astype(BF))


def rows_of(parts, count):
    width = parts[0].shape[1]
    index = iota((count, width), 0)
    total = jnp.zeros((count, width), F32)
    for place, part in enumerate(parts):
        total = jnp.where(index == place, jnp.broadcast_to(part, (count, width)), total)
    return total


def column_of(row, width=128):
    stacked = rows_of(split3(row), 16).astype(BF)
    return dot(stacked, jnp.ones((16, width), BF), 0, 0)


def wide(column, copies):
    return jnp.concatenate([column] * copies, axis=1)


def kernel_call(
    body, idx, args, outs, flops, grid=None, in_specs=None, out_specs=None, scratch=(), share=1
):
    moved = sum(a.size * a.dtype.itemsize for a in args)
    moved += sum(math.prod(s) * jnp.dtype(d).itemsize for s, d in outs)
    whole = pl.BlockSpec(memory_space=pltpu.VMEM)
    extra = {} if grid is None else {"grid": grid}
    return pl.pallas_call(
        body,
        out_shape=[jax.ShapeDtypeStruct(s, d) for s, d in outs],
        in_specs=[pl.BlockSpec(memory_space=pltpu.SMEM)]
        + (in_specs if in_specs is not None else [whole] * len(args)),
        out_specs=out_specs if out_specs is not None else [whole] * len(outs),
        scratch_shapes=list(scratch),
        compiler_params=pltpu.CompilerParams(vmem_limit_bytes=VMEM_BYTES),
        cost_estimate=pl.CostEstimate(
            flops=flops // share, bytes_accessed=moved // share, transcendentals=0
        ),
        **extra,
    )(idx, *args)


def rope_tables(length):
    half = HEAD_DIM // 2
    inverse = (10000.0 ** (-np.arange(half, dtype=np.float32) / half)).astype(np.float32)
    angles = (np.arange(length, dtype=np.float32)[:, None] * inverse[None, :]).astype(np.float64)
    cosine, sine = np.cos(angles), np.sin(angles)
    cosine = np.concatenate([cosine] * 4, axis=1).astype(np.float32)
    sine = np.concatenate([-sine, sine] * 2, axis=1).astype(np.float32)
    return cosine, sine


def turn(values, cosine, sine, direction):
    width = values.shape[1]
    copies = width // cosine.shape[1]
    ahead = pltpu.roll(values, width - HEAD_DIM // 2, 1)
    behind = pltpu.roll(values, HEAD_DIM // 2, 1)
    first = (iota(values.shape, 1) & (HEAD_DIM - 1)) < HEAD_DIM // 2
    partner = jnp.where(first, ahead, behind)
    return values * wide(cosine, copies) + direction * (partner * wide(sine, copies))


def project_kernel(idx, xa, xb, theirs, columns, w_ref, cosine, sine, *outs):
    q_ref, k_ref, v_ref, normed_ref, params_ref, seg_row, seg_col, x_ref = outs
    core, flip = idx[2], idx[3]
    row, column = iota((16, 128), 0), iota((16, 128), 1)
    spread = (row == column) | ((row >= 12) & ((column == row + 4) | (column == row + 8)))
    params_ref[...] = dot(jnp.where(spread, 1.0, 0.0).astype(BF), columns[...], 1, 1)
    sources = (
        (xa, core, 0),
        (xb, core, 1),
        (theirs.at[0], 1 - core, 0),
        (theirs.at[1], 1 - core, 1),
    )
    for ref, half, slot in sources:
        block = 2 * half + (flip if slot == 0 else 1 - flip)
        rows = pl.ds(pl.multiple_of(block * BLOCK, BLOCK), BLOCK)
        x_ref[rows, :] = ref[:BLOCK, :]
        segment = ref[ref.shape[0] - 16 :, :BLOCK].astype(F32)[10:11]
        seg_row[:, rows] = jnp.broadcast_to(segment, (8, BLOCK))
        seg_col[rows, :] = column_of(segment)
    gain = params_ref[14:15, :]
    tiles = [slice(i * BLOCK, (i + 1) * BLOCK) for i in range(x_ref.shape[0] // BLOCK)]
    for rows in tiles:
        x = x_ref[rows, :].astype(F32)
        normed_ref[rows, :] = (x * norm_scale(x) * gain).astype(BF)
    queries, keys, values = (dot(normed_ref[...], w_ref[j], 1, 0) for j in range(3))
    for rows in tiles:
        turned = turn(queries[rows], cosine[rows, :], sine[rows, :], 1.0)
        q_ref[rows, :] = (turned * HEAD_DIM**-0.5).astype(BF)
        k_ref[rows, :] = turn(keys[rows], cosine[rows, :], sine[rows, :], 1.0).astype(BF)
        v_ref[rows, :] = values[rows].astype(BF)


def mask_of(seg_row, seg_col, i):
    n = (i + 1) * BLOCK
    mine = seg_row[:1, i * BLOCK : n]
    key_index, query_index = iota((BLOCK, BLOCK), 0), iota((BLOCK, BLOCK), 1)
    last = (seg_col[i * BLOCK : n, :1] == mine) & (key_index <= query_index)
    bias = jnp.where(last, 0.0, MASKED)
    if i > 0:
        before = jnp.where(seg_col[: i * BLOCK, :1] == mine, 0.0, MASKED)
        bias = jnp.concatenate([before, bias], axis=0)
    return bias


def both_heads(values, low_lanes):
    return jnp.concatenate(
        [jnp.where(low_lanes, values, 0), jnp.where(low_lanes, 0, values)], axis=0
    )


def attend_kernel(idx, q_ref, k_ref, v_ref, seg_row, seg_col, keep_ref, send_ref, lse_ref):
    core, flip = idx[2], idx[3]
    low_lanes = iota((BLOCK, 2 * HEAD_DIM), 1) < HEAD_DIM
    results = []
    for i in range(q_ref.shape[0] // BLOCK):
        n = (i + 1) * BLOCK
        queries = q_ref[i * BLOCK : n, :]
        keys, values = k_ref[:n, :], v_ref[:n, :]
        bias = mask_of(seg_row, seg_col, i)
        both = both_heads(queries, low_lanes)
        scores = dot(keys, both, 1, 1) + wide(bias, 2)
        peak = jnp.max(scores, axis=0, keepdims=True)
        weights = jnp.exp(scores - peak)
        total = jnp.sum(weights, axis=0, keepdims=True)
        out = dot(values, weights.astype(BF), 0, 0)
        lse = peak + jnp.log(total)
        out = out / total
        out = jnp.concatenate([out[:HEAD_DIM, :BLOCK], out[HEAD_DIM:, BLOCK:]], axis=0)
        lse_ref[0, 0:1, i * BLOCK : n] = lse[:, :BLOCK]
        lse_ref[0, 1:2, i * BLOCK : n] = lse[:, BLOCK:]
        half, slot = i // 2, (i % 2) ^ flip
        results.append((half, slot, out.T.astype(BF)))
    for half, slot, attended in results:
        rows = pl.ds(pl.multiple_of(slot * BLOCK, BLOCK), BLOCK)

        @pl.when(half == core)
        def _(attended=attended, rows=rows):
            keep_ref[rows, :] = attended

        @pl.when(half != core)
        def _(attended=attended, rows=rows):
            send_ref[rows, :] = attended


def pair_back_kernel(
    first, idx, q_ref, k_ref, v_ref, own_ref, other_ref, seg_row, seg_col, lse_ref, cosine, sine,
    normed_ref, og_ref, og_recv, *refs,
):
    if first:
        small_ref, grads_ref, shared, key_sum, value_sum = refs
    else:
        grads_ref, shared, key_sum, value_sum = refs
    core, flip = idx[2], idx[3]
    lanes = 2 * HEAD_DIM
    low_lanes = iota((BLOCK, lanes), 1) < HEAD_DIM
    key_sum[...] = jnp.zeros(key_sum.shape, F32)
    value_sum[...] = jnp.zeros(value_sum.shape, F32)
    for i in range(q_ref.shape[0] // BLOCK):
        n = (i + 1) * BLOCK
        keys, values = k_ref[:n, :], v_ref[:n, :]
        half, slot = i // 2, (i % 2) ^ flip
        rows = pl.ds(pl.multiple_of(slot * BLOCK, BLOCK), BLOCK)
        grads = jnp.where(half == core, own_ref[rows, :], other_ref[rows, :])
        queries = both_heads(q_ref[i * BLOCK : n, :], low_lanes)
        grads = both_heads(grads, low_lanes)
        bias = mask_of(seg_row, seg_col, i)
        lse = jnp.concatenate([lse_ref[0, 0:1, i * BLOCK : n], lse_ref[0, 1:2, i * BLOCK : n]], 1)
        weights = jnp.exp(dot(keys, queries, 1, 1) + wide(bias, 2) - lse)
        grad_weights = dot(values, grads, 1, 1)
        delta = jnp.sum(weights * grad_weights, axis=0, keepdims=True)
        grad_scores = (weights * (grad_weights - delta)).astype(BF)
        key_sum[:n, :] += dot(grad_scores, queries, 1, 0)
        value_sum[:n, :] += dot(weights.astype(BF), grads, 1, 0)
        grad_query = dot(grad_scores, keys, 0, 0)
        grad_query = jnp.where(low_lanes, grad_query[:BLOCK], grad_query[BLOCK:]) * HEAD_DIM**-0.5
        tile = slice(i * BLOCK, n)
        turned = turn(grad_query, cosine[tile, :], sine[tile, :], -1.0)
        grads_ref[tile, :lanes] = turned.astype(BF)
    for i in range(q_ref.shape[0] // BLOCK):
        tile = slice(i * BLOCK, (i + 1) * BLOCK)
        turned = turn(key_sum[tile, :], cosine[tile, :], sine[tile, :], -1.0)
        grads_ref[tile, lanes : 2 * lanes] = turned.astype(BF)
        grads_ref[tile, 2 * lanes :] = value_sum[tile, :].astype(BF)
    model = normed_ref.shape[1]
    depth = model // RING
    weight_grads = dot(normed_ref[...], grads_ref[...], 0, 0)
    out_grads = og_ref[...].astype(F32) + og_recv[...].astype(F32)
    for z in range(RING):
        rows = slice(z * depth, (z + 1) * depth)
        for j in range(3):
            piece = weight_grads[rows, j * lanes : (j + 1) * lanes]
            shared[j, z, :depth, :] = piece.astype(BF)
        shared[3, z, :depth, :] = out_grads[rows].astype(BF)
        if first:
            shard = depth // 2
            for j in range(2):
                lane = iota((model, lanes), 1)
                pick = iota((model, lanes), 0) == lane + (z * depth + j * shard)
                pick = jnp.where(pick & (lane < shard), 1.0, 0.0).astype(BF)
                picked = dot(small_ref[...].astype(BF), pick, 1, 0)
                shared[j, z, depth:, :] = picked.astype(BF)
            for j in range(2, RING):
                shared[j, z, depth:, :] = jnp.zeros((16, lanes), BF)


def routed_rows(small, routed):
    index = iota((routed, small.shape[1]), 0).astype(F32)
    return jnp.where((small[8:9, :] == index) | (small[9:10, :] == index), 1.0, 0.0)


def ranks_of(named):
    tokens = named.shape[1]
    before, here = iota((tokens, tokens), 0), iota((tokens, tokens), 1)
    earlier = (before < here) & (before // BLOCK == here // BLOCK)
    stacked = jnp.concatenate([named, jnp.zeros_like(named)], axis=0).astype(BF)
    return dot(stacked, jnp.where(earlier, 1.0, 0.0).astype(BF), 1, 0)[: named.shape[0]]


def pick_row(values, index):
    return jnp.sum(jnp.where(iota(values.shape, 0) == index, values, 0.0), axis=0, keepdims=True)


def slots_of(named, rank, expert, capacity):
    tokens = named.shape[1]
    place = pick_row(rank, expert)
    place = place + jnp.where(iota((1, tokens), 1) >= BLOCK, float(capacity), 0.0)
    slot = iota((2 * capacity, tokens), 0).astype(F32)
    taken = (slot == place) & (pick_row(named, expert) > 0.5)
    return jnp.where(taken, 1.0, 0.0).astype(BF)


def pair_of(first, second):
    return jnp.concatenate([first[:BLOCK, :], second[:BLOCK, :]], axis=0)


def small_of(xa, xb):
    blocks = []
    for packed in (xa, xb):
        values = packed[BLOCK:, :].astype(F32)
        width = values.shape[1] // 3
        logits = values[:8, :width] + values[:8, width : 2 * width] + values[:8, 2 * width :]
        blocks.append(jnp.concatenate([logits, values[8:, :width]], axis=0))
    return jnp.concatenate(blocks, axis=1)


def grad_slots_kernel(idx, xa, xb, ca, cb, out):
    named = routed_rows(small_of(xa, xb), 8)
    rank = ranks_of(named)
    grads = pair_of(ca, cb)
    for expert in range(out.shape[0]):
        taken = slots_of(named, rank, expert, out.shape[1] // 2)
        out[expert] = dot(taken, grads, 1, 0).astype(BF)


def route_kernel(idx, keep, recv, xa, xb, params, mine, theirs, *refs):
    (hidden_ref, ow_ref, state_ref), outs = refs[:3], refs[3:]
    core = idx[2]
    width = keep.shape[1]
    own = pl.ds(pl.multiple_of(core * width, 128), width)
    other = pl.ds(pl.multiple_of((1 - core) * width, 128), width)
    ow_ref[:, own] = mine[...]
    ow_ref[:, other] = theirs[...]
    hidden = (
        pair_of(xa, xb).astype(F32)
        + dot(keep[...], ow_ref[own, :], 1, 0)
        + dot(recv[...], ow_ref[other, :], 1, 0)
    )
    hidden_ref[...] = hidden
    normed = (hidden * norm_scale(hidden) * params[15:16, :]).astype(BF)
    small = small_of(xa, xb)
    logits = dot(params[...].astype(BF), normed, 1, 1)
    named = routed_rows(small, 8)
    rank = ranks_of(named)
    shifted = logits[:8] + small[:8]
    shifted = jnp.exp(shifted - jnp.max(shifted, axis=0, keepdims=True))
    probabilities = shifted / jnp.sum(shifted, axis=0, keepdims=True)
    mixed = []
    for c in range(2):
        first, second = logits[8 + 2 * c : 9 + 2 * c], logits[9 + 2 * c : 10 + 2 * c]
        peak = jnp.maximum(first, second)
        first, second = jnp.exp(first - peak), jnp.exp(second - peak)
        mixed += [first / (first + second), second / (first + second)]
    state_ref[0:8, :] = probabilities
    state_ref[8:16, :] = rows_of(mixed, 8)
    state_ref[16:24, :] = rank
    slots = outs[0].shape[0] - 16
    for k, out in enumerate(outs):
        expert = idx[0] ^ k
        taken = slots_of(named, rank, expert, slots // 2)
        out[:slots, :] = dot(taken, normed, 1, 0).astype(BF)
        gates = rows_of(split3(pick_row(probabilities, expert)), 16).astype(BF)
        out[slots:, :] = jnp.zeros((16, out.shape[1]), BF)
        out[slots:, :slots] = dot(gates, taken, 1, 1).astype(BF)


def expert_kernel(idx, g_own, g_other, weights, *refs):
    pieces, refs = refs[:8], refs[8:]
    lefts, acts, keep, send = refs[:4]
    g_all, scale_all, products, joined, joined_w, entry_sum, dot_sum = refs[4:]
    core = idx[2]
    j = pl.program_id(0)
    slots = g_own.shape[1]
    count, model = g_all.shape
    lanes = dot_sum.shape[1]
    chunk = weights.shape[3]

    @pl.when(j == 0)
    def _():
        for p in range(8):
            grads = (g_own if p < RING else g_other)[idx[0] ^ (p % RING)]
            rows = slice(p * slots, (p + 1) * slots)
            lefts[0, rows, :] = pieces[p][:slots, :]
            scale = dot(pieces[p][slots:, :slots], jnp.ones((16, lanes), BF), 0, 0)
            scale_all[rows, :] = scale
            g_all[rows, :] = grads
            scaled = grads.astype(F32) * wide(scale, model // lanes)
            lefts[1, rows, :] = scaled.astype(BF)
        dot_sum[...] = jnp.zeros(dot_sum.shape, F32)
        entry_sum[...] = jnp.zeros(entry_sum.shape, F32)

    joined_w[:, :chunk] = weights[0, 0]
    joined_w[:, chunk:] = weights[0, 1]
    products[:, : 2 * chunk] = dot(lefts[0], joined_w[...], 1, 0)
    products[:, 2 * chunk :] = dot(g_all[...], weights[0, 2], 1, 0)
    tile = 64
    for i in range(count // tile):
        rows = slice(i * tile, (i + 1) * tile)
        gate, up, back = (products[rows, p * chunk : (p + 1) * chunk] for p in range(3))
        sigma = 0.5 * jnp.tanh(0.5 * gate) + 0.5
        silu = gate * sigma
        inner = silu * up
        acts[2, rows, :] = inner.astype(BF)
        product = inner * back
        dot_sum[rows, :] += product[:, :lanes] + product[:, lanes:]
        back = back * wide(scale_all[rows, :], chunk // lanes)
        grad_gate = (back * up * (sigma + silu - silu * sigma)).astype(BF)
        grad_up = (back * silu).astype(BF)
        acts[0, rows, :] = grad_gate
        acts[1, rows, :] = grad_up
        joined[rows, :chunk] = grad_gate
        joined[rows, chunk:] = grad_up
    entry_sum[...] += dot(joined[...], joined_w[...], 1, 1)

    @pl.when(j == pl.num_programs(0) - 1)
    def _():
        ones = jnp.ones((16, lanes), BF)
        index = iota((16, slots), 0)
        for p in range(8):
            rows = slice(p * slots, (p + 1) * slots)
            high, low = split2(dot_sum[rows, :])
            high, middle, rest = split3(dot(ones, high, 1, 1) + dot(ones, low, 1, 1))
            packed = jnp.where(
                index == 4 * core,
                high,
                jnp.where(
                    index == 4 * core + 1, middle, jnp.where(index == 4 * core + 2, rest, 0.0)
                ),
            )
            out = (keep if p < RING else send).at[idx[0] ^ (p % RING)]
            out[:slots, :] = entry_sum[rows, :].astype(BF)
            out[slots:, :] = jnp.zeros((16, model), BF)
            out[slots:, :slots] = packed.astype(BF)


def expert_out_kernel(idx, inner_ref, weights, keep, send, down):
    slots = keep.shape[1]
    chunk = weights.shape[3]
    for k in range(RING):
        down[:, k * chunk : (k + 1) * chunk] = weights[k, 0]
    out = dot(inner_ref[0], down[...], 1, 1).astype(BF)
    for p in range(8):
        place = idx[0] ^ (p % RING)
        (keep if p < RING else send)[place] = out[p * slots : (p + 1) * slots]


def expert_grads_kernel(idx, left, right, out):
    chunk = out.shape[3]
    grad = dot(left[0], right[0], 0, 0).astype(BF)
    for k in range(out.shape[0]):
        out[k, 0] = grad[:, k * chunk : (k + 1) * chunk]


def slot_table(small, state, capacity):
    named = routed_rows(small, 8)
    rank = state[16:24, :]
    return [slots_of(named, rank, expert, capacity) for expert in range(RING)], named


def branch_weights(state, named):
    gates = state[0:8, :] * named
    consts = [gates[6 + c : 7 + c] for c in range(2)]
    normed_weight = gates[5:6]
    for c in range(2):
        normed_weight = normed_weight + consts[c] * state[8 + 2 * c : 9 + 2 * c, :]
    vector_weights = [consts[c] * state[9 + 2 * c : 10 + 2 * c, :] for c in range(2)]
    return consts, normed_weight, vector_weights


def output_kernel(idx, hidden_ref, state_ref, xa, xb, params, returned, logits_ref, oa, ob):
    state = state_ref[...]
    tables, named = slot_table(small_of(xa, xb), state, returned.shape[1] // 2)
    hidden = hidden_ref[...]
    normed = hidden * norm_scale(hidden) * params[15:16, :]
    _, normed_weight, vector_weights = branch_weights(state, named)
    output = hidden + wide(column_of(normed_weight), normed.shape[1] // 128) * normed
    vector_rows = rows_of(split3(params[12:13, :])[:2] * 2 + split3(params[13:14, :])[:2] * 2, 16)
    first, second = split3(vector_weights[0])[:2], split3(vector_weights[1])[:2]
    weight_rows = rows_of(
        (first[0], first[0], first[1], first[1], second[0], second[0], second[1], second[1]), 16
    )
    output += dot(weight_rows.astype(BF), vector_rows.astype(BF), 0, 0)
    for k in range(RING):
        gate = state[k : k + 1, :]
        high, low, _ = split3(gate)
        table = tables[k].astype(F32)
        output += dot((table * high).astype(BF), returned[k], 0, 0)
        output += dot((table * low).astype(BF), returned[k], 0, 0)
    for slot, out in enumerate((oa, ob)):
        out[:BLOCK, :] = output[slot * BLOCK : (slot + 1) * BLOCK].astype(BF)
        parts = split3(logits_ref[:, slot * BLOCK : (slot + 1) * BLOCK])
        parts = jnp.concatenate(parts, axis=1)
        out[BLOCK:, :] = jnp.concatenate([parts, jnp.zeros_like(parts)], axis=0).astype(BF)


def hidden_back_kernel(
    idx, hidden_ref, state_ref, xa, xb, ca, cb, params, ow_ref, returned, *outs
):
    gh_ref, low_ref, own_ref, send_ref, logits_ref, small_ref = outs
    core = idx[2]
    state = state_ref[...]
    slots = returned.shape[1] - 16
    tables, named = slot_table(small_of(xa, xb), state, slots // 2)
    probabilities = state[0:8, :]
    hidden = hidden_ref[...]
    factor = norm_scale(hidden)
    scaled_hidden = hidden * factor
    normed = scaled_hidden * params[15:16, :]
    normed_low = normed.astype(BF)
    grads_low = pair_of(ca, cb)
    grads = grads_low.astype(F32)
    ones = jnp.ones((16, hidden.shape[1]), BF)
    high, low = split2(grads * normed)
    on_normed = (dot(ones, high, 1, 1) + dot(ones, low, 1, 1))[0:1]
    first, second = split3(params[12:13, :])[:2], split3(params[13:14, :])[:2]
    on_vectors = dot(rows_of(first + second, 16).astype(BF), grads_low, 1, 1)
    on_vector = (on_vectors[0:1] + on_vectors[1:2], on_vectors[2:3] + on_vectors[3:4])
    consts, normed_weight, vector_weights = branch_weights(state, named)
    index = iota(probabilities.shape, 0)
    grad_probs = jnp.where(index == 5, on_normed, 0.0)
    mix_rows = []
    for c in range(2):
        mix_first, mix_second = state[8 + 2 * c : 9 + 2 * c, :], state[9 + 2 * c : 10 + 2 * c, :]
        dot_c = mix_first * on_normed + mix_second * on_vector[c]
        grad_probs = jnp.where(index == 6 + c, dot_c, grad_probs)
        grad_first, grad_second = consts[c] * on_normed, consts[c] * on_vector[c]
        mean = mix_first * grad_first + mix_second * grad_second
        mix_rows += [mix_first * (grad_first - mean), mix_second * (grad_second - mean)]
    back = jnp.zeros(hidden.shape, F32)
    for k in range(RING):
        packed = returned[k, slots:, :slots]
        found = jnp.sum(dot(packed, tables[k], 1, 0), axis=0, keepdims=True)
        grad_probs = jnp.where(index == k, found, grad_probs)
        back += dot(tables[k], returned[k, :slots, :], 0, 0)
    grad_probs = grad_probs * named
    grad_logits = probabilities * (
        grad_probs - jnp.sum(probabilities * grad_probs, axis=0, keepdims=True)
    )
    logits_ref[...] = grad_logits
    router_rows = jnp.concatenate([grad_logits, rows_of(mix_rows, 8)], axis=0)
    rows_high, rows_low = split2(router_rows)
    weights_low = params[...].astype(BF)
    grad_normed = (
        back
        + dot(rows_high, weights_low, 0, 0)
        + dot(rows_low, weights_low, 0, 0)
        + wide(column_of(normed_weight), hidden.shape[1] // 128) * grads
    )
    router_grad = dot(rows_high, normed_low, 1, 0) + dot(rows_low, normed_low, 1, 0)
    first, second = split3(vector_weights[0])[:2], split3(vector_weights[1])[:2]
    vector_grad = dot(rows_of(first + second, 16).astype(BF), grads_low, 1, 0)
    gain_grad = jnp.sum(grad_normed * scaled_hidden, axis=0, keepdims=True)
    small_ref[...] = jnp.where(
        iota(router_grad.shape, 0) < 12,
        router_grad,
        rows_of(
            [jnp.zeros_like(gain_grad)] * 12
            + [vector_grad[0:1] + vector_grad[1:2], vector_grad[2:3] + vector_grad[3:4], gain_grad],
            16,
        ),
    )
    scaled = grad_normed * params[15:16, :]
    mean = jnp.mean(scaled * hidden, axis=-1, keepdims=True)
    grad_hidden = grads + factor * scaled - hidden * (factor * factor * factor * mean)
    gh_ref[...] = grad_hidden
    grad_low = grad_hidden.astype(BF)
    low_ref[...] = grad_low
    width = own_ref.shape[1]
    own_rows = pl.ds(pl.multiple_of(core * width, 16), width)
    other_rows = pl.ds(pl.multiple_of((1 - core) * width, 16), width)
    own_ref[...] = dot(grad_low, ow_ref[own_rows, :], 1, 1).astype(BF)
    send_ref[...] = dot(grad_low, ow_ref[other_rows, :], 1, 1).astype(BF)


def out_grad_kernel(idx, keep, recv, low_ref, own_ref, send_ref):
    core = idx[2]
    width = keep.shape[1]
    own = pl.ds(pl.multiple_of(core * width, 128), width)
    other = pl.ds(pl.multiple_of((1 - core) * width, 128), width)
    for out, columns in ((own_ref, own), (send_ref, other)):
        grads = low_ref[:, columns]
        out[own, :] = dot(keep[...], grads, 0, 0).astype(BF)
        out[other, :] = dot(recv[...], grads, 0, 0).astype(BF)


def normed_back_kernel(idx, *refs):
    pair_grads, w_ref, keep_ref, send_ref, grads, weights = refs[:3], *refs[3:]
    core, flip = idx[2], idx[3]
    lanes = 2 * HEAD_DIM
    for h, ref in enumerate(pair_grads):
        columns = slice(h * 3 * lanes, (h + 1) * 3 * lanes)
        grads[:, columns] = ref[...]
        for j in range(3):
            place = (3 * h + j) * lanes
            weights[:, place : place + lanes] = w_ref[j, :, h * lanes : (h + 1) * lanes]
    total = dot(grads[...], weights[...], 1, 1).astype(BF)
    for half in range(2):
        for out, there in ((keep_ref, half == core), (send_ref, half != core)):

            @pl.when(there)
            def _(half=half, out=out):
                for part in range(2):
                    place = 2 * half + part
                    rows = pl.ds(pl.multiple_of((part ^ flip) * BLOCK, BLOCK), BLOCK)
                    out[rows, :] = total[place * BLOCK : (place + 1) * BLOCK]


def input_back_kernel(idx, keep_ref, recv_ref, gh_ref, xa, xb, params, oa, ob):
    gain = params[14:15, :]
    for slot, (x_ref, out) in enumerate(((xa, oa), (xb, ob))):
        tile = slice(slot * BLOCK, (slot + 1) * BLOCK)
        x = x_ref[:BLOCK, :].astype(F32)
        factor = norm_scale(x)
        scaled = (keep_ref[tile, :].astype(F32) + recv_ref[tile, :].astype(F32)) * gain
        mean = jnp.mean(scaled * x, axis=-1, keepdims=True)
        out[...] = (
            gh_ref[tile, :] + factor * scaled - x * (factor * factor * factor * mean)
        ).astype(BF)


def across(values):
    return lax.ppermute(values, "dp", [(0, 1), (1, 0)])


def over(values, k):
    return lax.ppermute(values, "experts", [(i, i ^ k) for i in range(RING)])


def exchange(values, axis):
    return lax.all_to_all(values, axis, 0, 0, tiled=True)


def after(values, *others):
    return lax.optimization_barrier((values, others))[0]


def handed_to_all(values, axis):
    return exchange(jnp.broadcast_to(values[None], (RING, *values.shape)), axis)


def chip_local(
    inputs, cotangent, qkv_weight, out_weight, norm_gains, route_weight, const_gate, const_vec,
    w_gate, w_up, w_down, prev_logits, routes, segments,
):
    e, z, core = lax.axis_index("experts"), lax.axis_index("context"), lax.axis_index("dp")
    flip = z // 2
    idx = jnp.stack([e, z, core, flip]).astype(jnp.int32)
    odd = lax.rem(z, 2)
    rows, model = inputs.shape[2], inputs.shape[3]
    length = rows * RING
    half_model = model // 2
    slots = 2 * (rows * 5 // 16)

    def place(z_index, d, which):
        micro = z_index % 2 if which == 0 else 1 - z_index % 2
        return (2 * micro + d) * 2 + z_index // 2

    routes_of = [
        [(zi * 2 + d, place(zi, d, which)) for zi in range(RING) for d in range(2)]
        for which in range(2)
    ]

    def leave(values):
        return [
            lax.ppermute(
                lax.dynamic_index_in_dim(values, odd if which == 0 else 1 - odd, 0, False),
                ("context", "dp"),
                routes_of[which],
            )
            for which in range(2)
        ]

    def go_home(values, which):
        return lax.ppermute(values, ("context", "dp"), [(b, a) for a, b in routes_of[which]])

    def at_home(*got):
        return jnp.where(odd == 0, jnp.stack(got), jnp.stack(got[::-1]))

    def columns_of(values, side):
        return lax.dynamic_slice_in_dim(values, side * half_model, half_model, values.ndim - 1)

    def in_order(mine, theirs, axis):
        pair = jnp.stack([mine, theirs], axis=axis), jnp.stack([theirs, mine], axis=axis)
        return jnp.where(core == 0, *pair)

    vectors = split3(jnp.concatenate([const_vec, norm_gains], axis=0).T)
    columns = jnp.concatenate(
        [route_weight, const_gate, *(part.astype(BF) for part in vectors)], axis=1
    )
    columns = jnp.pad(columns, ((0, 0), (0, 128 - columns.shape[1])))
    matrix = lax.dynamic_index_in_dim(
        jnp.concatenate([qkv_weight, out_weight[None]], axis=0), e, 0, False
    )
    ring = handed_to_all(jnp.concatenate([matrix, columns], axis=1), "context")
    logit_parts = jnp.concatenate(split3(jnp.swapaxes(prev_logits[:, 0], 1, 2)), axis=2)
    ids = jnp.concatenate([jnp.swapaxes(routes[:, 0], 1, 2), segments], axis=1).astype(F32)
    ids = jnp.pad(ids, ((0, 0), (0, 5), (0, 2 * rows)))
    xa, xb = leave(
        jnp.concatenate([inputs[:, 0], logit_parts.astype(BF), ids.astype(BF)], axis=1)
    )
    ring, xa, xb = lax.optimization_barrier((ring, xa, xb))

    def my_part(side):
        return jnp.concatenate([columns_of(ring[:, :, :model], side), ring[:, :, model:]], axis=2)

    shared = in_order(my_part(core), across(my_part(1 - core)), 1)
    shared = shared.reshape(model, half_model + 128)
    columns = shared[:, half_model:]
    w_all = handed_to_all(shared[:, :half_model], "experts")
    theirs = across(jnp.stack([xa, xb]))

    stacked = jnp.stack([w_gate[0], w_up[0], w_down[0]])
    expert_w = lax.all_gather(after(stacked, ring), "context", axis=0)
    ca, cb = leave(after(cotangent[:, 0], shared))

    cosine, sine = (jnp.asarray(t) for t in rope_tables(length))
    q, k, v, normed_in, params, seg_row, seg_col = kernel_call(
        project_kernel,
        idx,
        [xa, xb, theirs, columns, w_all, cosine, sine],
        [((length, half_model), BF)] * 3
        + [((length, model), BF)]
        + [((16, model), F32), ((8, length), F32), ((length, 128), F32)],
        flops=2 * length * model * 3 * half_model,
        share=100,
        scratch=[pltpu.VMEM((length, model), BF)],
    )
    pairs = half_model // (2 * HEAD_DIM)
    lanes = 2 * HEAD_DIM
    by_pair = pl.BlockSpec((length, lanes), lambda h: (0, h))
    half_by_pair = pl.BlockSpec((length // 2, lanes), lambda h: (0, h))
    all_of = pl.BlockSpec(memory_space=pltpu.VMEM)
    lse_spec = pl.BlockSpec((1, 8, length), lambda h: (h, 0, 0))
    keep, send, lse = kernel_call(
        attend_kernel,
        idx,
        [q, k, v, seg_row, seg_col],
        [((length // 2, half_model), BF)] * 2 + [((pairs, 8, length), F32)],
        flops=4 * length * length * half_model,
        share=100,
        grid=(pairs,),
        in_specs=[by_pair] * 3 + [all_of] * 2,
        out_specs=[half_by_pair] * 2 + [lse_spec],
    )
    ca, cb = after((ca, cb), keep)
    (g_slots,) = kernel_call(
        grad_slots_kernel,
        idx,
        [xa, xb, ca, cb],
        [((RING, slots, model), BF)],
        flops=2 * RING * slots * 2 * rows * model,
    )
    g_mine = exchange(g_slots, "experts")
    recv = after(across(send), g_slots)

    hidden, ow_all, state, *sent = kernel_call(
        route_kernel,
        idx,
        [keep, recv, xa, xb, params, w_all[3], across(w_all[3])],
        [((2 * rows, model), F32), ((model, model), BF), ((24, 2 * rows), F32)]
        + [((slots + 16, model), BF)] * RING,
        flops=2 * 2 * rows * model * model + 2 * RING * slots * 2 * rows * model,
    )
    t_mine = [sent[0]] + [over(after(sent[k], g_mine), k) for k in range(1, RING)]
    g_theirs = across(g_mine)
    t_theirs = [across(t) for t in t_mine]

    count = 8 * slots
    chunk = w_gate.shape[2]
    hidden_units = RING * chunk
    lefts, acts, entry_keep, entry_send = kernel_call(
        expert_kernel,
        idx,
        [g_mine, g_theirs, expert_w, *t_mine, *t_theirs],
        [((2, count, model), BF), ((3, count, hidden_units), BF)]
        + [((RING, slots + 16, model), BF)] * 2,
        flops=10 * count * model * hidden_units,
        grid=(RING,),
        in_specs=[all_of] * 2
        + [pl.BlockSpec((1, 3, model, chunk), lambda j: (j, 0, 0, 0))]
        + [all_of] * 8,
        out_specs=[all_of, pl.BlockSpec((3, count, chunk), lambda j: (0, 0, j))] + [all_of] * 2,
        scratch=[
            pltpu.VMEM((count, model), BF),
            pltpu.VMEM((count, 128), F32),
            pltpu.VMEM((count, 3 * chunk), F32),
            pltpu.VMEM((count, 2 * chunk), BF),
            pltpu.VMEM((model, 2 * chunk), BF),
            pltpu.VMEM((count, model), F32),
            pltpu.VMEM((count, 128), F32),
        ],
    )

    def both_cores(kept, received):
        return (kept.astype(F32) + received.astype(F32)).astype(BF)

    entry_sum = both_cores(entry_keep, across(entry_send))
    entry_back = exchange(entry_sum, "experts")
    (far_grads,) = kernel_call(
        expert_grads_kernel,
        idx,
        [after(lefts, entry_sum), acts],
        [((RING, 3, model, chunk), BF)],
        flops=6 * count * model * hidden_units,
        grid=(3,),
        in_specs=[
            pl.BlockSpec((1, count, model), lambda j: (j // 2, 0, 0)),
            pl.BlockSpec((1, count, hidden_units), lambda j: (j, 0, 0)),
        ],
        out_specs=[pl.BlockSpec((RING, 1, model, chunk), lambda j: (0, j, 0, 0))],
    )
    out_keep, out_send = kernel_call(
        expert_out_kernel,
        idx,
        [after(acts, far_grads), expert_w],
        [((RING, slots, model), BF)] * 2,
        flops=2 * count * model * hidden_units,
        grid=(1,),
        in_specs=[
            pl.BlockSpec((1, count, hidden_units), lambda j: (2, 0, 0)),
            pl.BlockSpec((RING, 1, model, chunk), lambda j: (0, 2, 0, 0)),
        ],
        out_specs=[all_of] * 2,
        scratch=[pltpu.VMEM((model, hidden_units), BF)],
    )
    entry_back, out_send, far_grads = lax.optimization_barrier(
        (entry_back, out_send, far_grads)
    )
    expert_grads = lax.psum_scatter(far_grads, "context", scatter_dimension=0).astype(F32)

    grad_hidden, grad_low, ga_own, ga_send, logit_rows, small_grad = kernel_call(
        hidden_back_kernel,
        idx,
        [hidden, state, xa, xb, ca, cb, params, ow_all, entry_back],
        [((2 * rows, model), F32), ((2 * rows, model), BF)]
        + [((2 * rows, half_model), BF)] * 2
        + [((8, 2 * rows), F32), ((16, model), F32)],
        flops=2 * 2 * rows * model * model + 2 * RING * slots * 2 * rows * model,
    )
    ga_other = across(ga_send)
    out_sum = both_cores(out_keep, after(across(out_send), ga_send))
    out_back = exchange(out_sum, "experts")
    og_own, og_send = kernel_call(
        out_grad_kernel,
        idx,
        [keep, recv, grad_low],
        [((model, half_model), BF)] * 2,
        flops=2 * 2 * rows * model * model,
    )
    og_other = across(og_send)
    q = after(q, out_sum)
    shared_parts, pair_grads = [], []
    for h in range(pairs):
        at = lambda n, h=h: pl.BlockSpec((n, lanes), lambda i: (0, h))
        extra = 16 if h == 0 else 0
        grads, part = kernel_call(
            functools.partial(pair_back_kernel, h == 0),
            idx,
            [q, k, v, ga_own, ga_other, seg_row, seg_col, lse, cosine, sine, normed_in]
            + [og_own, og_other]
            + ([small_grad] if h == 0 else []),
            [((length, 3 * lanes), BF), ((RING, RING, model // RING + extra, lanes), BF)],
            flops=10 * length * length * lanes + 6 * length * model * lanes,
            grid=(1,),
            in_specs=[at(length)] * 3
            + [at(length // 2)] * 2
            + [all_of] * 2
            + [pl.BlockSpec((1, 8, length), lambda i, h=h: (h, 0, 0))]
            + [all_of] * 3
            + [at(model)] * 2
            + ([all_of] if h == 0 else []),
            out_specs=[all_of] * 2,
            scratch=[pltpu.VMEM((length, lanes), F32)] * 2,
        )
        pair_grads.append(grads)
        shared_parts.append(exchange(part, "experts"))
        if h == 0:
            q = after(q, out_back)
        if h == 1:
            q = after(q, shared_parts[0])
        if h == 2:
            w_all = after(w_all, shared_parts[1])
    depth = model // RING
    gn_keep, gn_send = kernel_call(
        normed_back_kernel,
        idx,
        [*pair_grads, w_all],
        [((2 * rows, model), BF)] * 2,
        flops=2 * length * model * 3 * half_model,
        scratch=[pltpu.VMEM((length, 3 * half_model), BF), pltpu.VMEM((model, 3 * half_model), BF)],
    )

    ia, ib = kernel_call(
        input_back_kernel,
        idx,
        [gn_keep, across(gn_send), grad_hidden, xa, xb, params],
        [((rows, model), BF)] * 2,
        flops=0,
    )
    oa, ob = kernel_call(
        output_kernel,
        idx,
        [after(hidden, ia), state, xa, xb, params, out_back, logit_rows],
        [((rows + 16, model), BF)] * 2,
        flops=4 * RING * slots * 2 * rows * model,
    )
    home = at_home(go_home(oa, 0), go_home(ob, 1))
    output = home[:, None, :rows]
    logit_grad = home[:, rows : rows + 8].astype(F32).reshape(2, 8, 3, rows).sum(axis=2)
    logit_grad = jnp.swapaxes(logit_grad, 1, 2)[:, None]
    shared_parts[2] = after(shared_parts[2], ia, oa)
    sums = [part.astype(F32).sum(axis=0).astype(BF) for part in shared_parts]
    parts = jnp.concatenate([part[:, :depth] for part in sums], axis=2)
    rest = jnp.pad(sums[0][:, depth:], ((0, 0), (0, 0), (0, half_model - lanes)))
    parts = jnp.concatenate([parts, rest], axis=1)
    ia, ib = go_home(ia, 0), go_home(ib, 1)
    input_grad = at_home(ia, ib).astype(F32)[:, None]
    parts = after(exchange(parts, "context"), ia, ib).astype(F32).sum(axis=0)
    shard = depth // 2
    rest = parts[depth:]
    given = jnp.concatenate(
        [lax.dynamic_slice_in_dim(parts, (1 - core) * shard, shard, 0), rest], axis=0
    )
    taken = across(given.astype(BF)).astype(F32)
    grads = in_order(lax.dynamic_slice_in_dim(parts, core * shard, shard, 0), taken[:shard], 1)
    rest = jnp.pad(rest + taken[shard:], ((0, 0), (0, half_model)))
    grads = jnp.concatenate([grads.reshape(shard, model), rest], axis=0).astype(BF)
    grads = handed_to_all(grads, "experts").astype(F32)
    small_grad = lax.dynamic_index_in_dim(grads, core, 0, False)[shard:, :shard]
    qkv_grad = grads[:3, :shard]
    gain_first = (qkv_grad * qkv_weight.astype(F32)).sum(axis=(0, 2)) / norm_gains[0]
    return (
        output,
        input_grad,
        logit_grad,
        qkv_grad,
        grads[3, :shard],
        jnp.stack([gain_first, small_grad[14]]),
        small_grad[:8].T,
        small_grad[8:12].T,
        small_grad[12:14],
        expert_grads[0][None],
        expert_grads[1][None],
        expert_grads[2][None],
    )


def whole_sequence_fits(mesh):
    return (mesh.shape["experts"], mesh.shape["context"], mesh.shape["dp"]) == (4, 4, 2)


def solution(mesh):
    local = chip_local if whole_sequence_fits(mesh) else general_local
    in_specs = (
        P(None, ("experts", "dp"), "context", None),
        P(None, ("experts", "dp"), "context", None),
        P(None, ("context", "dp"), None),
        P(("context", "dp"), None),
        P(None, ("context", "dp")),
        P(("context", "dp"), None),
        P(("context", "dp"), None),
        P(None, ("context", "dp")),
        P("experts", None, ("context", "dp")),
        P("experts", None, ("context", "dp")),
        P("experts", None, ("context", "dp")),
        P(None, ("experts", "dp"), "context", None),
        P(None, ("experts", "dp"), "context", None),
        P(None, ("experts", "dp"), "context"),
    )
    out_specs = (
        P(None, ("experts", "dp"), "context", None),
        P(None, ("experts", "dp"), "context", None),
        P(None, ("experts", "dp"), "context", None),
        P(None, ("context", "dp"), None),
        P(("context", "dp"), None),
        P(None, ("context", "dp")),
        P(("context", "dp"), None),
        P(("context", "dp"), None),
        P(None, ("context", "dp")),
        P("experts", None, ("context", "dp")),
        P("experts", None, ("context", "dp")),
        P("experts", None, ("context", "dp")),
    )
    return jax.shard_map(local, mesh=mesh, in_specs=in_specs, out_specs=out_specs, check_vma=False)
```

```python
import functools
import functools
import math

import jax
import jax.numpy as jnp
import numpy as np
from jax import lax
from jax.experimental import pallas as pl
from jax.experimental.pallas import tpu as pltpu
from jax.sharding import PartitionSpec as P

HEAD_DIM = 64
FF = 2048


EPSILON = 1e-05
MASKED = -1e30


def rotate(values, positions, direction):
    half_dim = values.shape[-1] // 2
    inverse = 10000.0 ** (-jnp.arange(half_dim, dtype=jnp.float32) / half_dim)
    angles = positions.astype(jnp.float32)[:, None] * inverse[None, :]
    cosine = jnp.cos(angles)[:, None, :]
    sine_part = jnp.sin(angles)[:, None, :]
    first_half = values[..., :half_dim]
    second = values[..., half_dim:]
    return jnp.concatenate(
        [
            first_half * cosine - direction * second * sine_part,
            second * cosine + direction * first_half * sine_part,
        ],
        axis=-1,
    )


def softmax_last(logits):
    shifted = jnp.exp(logits - jnp.max(logits, axis=-1, keepdims=True))
    return shifted / jnp.sum(shifted, axis=-1, keepdims=True)


def norm_scale(values):
    return lax.rsqrt(jnp.mean(values * values, axis=-1, keepdims=True) + EPSILON)


def norm_back(grad_in, values, factor, gain_vec):
    scaled = grad_in * gain_vec
    grad_gain = jnp.sum(grad_in * values * factor, axis=0)
    grad_values = factor * scaled - values * factor * factor * factor * jnp.mean(
        scaled * values, axis=-1, keepdims=True
    )
    return (grad_values, grad_gain)


def masked_scores(
    queries, key_rows, query_segments, key_segments, query_positions, key_positions, score_scale
):
    scores = (
        jnp.einsum("qhd,khd->hqk", queries, key_rows, preferred_element_type=jnp.float32)
        * score_scale
    )
    allowed = (query_segments[:, None] == key_segments[None, :]) & (
        key_positions[None, :] <= query_positions[:, None]
    )
    return (jnp.where(allowed[None], scores, MASKED), allowed)


def general_local(
    inputs,
    cotangent,
    qkv_weight,
    out_weight,
    norm_gains,
    route_weight,
    const_gate,
    const_vec,
    w_gate,
    w_up,
    w_down,
    prev_logits,
    routes,
    segments,
):
    micro_count = inputs.shape[0]
    row_count = inputs.shape[2]
    model_width = inputs.shape[3]
    head_count = model_width // HEAD_DIM
    score_scale = HEAD_DIM ** (-0.5)
    local_experts = w_gate.shape[0]
    experts = local_experts * lax.axis_size("experts")
    capacity = row_count * 5 // 16
    routed = prev_logits.shape[3]
    assigned = 2 * row_count
    head_shape = (row_count, head_count, HEAD_DIM)
    positions = lax.axis_index("context") * row_count + jnp.arange(row_count, dtype=jnp.int32)
    grad_qkv = jnp.zeros((3, model_width, model_width), jnp.float32)
    grad_out = jnp.zeros((model_width, model_width), jnp.float32)
    gain_first = jnp.zeros((model_width,), jnp.float32)
    gain_second = jnp.zeros((model_width,), jnp.float32)
    grad_vec = jnp.zeros((2, model_width), jnp.float32)
    grad_route = jnp.zeros((model_width, routed), jnp.float32)
    grad_mixer = jnp.zeros((model_width, 4), jnp.float32)
    grad_gate = jnp.zeros((local_experts, model_width, FF), jnp.float32)
    grad_up = jnp.zeros((local_experts, model_width, FF), jnp.float32)
    grad_down = jnp.zeros((local_experts, model_width, FF), jnp.float32)
    output_rows = []
    input_rows = []
    logit_rows = []
    for batch_index in range(micro_count):
        qkv_full, out_full, gains, vectors, route_full, mixer_full = (
            lax.all_gather(qkv_weight, ("context", "dp"), axis=1, tiled=True),
            lax.all_gather(out_weight, ("context", "dp"), axis=0, tiled=True),
            lax.all_gather(
                norm_gains.astype(jnp.bfloat16), ("context", "dp"), axis=1, tiled=True
            ).astype(norm_gains.dtype),
            lax.all_gather(
                const_vec.astype(jnp.bfloat16), ("context", "dp"), axis=1, tiled=True
            ).astype(const_vec.dtype),
            lax.all_gather(route_weight, ("context", "dp"), axis=0, tiled=True),
            lax.all_gather(const_gate, ("context", "dp"), axis=0, tiled=True),
        )
        gate_full, up_full, down_full = (
            lax.all_gather(w_gate, ("context", "dp"), axis=2, tiled=True),
            lax.all_gather(w_up, ("context", "dp"), axis=2, tiled=True),
            lax.all_gather(w_down, ("context", "dp"), axis=2, tiled=True),
        )
        token_rows = inputs[batch_index, 0].astype(jnp.float32)
        seg_rows = segments[batch_index, 0]
        route_rows = routes[batch_index, 0]
        grad_rows = cotangent[batch_index, 0].astype(jnp.float32)
        scale_first = norm_scale(token_rows)
        normed_in = (token_rows * scale_first * gains[0]).astype(jnp.bfloat16)
        projected = jnp.einsum(
            "qd,cde->cqe", normed_in, qkv_full, preferred_element_type=jnp.float32
        )
        queries = rotate(projected[0].reshape(head_shape), positions, 1.0).astype(jnp.bfloat16)
        rotated_keys = rotate(projected[1].reshape(head_shape), positions, 1.0).astype(jnp.bfloat16)
        values = projected[2].reshape(head_shape).astype(jnp.bfloat16)
        row_peak = jnp.full((head_count, row_count), MASKED, jnp.float32)
        key_block = lax.all_gather(rotated_keys, "context", axis=0, tiled=True)
        value_block = lax.all_gather(values, "context", axis=0, tiled=True)
        segment_block = lax.all_gather(seg_rows, "context", axis=0, tiled=True)
        key_positions = jnp.arange(key_block.shape[0], dtype=jnp.int32)
        scores, allowed = masked_scores(
            queries, key_block, seg_rows, segment_block, positions, key_positions, score_scale
        )
        new_peak = jnp.maximum(row_peak, jnp.max(scores, axis=-1))
        expo = jnp.where(allowed[None], jnp.exp(scores - new_peak[:, :, None]), 0.0)
        weighted = jnp.einsum(
            "hqk,khd->hqd",
            expo.astype(jnp.bfloat16),
            value_block,
            preferred_element_type=jnp.float32,
        )
        row_peak, row_total, weighted = (new_peak, jnp.sum(expo, axis=-1), weighted)
        log_total = row_peak + jnp.log(row_total)
        attn_heads = jnp.transpose(weighted / row_total[:, :, None], (1, 0, 2))
        attended = attn_heads.reshape(row_count, model_width).astype(jnp.bfloat16)
        hidden = token_rows + jnp.dot(attended, out_full, preferred_element_type=jnp.float32)
        scale_second = norm_scale(hidden)
        normed = hidden * scale_second * gains[1]
        normed_low = normed.astype(jnp.bfloat16)
        logits = (
            jnp.dot(normed_low, route_full, preferred_element_type=jnp.float32)
            + prev_logits[batch_index, 0]
        )
        probabilities = softmax_last(logits)
        gate_values = jnp.take_along_axis(probabilities, route_rows, axis=-1)
        route_ids = route_rows.reshape(-1)
        routed_ffn = route_ids < experts
        onehot = (route_ids[:, None] == jnp.arange(experts, dtype=jnp.int32)[None, :]).astype(
            jnp.int32
        )
        slot_index = jnp.sum((jnp.cumsum(onehot, axis=0) - onehot) * onehot, axis=-1)
        slot_table = (
            jnp.full((experts, capacity), assigned, jnp.int32)
            .at[jnp.where(routed_ffn, route_ids, experts), slot_index]
            .set(jnp.arange(assigned, dtype=jnp.int32), mode="drop")
        )
        token_of = jnp.where(slot_table < assigned, slot_table // 2, row_count)
        pad_rows = jnp.concatenate([normed_low, jnp.zeros((1, model_width), jnp.bfloat16)], axis=0)
        received = lax.all_to_all(
            pad_rows[token_of], "experts", split_axis=0, concat_axis=1, tiled=True
        )
        gate_act = jnp.einsum(
            "erd,edf->erf", received, gate_full, preferred_element_type=jnp.float32
        )
        up_act = jnp.einsum("erd,edf->erf", received, up_full, preferred_element_type=jnp.float32)
        sigma = jax.nn.sigmoid(gate_act)
        silu_act = gate_act * sigma
        inner_low = (silu_act * up_act).astype(jnp.bfloat16)
        expert_low = jnp.einsum(
            "erf,edf->erd", inner_low, down_full, preferred_element_type=jnp.float32
        ).astype(jnp.bfloat16)
        returned = lax.all_to_all(
            expert_low, "experts", split_axis=1, concat_axis=0, tiled=True
        ).reshape(experts * capacity, model_width)
        pick_index = jnp.where(routed_ffn, route_ids * capacity + slot_index, 0)
        expert_out = jnp.where(
            routed_ffn[:, None], returned[pick_index].astype(jnp.float32), 0.0
        ).reshape(row_count, 2, model_width)
        const_mix = softmax_last(
            jnp.dot(normed_low, mixer_full, preferred_element_type=jnp.float32).reshape(
                row_count, 2, 2
            )
        )
        const_out = (
            const_mix[:, :, 0:1] * normed[:, None, :] + const_mix[:, :, 1:2] * vectors[None, :, :]
        )
        copy_mask = (route_rows == experts + 1).astype(jnp.float32)
        const_pick = (
            route_rows[:, :, None] == experts + 2 + jnp.arange(2, dtype=jnp.int32)[None, None, :]
        ).astype(jnp.float32)
        branch = (
            expert_out
            + copy_mask[:, :, None] * normed[:, None, :]
            + jnp.einsum("qjc,qcd->qjd", const_pick, const_out, precision=lax.Precision.HIGHEST)
        )
        output_rows.append(
            (hidden + jnp.sum(gate_values[:, :, None] * branch, axis=1)).astype(jnp.bfloat16)
        )
        grad_branch = gate_values[:, :, None] * grad_rows[:, None, :]
        grad_gates = jnp.sum(grad_rows[:, None, :] * branch, axis=-1)
        grad_probs = jnp.sum(
            (route_rows[:, :, None] == jnp.arange(routed, dtype=jnp.int32)[None, None, :]).astype(
                jnp.float32
            )
            * grad_gates[:, :, None],
            axis=1,
        )
        grad_logits = probabilities * (
            grad_probs - jnp.sum(probabilities * grad_probs, axis=-1, keepdims=True)
        )
        logit_rows.append(grad_logits)
        normed_wide = normed_low.astype(jnp.float32)
        grad_route = grad_route + jnp.dot(
            normed_wide.T, grad_logits, precision=lax.Precision.HIGHEST
        )
        grad_normed = jnp.dot(
            grad_logits, route_full.astype(jnp.float32).T, precision=lax.Precision.HIGHEST
        )
        grad_normed = grad_normed + jnp.sum(copy_mask[:, :, None] * grad_branch, axis=1)
        grad_const = jnp.einsum(
            "qjc,qjd->qcd", const_pick, grad_branch, precision=lax.Precision.HIGHEST
        )
        grad_mix = jnp.stack(
            [
                jnp.sum(grad_const * normed[:, None, :], axis=-1),
                jnp.sum(grad_const * vectors[None, :, :], axis=-1),
            ],
            axis=-1,
        )
        grad_mix_logits = (
            const_mix * (grad_mix - jnp.sum(const_mix * grad_mix, axis=-1, keepdims=True))
        ).reshape(row_count, 4)
        grad_mixer = grad_mixer + jnp.dot(
            normed_wide.T, grad_mix_logits, precision=lax.Precision.HIGHEST
        )
        grad_normed = grad_normed + jnp.dot(
            grad_mix_logits, mixer_full.astype(jnp.float32).T, precision=lax.Precision.HIGHEST
        )
        grad_normed = grad_normed + jnp.sum(const_mix[:, :, 0:1] * grad_const, axis=1)
        grad_vec = grad_vec + jnp.sum(const_mix[:, :, 1:2] * grad_const, axis=0)
        grad_slots = jnp.where(
            routed_ffn[:, None], grad_branch.reshape(assigned, model_width), 0.0
        ).astype(jnp.bfloat16)
        grad_pad = jnp.concatenate([grad_slots, jnp.zeros((1, model_width), jnp.bfloat16)], axis=0)
        grad_received = lax.all_to_all(
            grad_pad[slot_table], "experts", split_axis=0, concat_axis=1, tiled=True
        )
        grad_inner = jnp.einsum(
            "erd,edf->erf", grad_received, down_full, preferred_element_type=jnp.float32
        )
        grad_down = grad_down + jnp.einsum(
            "erd,erf->edf", grad_received, inner_low, preferred_element_type=jnp.float32
        )
        grad_gate_low = (grad_inner * up_act * sigma * (1.0 + gate_act * (1.0 - sigma))).astype(
            jnp.bfloat16
        )
        grad_up_low = (grad_inner * silu_act).astype(jnp.bfloat16)
        grad_gate = grad_gate + jnp.einsum(
            "erd,erf->edf", received, grad_gate_low, preferred_element_type=jnp.float32
        )
        grad_up = grad_up + jnp.einsum(
            "erd,erf->edf", received, grad_up_low, preferred_element_type=jnp.float32
        )
        grad_entry = (
            jnp.einsum("erf,edf->erd", grad_gate_low, gate_full, preferred_element_type=jnp.float32)
            + jnp.einsum("erf,edf->erd", grad_up_low, up_full, preferred_element_type=jnp.float32)
        ).astype(jnp.bfloat16)
        grad_back = lax.all_to_all(
            grad_entry, "experts", split_axis=1, concat_axis=0, tiled=True
        ).reshape(experts * capacity, model_width)
        grad_normed = grad_normed + jnp.sum(
            jnp.where(routed_ffn[:, None], grad_back[pick_index].astype(jnp.float32), 0.0).reshape(
                row_count, 2, model_width
            ),
            axis=1,
        )
        grad_hidden_norm, gain_term = norm_back(grad_normed, hidden, scale_second, gains[1])
        gain_second = gain_second + gain_term
        grad_hidden = grad_rows + grad_hidden_norm
        grad_attn_low = grad_hidden.astype(jnp.bfloat16)
        grad_out = grad_out + jnp.dot(attended.T, grad_attn_low, preferred_element_type=jnp.float32)
        grad_attended = (
            jnp.dot(grad_attn_low, out_full.T, preferred_element_type=jnp.float32)
            .astype(jnp.bfloat16)
            .reshape(head_shape)
        )
        delta = jnp.sum(grad_attended.astype(jnp.float32) * attn_heads, axis=-1).T
        zero_heads = jnp.zeros(head_shape, jnp.float32)
        key_all, value_all, segment_all = (
            lax.all_gather(rotated_keys, "context", axis=0, tiled=True),
            lax.all_gather(values, "context", axis=0, tiled=True),
            lax.all_gather(seg_rows, "context", axis=0, tiled=True),
        )
        total_keys = key_all.shape[0]
        group_count = math.gcd(total_keys // row_count, max(1, 512 // row_count))
        block_rows = row_count * group_count
        block_count = total_keys // block_rows

        def back_block(grad_query, block_parts):
            key_block, value_block, segment_block, block_start = block_parts
            key_positions = block_start + jnp.arange(block_rows, dtype=jnp.int32)
            scores, allowed = masked_scores(
                queries, key_block, seg_rows, segment_block, positions, key_positions, score_scale
            )
            probability = jnp.where(allowed[None], jnp.exp(scores - log_total[:, :, None]), 0.0)
            grad_prob = jnp.einsum(
                "qhd,khd->hqk", grad_attended, value_block, preferred_element_type=jnp.float32
            )
            grad_score = (probability * (grad_prob - delta[:, :, None])).astype(jnp.bfloat16)
            grad_query = (
                grad_query
                + jnp.einsum(
                    "hqk,khd->qhd", grad_score, key_block, preferred_element_type=jnp.float32
                )
                * score_scale
            )
            grad_key = (
                jnp.einsum("hqk,qhd->khd", grad_score, queries, preferred_element_type=jnp.float32)
                * score_scale
            )
            grad_value = jnp.einsum(
                "hqk,qhd->khd",
                probability.astype(jnp.bfloat16),
                grad_attended,
                preferred_element_type=jnp.float32,
            )
            return (grad_query, (grad_key, grad_value))

        block_starts = jnp.arange(block_count, dtype=jnp.int32) * block_rows
        grad_query, (key_terms, value_terms) = lax.scan(
            back_block,
            zero_heads,
            (
                key_all.reshape(block_count, block_rows, head_count, HEAD_DIM),
                value_all.reshape(block_count, block_rows, head_count, HEAD_DIM),
                segment_all.reshape(block_count, block_rows),
                block_starts,
            ),
        )
        grad_key, grad_value = (
            lax.psum_scatter(
                key_terms.reshape(total_keys, head_count, HEAD_DIM).astype(jnp.bfloat16),
                "context",
                scatter_dimension=0,
                tiled=True,
            ).astype(jnp.float32),
            lax.psum_scatter(
                value_terms.reshape(total_keys, head_count, HEAD_DIM).astype(jnp.bfloat16),
                "context",
                scatter_dimension=0,
                tiled=True,
            ).astype(jnp.float32),
        )
        grad_projected = jnp.stack(
            [
                rotate(grad_query, positions, -1.0).reshape(row_count, model_width),
                rotate(grad_key, positions, -1.0).reshape(row_count, model_width),
                grad_value.reshape(row_count, model_width),
            ]
        ).astype(jnp.bfloat16)
        grad_qkv = grad_qkv + jnp.einsum(
            "qd,cqe->cde", normed_in, grad_projected, preferred_element_type=jnp.float32
        )
        grad_normed_in = jnp.einsum(
            "cqe,cde->qd", grad_projected, qkv_full, preferred_element_type=jnp.float32
        )
        grad_token_norm, gain_term = norm_back(grad_normed_in, token_rows, scale_first, gains[0])
        gain_first = gain_first + gain_term
        input_rows.append(grad_hidden + grad_token_norm)
    grad_gain = jnp.stack([gain_first, gain_second])
    (
        grad_qkv,
        grad_out,
        grad_gain,
        grad_vec,
        grad_route,
        grad_mixer,
        grad_gate,
        grad_up,
        grad_down,
    ) = (
        lax.psum_scatter(
            grad_qkv.astype(jnp.bfloat16), ("context", "dp"), scatter_dimension=1, tiled=True
        ).astype(jnp.float32),
        lax.psum_scatter(
            grad_out.astype(jnp.bfloat16), ("context", "dp"), scatter_dimension=0, tiled=True
        ).astype(jnp.float32),
        lax.psum_scatter(
            grad_gain.astype(jnp.bfloat16), ("context", "dp"), scatter_dimension=1, tiled=True
        ).astype(jnp.float32),
        lax.psum_scatter(
            grad_vec.astype(jnp.bfloat16), ("context", "dp"), scatter_dimension=1, tiled=True
        ).astype(jnp.float32),
        lax.psum_scatter(
            grad_route.astype(jnp.bfloat16), ("context", "dp"), scatter_dimension=0, tiled=True
        ).astype(jnp.float32),
        lax.psum_scatter(
            grad_mixer.astype(jnp.bfloat16), ("context", "dp"), scatter_dimension=0, tiled=True
        ).astype(jnp.float32),
        lax.psum_scatter(
            grad_gate.astype(jnp.bfloat16), ("context", "dp"), scatter_dimension=2, tiled=True
        ).astype(jnp.float32),
        lax.psum_scatter(
            grad_up.astype(jnp.bfloat16), ("context", "dp"), scatter_dimension=2, tiled=True
        ).astype(jnp.float32),
        lax.psum_scatter(
            grad_down.astype(jnp.bfloat16), ("context", "dp"), scatter_dimension=2, tiled=True
        ).astype(jnp.float32),
    )
    grad_qkv, grad_out, grad_gain, grad_vec, grad_route, grad_mixer = (
        lax.psum(grad_qkv.astype(jnp.bfloat16), "experts").astype(jnp.float32),
        lax.psum(grad_out.astype(jnp.bfloat16), "experts").astype(jnp.float32),
        lax.psum(grad_gain.astype(jnp.bfloat16), "experts").astype(jnp.float32),
        lax.psum(grad_vec.astype(jnp.bfloat16), "experts").astype(jnp.float32),
        lax.psum(grad_route.astype(jnp.bfloat16), "experts").astype(jnp.float32),
        lax.psum(grad_mixer.astype(jnp.bfloat16), "experts").astype(jnp.float32),
    )
    output = jnp.stack(output_rows)[:, None]
    input_grad = jnp.stack(input_rows)[:, None]
    logit_grad = jnp.stack(logit_rows)[:, None]
    return (
        output,
        input_grad,
        logit_grad,
        grad_qkv,
        grad_out,
        grad_gain,
        grad_route,
        grad_mixer,
        grad_vec,
        grad_gate,
        grad_up,
        grad_down,
    )


BF = jnp.bfloat16
F32 = jnp.float32
BLOCK = 256
RING = 4
VMEM_BYTES = 60 * 2**20


def dot(left, right, left_dim, right_dim):
    return lax.dot_general(
        left, right, (((left_dim,), (right_dim,)), ((), ())), preferred_element_type=F32
    )


def iota(shape, dim):
    return lax.broadcasted_iota(jnp.int32, shape, dim)


def split3(values):
    high = values.astype(BF).astype(F32)
    rest = values - high
    middle = rest.astype(BF).astype(F32)
    return (high, middle, rest - middle)


def split2(values):
    high = values.astype(BF)
    return (high, (values - high.astype(F32)).astype(BF))


def rows_of(parts, count):
    width = parts[0].shape[1]
    index = iota((count, width), 0)
    total = jnp.zeros((count, width), F32)
    for place, part in enumerate(parts):
        total = jnp.where(index == place, jnp.broadcast_to(part, (count, width)), total)
    return total


def column_of(row, width=128):
    stacked = rows_of(split3(row), 16).astype(BF)
    return dot(stacked, jnp.ones((16, width), BF), 0, 0)


def wide(column, copies):
    return jnp.concatenate([column] * copies, axis=1)


def kernel_call(
    body, idx, args, outs, flops, grid=None, in_specs=None, out_specs=None, scratch=(), share=1
):
    moved = sum(a.size * a.dtype.itemsize for a in args)
    moved += sum(math.prod(s) * jnp.dtype(d).itemsize for s, d in outs)
    whole = pl.BlockSpec(memory_space=pltpu.VMEM)
    extra = {} if grid is None else {"grid": grid}
    return pl.pallas_call(
        body,
        out_shape=[jax.ShapeDtypeStruct(s, d) for s, d in outs],
        in_specs=[pl.BlockSpec(memory_space=pltpu.SMEM)]
        + (in_specs if in_specs is not None else [whole] * len(args)),
        out_specs=out_specs if out_specs is not None else [whole] * len(outs),
        scratch_shapes=list(scratch),
        compiler_params=pltpu.CompilerParams(vmem_limit_bytes=VMEM_BYTES),
        cost_estimate=pl.CostEstimate(
            flops=flops // share, bytes_accessed=moved // share, transcendentals=0
        ),
        **extra,
    )(idx, *args)


def rope_tables(length):
    half = HEAD_DIM // 2
    inverse = (10000.0 ** (-np.arange(half, dtype=np.float32) / half)).astype(np.float32)
    angles = (np.arange(length, dtype=np.float32)[:, None] * inverse[None, :]).astype(np.float64)
    cosine, sine = np.cos(angles), np.sin(angles)
    cosine = np.concatenate([cosine] * 4, axis=1).astype(np.float32)
    sine = np.concatenate([-sine, sine] * 2, axis=1).astype(np.float32)
    return cosine, sine


def turn(values, cosine, sine, direction):
    width = values.shape[1]
    copies = width // cosine.shape[1]
    ahead = pltpu.roll(values, width - HEAD_DIM // 2, 1)
    behind = pltpu.roll(values, HEAD_DIM // 2, 1)
    first = (iota(values.shape, 1) & (HEAD_DIM - 1)) < HEAD_DIM // 2
    partner = jnp.where(first, ahead, behind)
    return values * wide(cosine, copies) + direction * (partner * wide(sine, copies))


def project_kernel(idx, xa, xb, theirs, columns, w_ref, cosine, sine, *outs):
    q_ref, k_ref, v_ref, normed_ref, params_ref, seg_row, seg_col, x_ref = outs
    core, flip = idx[2], idx[3]
    row, column = iota((16, 128), 0), iota((16, 128), 1)
    spread = (row == column) | ((row >= 12) & ((column == row + 4) | (column == row + 8)))
    params_ref[...] = dot(jnp.where(spread, 1.0, 0.0).astype(BF), columns[...], 1, 1)
    sources = (
        (xa, core, 0),
        (xb, core, 1),
        (theirs.at[0], 1 - core, 0),
        (theirs.at[1], 1 - core, 1),
    )
    for ref, half, slot in sources:
        block = 2 * half + (flip if slot == 0 else 1 - flip)
        rows = pl.ds(pl.multiple_of(block * BLOCK, BLOCK), BLOCK)
        x_ref[rows, :] = ref[:BLOCK, :]
        segment = ref[ref.shape[0] - 16 :, :BLOCK].astype(F32)[10:11]
        seg_row[:, rows] = jnp.broadcast_to(segment, (8, BLOCK))
        seg_col[rows, :] = column_of(segment)
    gain = params_ref[14:15, :]
    tiles = [slice(i * BLOCK, (i + 1) * BLOCK) for i in range(x_ref.shape[0] // BLOCK)]
    for rows in tiles:
        x = x_ref[rows, :].astype(F32)
        normed_ref[rows, :] = (x * norm_scale(x) * gain).astype(BF)
    queries, keys, values = (dot(normed_ref[...], w_ref[j], 1, 0) for j in range(3))
    for rows in tiles:
        turned = turn(queries[rows], cosine[rows, :], sine[rows, :], 1.0)
        q_ref[rows, :] = (turned * HEAD_DIM**-0.5).astype(BF)
        k_ref[rows, :] = turn(keys[rows], cosine[rows, :], sine[rows, :], 1.0).astype(BF)
        v_ref[rows, :] = values[rows].astype(BF)


def mask_of(seg_row, seg_col, i):
    n = (i + 1) * BLOCK
    mine = seg_row[:1, i * BLOCK : n]
    key_index, query_index = iota((BLOCK, BLOCK), 0), iota((BLOCK, BLOCK), 1)
    last = (seg_col[i * BLOCK : n, :1] == mine) & (key_index <= query_index)
    bias = jnp.where(last, 0.0, MASKED)
    if i > 0:
        before = jnp.where(seg_col[: i * BLOCK, :1] == mine, 0.0, MASKED)
        bias = jnp.concatenate([before, bias], axis=0)
    return bias


def both_heads(values, low_lanes):
    return jnp.concatenate(
        [jnp.where(low_lanes, values, 0), jnp.where(low_lanes, 0, values)], axis=0
    )


def attend_kernel(idx, q_ref, k_ref, v_ref, seg_row, seg_col, keep_ref, send_ref, lse_ref):
    core, flip = idx[2], idx[3]
    low_lanes = iota((BLOCK, 2 * HEAD_DIM), 1) < HEAD_DIM
    results = []
    for i in range(q_ref.shape[0] // BLOCK):
        n = (i + 1) * BLOCK
        queries = q_ref[i * BLOCK : n, :]
        keys, values = k_ref[:n, :], v_ref[:n, :]
        bias = mask_of(seg_row, seg_col, i)
        both = both_heads(queries, low_lanes)
        scores = dot(keys, both, 1, 1) + wide(bias, 2)
        peak = jnp.max(scores, axis=0, keepdims=True)
        weights = jnp.exp(scores - peak)
        total = jnp.sum(weights, axis=0, keepdims=True)
        out = dot(values, weights.astype(BF), 0, 0)
        lse = peak + jnp.log(total)
        out = out / total
        out = jnp.concatenate([out[:HEAD_DIM, :BLOCK], out[HEAD_DIM:, BLOCK:]], axis=0)
        lse_ref[0, 0:1, i * BLOCK : n] = lse[:, :BLOCK]
        lse_ref[0, 1:2, i * BLOCK : n] = lse[:, BLOCK:]
        half, slot = i // 2, (i % 2) ^ flip
        results.append((half, slot, out.T.astype(BF)))
    for half, slot, attended in results:
        rows = pl.ds(pl.multiple_of(slot * BLOCK, BLOCK), BLOCK)

        @pl.when(half == core)
        def _(attended=attended, rows=rows):
            keep_ref[rows, :] = attended

        @pl.when(half != core)
        def _(attended=attended, rows=rows):
            send_ref[rows, :] = attended


def pair_back_kernel(
    first, idx, q_ref, k_ref, v_ref, own_ref, other_ref, seg_row, seg_col, lse_ref, cosine, sine,
    normed_ref, og_ref, og_recv, *refs,
):
    if first:
        small_ref, grads_ref, shared, key_sum, value_sum = refs
    else:
        grads_ref, shared, key_sum, value_sum = refs
    core, flip = idx[2], idx[3]
    lanes = 2 * HEAD_DIM
    low_lanes = iota((BLOCK, lanes), 1) < HEAD_DIM
    key_sum[...] = jnp.zeros(key_sum.shape, F32)
    value_sum[...] = jnp.zeros(value_sum.shape, F32)
    for i in range(q_ref.shape[0] // BLOCK):
        n = (i + 1) * BLOCK
        keys, values = k_ref[:n, :], v_ref[:n, :]
        half, slot = i // 2, (i % 2) ^ flip
        rows = pl.ds(pl.multiple_of(slot * BLOCK, BLOCK), BLOCK)
        grads = jnp.where(half == core, own_ref[rows, :], other_ref[rows, :])
        queries = both_heads(q_ref[i * BLOCK : n, :], low_lanes)
        grads = both_heads(grads, low_lanes)
        bias = mask_of(seg_row, seg_col, i)
        lse = jnp.concatenate([lse_ref[0, 0:1, i * BLOCK : n], lse_ref[0, 1:2, i * BLOCK : n]], 1)
        weights = jnp.exp(dot(keys, queries, 1, 1) + wide(bias, 2) - lse)
        grad_weights = dot(values, grads, 1, 1)
        delta = jnp.sum(weights * grad_weights, axis=0, keepdims=True)
        grad_scores = (weights * (grad_weights - delta)).astype(BF)
        key_sum[:n, :] += dot(grad_scores, queries, 1, 0)
        value_sum[:n, :] += dot(weights.astype(BF), grads, 1, 0)
        grad_query = dot(grad_scores, keys, 0, 0)
        grad_query = jnp.where(low_lanes, grad_query[:BLOCK], grad_query[BLOCK:]) * HEAD_DIM**-0.5
        tile = slice(i * BLOCK, n)
        turned = turn(grad_query, cosine[tile, :], sine[tile, :], -1.0)
        grads_ref[tile, :lanes] = turned.astype(BF)
    for i in range(q_ref.shape[0] // BLOCK):
        tile = slice(i * BLOCK, (i + 1) * BLOCK)
        turned = turn(key_sum[tile, :], cosine[tile, :], sine[tile, :], -1.0)
        grads_ref[tile, lanes : 2 * lanes] = turned.astype(BF)
        grads_ref[tile, 2 * lanes :] = value_sum[tile, :].astype(BF)
    model = normed_ref.shape[1]
    depth = model // RING
    weight_grads = dot(normed_ref[...], grads_ref[...], 0, 0)
    out_grads = og_ref[...].astype(F32) + og_recv[...].astype(F32)
    for z in range(RING):
        rows = slice(z * depth, (z + 1) * depth)
        for j in range(3):
            piece = weight_grads[rows, j * lanes : (j + 1) * lanes]
            shared[j, z, :depth, :] = piece.astype(BF)
        shared[3, z, :depth, :] = out_grads[rows].astype(BF)
        if first:
            shard = depth // 2
            for j in range(2):
                lane = iota((model, lanes), 1)
                pick = iota((model, lanes), 0) == lane + (z * depth + j * shard)
                pick = jnp.where(pick & (lane < shard), 1.0, 0.0).astype(BF)
                picked = dot(small_ref[...].astype(BF), pick, 1, 0)
                shared[j, z, depth:, :] = picked.astype(BF)
            for j in range(2, RING):
                shared[j, z, depth:, :] = jnp.zeros((16, lanes), BF)


def routed_rows(small, routed):
    index = iota((routed, small.shape[1]), 0).astype(F32)
    return jnp.where((small[8:9, :] == index) | (small[9:10, :] == index), 1.0, 0.0)


def ranks_of(named):
    tokens = named.shape[1]
    before, here = iota((tokens, tokens), 0), iota((tokens, tokens), 1)
    earlier = (before < here) & (before // BLOCK == here // BLOCK)
    stacked = jnp.concatenate([named, jnp.zeros_like(named)], axis=0).astype(BF)
    return dot(stacked, jnp.where(earlier, 1.0, 0.0).astype(BF), 1, 0)[: named.shape[0]]


def pick_row(values, index):
    return jnp.sum(jnp.where(iota(values.shape, 0) == index, values, 0.0), axis=0, keepdims=True)


def slots_of(named, rank, expert, capacity):
    tokens = named.shape[1]
    place = pick_row(rank, expert)
    place = place + jnp.where(iota((1, tokens), 1) >= BLOCK, float(capacity), 0.0)
    slot = iota((2 * capacity, tokens), 0).astype(F32)
    taken = (slot == place) & (pick_row(named, expert) > 0.5)
    return jnp.where(taken, 1.0, 0.0).astype(BF)


def pair_of(first, second):
    return jnp.concatenate([first[:BLOCK, :], second[:BLOCK, :]], axis=0)


def small_of(xa, xb):
    blocks = []
    for packed in (xa, xb):
        values = packed[BLOCK:, :].astype(F32)
        width = values.shape[1] // 3
        logits = values[:8, :width] + values[:8, width : 2 * width] + values[:8, 2 * width :]
        blocks.append(jnp.concatenate([logits, values[8:, :width]], axis=0))
    return jnp.concatenate(blocks, axis=1)


def grad_slots_kernel(idx, xa, xb, ca, cb, out):
    named = routed_rows(small_of(xa, xb), 8)
    rank = ranks_of(named)
    grads = pair_of(ca, cb)
    for expert in range(out.shape[0]):
        taken = slots_of(named, rank, expert, out.shape[1] // 2)
        out[expert] = dot(taken, grads, 1, 0).astype(BF)


def route_kernel(idx, keep, recv, xa, xb, params, mine, theirs, *refs):
    (hidden_ref, ow_ref, state_ref), outs = refs[:3], refs[3:]
    core = idx[2]
    width = keep.shape[1]
    own = pl.ds(pl.multiple_of(core * width, 128), width)
    other = pl.ds(pl.multiple_of((1 - core) * width, 128), width)
    ow_ref[:, own] = mine[...]
    ow_ref[:, other] = theirs[...]
    hidden = (
        pair_of(xa, xb).astype(F32)
        + dot(keep[...], ow_ref[own, :], 1, 0)
        + dot(recv[...], ow_ref[other, :], 1, 0)
    )
    hidden_ref[...] = hidden
    normed = (hidden * norm_scale(hidden) * params[15:16, :]).astype(BF)
    small = small_of(xa, xb)
    logits = dot(params[...].astype(BF), normed, 1, 1)
    named = routed_rows(small, 8)
    rank = ranks_of(named)
    shifted = logits[:8] + small[:8]
    shifted = jnp.exp(shifted - jnp.max(shifted, axis=0, keepdims=True))
    probabilities = shifted / jnp.sum(shifted, axis=0, keepdims=True)
    mixed = []
    for c in range(2):
        first, second = logits[8 + 2 * c : 9 + 2 * c], logits[9 + 2 * c : 10 + 2 * c]
        peak = jnp.maximum(first, second)
        first, second = jnp.exp(first - peak), jnp.exp(second - peak)
        mixed += [first / (first + second), second / (first + second)]
    state_ref[0:8, :] = probabilities
    state_ref[8:16, :] = rows_of(mixed, 8)
    state_ref[16:24, :] = rank
    slots = outs[0].shape[0] - 16
    for k, out in enumerate(outs):
        expert = idx[0] ^ k
        taken = slots_of(named, rank, expert, slots // 2)
        out[:slots, :] = dot(taken, normed, 1, 0).astype(BF)
        gates = rows_of(split3(pick_row(probabilities, expert)), 16).astype(BF)
        out[slots:, :] = jnp.zeros((16, out.shape[1]), BF)
        out[slots:, :slots] = dot(gates, taken, 1, 1).astype(BF)


def expert_kernel(idx, g_own, g_other, weights, *refs):
    pieces, refs = refs[:8], refs[8:]
    lefts, acts, keep, send = refs[:4]
    g_all, scale_all, products, joined, joined_w, entry_sum, dot_sum = refs[4:]
    core = idx[2]
    j = pl.program_id(0)
    slots = g_own.shape[1]
    count, model = g_all.shape
    lanes = dot_sum.shape[1]
    chunk = weights.shape[3]

    @pl.when(j == 0)
    def _():
        for p in range(8):
            grads = (g_own if p < RING else g_other)[idx[0] ^ (p % RING)]
            rows = slice(p * slots, (p + 1) * slots)
            lefts[0, rows, :] = pieces[p][:slots, :]
            scale = dot(pieces[p][slots:, :slots], jnp.ones((16, lanes), BF), 0, 0)
            scale_all[rows, :] = scale
            g_all[rows, :] = grads
            scaled = grads.astype(F32) * wide(scale, model // lanes)
            lefts[1, rows, :] = scaled.astype(BF)
        dot_sum[...] = jnp.zeros(dot_sum.shape, F32)
        entry_sum[...] = jnp.zeros(entry_sum.shape, F32)

    joined_w[:, :chunk] = weights[0, 0]
    joined_w[:, chunk:] = weights[0, 1]
    products[:, : 2 * chunk] = dot(lefts[0], joined_w[...], 1, 0)
    products[:, 2 * chunk :] = dot(g_all[...], weights[0, 2], 1, 0)
    tile = 64
    for i in range(count // tile):
        rows = slice(i * tile, (i + 1) * tile)
        gate, up, back = (products[rows, p * chunk : (p + 1) * chunk] for p in range(3))
        sigma = 0.5 * jnp.tanh(0.5 * gate) + 0.5
        silu = gate * sigma
        inner = silu * up
        acts[2, rows, :] = inner.astype(BF)
        product = inner * back
        dot_sum[rows, :] += product[:, :lanes] + product[:, lanes:]
        back = back * wide(scale_all[rows, :], chunk // lanes)
        grad_gate = (back * up * (sigma + silu - silu * sigma)).astype(BF)
        grad_up = (back * silu).astype(BF)
        acts[0, rows, :] = grad_gate
        acts[1, rows, :] = grad_up
        joined[rows, :chunk] = grad_gate
        joined[rows, chunk:] = grad_up
    entry_sum[...] += dot(joined[...], joined_w[...], 1, 1)

    @pl.when(j == pl.num_programs(0) - 1)
    def _():
        ones = jnp.ones((16, lanes), BF)
        index = iota((16, slots), 0)
        for p in range(8):
            rows = slice(p * slots, (p + 1) * slots)
            high, low = split2(dot_sum[rows, :])
            high, middle, rest = split3(dot(ones, high, 1, 1) + dot(ones, low, 1, 1))
            packed = jnp.where(
                index == 4 * core,
                high,
                jnp.where(
                    index == 4 * core + 1, middle, jnp.where(index == 4 * core + 2, rest, 0.0)
                ),
            )
            out = (keep if p < RING else send).at[idx[0] ^ (p % RING)]
            out[:slots, :] = entry_sum[rows, :].astype(BF)
            out[slots:, :] = jnp.zeros((16, model), BF)
            out[slots:, :slots] = packed.astype(BF)


def expert_out_kernel(idx, inner_ref, weights, keep, send, down):
    slots = keep.shape[1]
    chunk = weights.shape[3]
    for k in range(RING):
        down[:, k * chunk : (k + 1) * chunk] = weights[k, 0]
    out = dot(inner_ref[0], down[...], 1, 1).astype(BF)
    for p in range(8):
        place = idx[0] ^ (p % RING)
        (keep if p < RING else send)[place] = out[p * slots : (p + 1) * slots]


def expert_grads_kernel(idx, left, right, out):
    chunk = out.shape[3]
    grad = dot(left[0], right[0], 0, 0).astype(BF)
    for k in range(out.shape[0]):
        out[k, 0] = grad[:, k * chunk : (k + 1) * chunk]


def slot_table(small, state, capacity):
    named = routed_rows(small, 8)
    rank = state[16:24, :]
    return [slots_of(named, rank, expert, capacity) for expert in range(RING)], named


def branch_weights(state, named):
    gates = state[0:8, :] * named
    consts = [gates[6 + c : 7 + c] for c in range(2)]
    normed_weight = gates[5:6]
    for c in range(2):
        normed_weight = normed_weight + consts[c] * state[8 + 2 * c : 9 + 2 * c, :]
    vector_weights = [consts[c] * state[9 + 2 * c : 10 + 2 * c, :] for c in range(2)]
    return consts, normed_weight, vector_weights


def output_kernel(idx, hidden_ref, state_ref, xa, xb, params, returned, logits_ref, oa, ob):
    state = state_ref[...]
    tables, named = slot_table(small_of(xa, xb), state, returned.shape[1] // 2)
    hidden = hidden_ref[...]
    normed = hidden * norm_scale(hidden) * params[15:16, :]
    _, normed_weight, vector_weights = branch_weights(state, named)
    output = hidden + wide(column_of(normed_weight), normed.shape[1] // 128) * normed
    vector_rows = rows_of(split3(params[12:13, :])[:2] * 2 + split3(params[13:14, :])[:2] * 2, 16)
    first, second = split3(vector_weights[0])[:2], split3(vector_weights[1])[:2]
    weight_rows = rows_of(
        (first[0], first[0], first[1], first[1], second[0], second[0], second[1], second[1]), 16
    )
    output += dot(weight_rows.astype(BF), vector_rows.astype(BF), 0, 0)
    for k in range(RING):
        gate = state[k : k + 1, :]
        high, low, _ = split3(gate)
        table = tables[k].astype(F32)
        output += dot((table * high).astype(BF), returned[k], 0, 0)
        output += dot((table * low).astype(BF), returned[k], 0, 0)
    for slot, out in enumerate((oa, ob)):
        out[:BLOCK, :] = output[slot * BLOCK : (slot + 1) * BLOCK].astype(BF)
        parts = split3(logits_ref[:, slot * BLOCK : (slot + 1) * BLOCK])
        parts = jnp.concatenate(parts, axis=1)
        out[BLOCK:, :] = jnp.concatenate([parts, jnp.zeros_like(parts)], axis=0).astype(BF)


def hidden_back_kernel(
    idx, hidden_ref, state_ref, xa, xb, ca, cb, params, ow_ref, returned, *outs
):
    gh_ref, low_ref, own_ref, send_ref, logits_ref, small_ref = outs
    core = idx[2]
    state = state_ref[...]
    slots = returned.shape[1] - 16
    tables, named = slot_table(small_of(xa, xb), state, slots // 2)
    probabilities = state[0:8, :]
    hidden = hidden_ref[...]
    factor = norm_scale(hidden)
    scaled_hidden = hidden * factor
    normed = scaled_hidden * params[15:16, :]
    normed_low = normed.astype(BF)
    grads_low = pair_of(ca, cb)
    grads = grads_low.astype(F32)
    ones = jnp.ones((16, hidden.shape[1]), BF)
    high, low = split2(grads * normed)
    on_normed = (dot(ones, high, 1, 1) + dot(ones, low, 1, 1))[0:1]
    first, second = split3(params[12:13, :])[:2], split3(params[13:14, :])[:2]
    on_vectors = dot(rows_of(first + second, 16).astype(BF), grads_low, 1, 1)
    on_vector = (on_vectors[0:1] + on_vectors[1:2], on_vectors[2:3] + on_vectors[3:4])
    consts, normed_weight, vector_weights = branch_weights(state, named)
    index = iota(probabilities.shape, 0)
    grad_probs = jnp.where(index == 5, on_normed, 0.0)
    mix_rows = []
    for c in range(2):
        mix_first, mix_second = state[8 + 2 * c : 9 + 2 * c, :], state[9 + 2 * c : 10 + 2 * c, :]
        dot_c = mix_first * on_normed + mix_second * on_vector[c]
        grad_probs = jnp.where(index == 6 + c, dot_c, grad_probs)
        grad_first, grad_second = consts[c] * on_normed, consts[c] * on_vector[c]
        mean = mix_first * grad_first + mix_second * grad_second
        mix_rows += [mix_first * (grad_first - mean), mix_second * (grad_second - mean)]
    back = jnp.zeros(hidden.shape, F32)
    for k in range(RING):
        packed = returned[k, slots:, :slots]
        found = jnp.sum(dot(packed, tables[k], 1, 0), axis=0, keepdims=True)
        grad_probs = jnp.where(index == k, found, grad_probs)
        back += dot(tables[k], returned[k, :slots, :], 0, 0)
    grad_probs = grad_probs * named
    grad_logits = probabilities * (
        grad_probs - jnp.sum(probabilities * grad_probs, axis=0, keepdims=True)
    )
    logits_ref[...] = grad_logits
    router_rows = jnp.concatenate([grad_logits, rows_of(mix_rows, 8)], axis=0)
    rows_high, rows_low = split2(router_rows)
    weights_low = params[...].astype(BF)
    grad_normed = (
        back
        + dot(rows_high, weights_low, 0, 0)
        + dot(rows_low, weights_low, 0, 0)
        + wide(column_of(normed_weight), hidden.shape[1] // 128) * grads
    )
    router_grad = dot(rows_high, normed_low, 1, 0) + dot(rows_low, normed_low, 1, 0)
    first, second = split3(vector_weights[0])[:2], split3(vector_weights[1])[:2]
    vector_grad = dot(rows_of(first + second, 16).astype(BF), grads_low, 1, 0)
    gain_grad = jnp.sum(grad_normed * scaled_hidden, axis=0, keepdims=True)
    small_ref[...] = jnp.where(
        iota(router_grad.shape, 0) < 12,
        router_grad,
        rows_of(
            [jnp.zeros_like(gain_grad)] * 12
            + [vector_grad[0:1] + vector_grad[1:2], vector_grad[2:3] + vector_grad[3:4], gain_grad],
            16,
        ),
    )
    scaled = grad_normed * params[15:16, :]
    mean = jnp.mean(scaled * hidden, axis=-1, keepdims=True)
    grad_hidden = grads + factor * scaled - hidden * (factor * factor * factor * mean)
    gh_ref[...] = grad_hidden
    grad_low = grad_hidden.astype(BF)
    low_ref[...] = grad_low
    width = own_ref.shape[1]
    own_rows = pl.ds(pl.multiple_of(core * width, 16), width)
    other_rows = pl.ds(pl.multiple_of((1 - core) * width, 16), width)
    own_ref[...] = dot(grad_low, ow_ref[own_rows, :], 1, 1).astype(BF)
    send_ref[...] = dot(grad_low, ow_ref[other_rows, :], 1, 1).astype(BF)


def out_grad_kernel(idx, keep, recv, low_ref, own_ref, send_ref):
    core = idx[2]
    width = keep.shape[1]
    own = pl.ds(pl.multiple_of(core * width, 128), width)
    other = pl.ds(pl.multiple_of((1 - core) * width, 128), width)
    for out, columns in ((own_ref, own), (send_ref, other)):
        grads = low_ref[:, columns]
        out[own, :] = dot(keep[...], grads, 0, 0).astype(BF)
        out[other, :] = dot(recv[...], grads, 0, 0).astype(BF)


def normed_back_kernel(idx, *refs):
    pair_grads, w_ref, keep_ref, send_ref, grads, weights = refs[:3], *refs[3:]
    core, flip = idx[2], idx[3]
    lanes = 2 * HEAD_DIM
    for h, ref in enumerate(pair_grads):
        columns = slice(h * 3 * lanes, (h + 1) * 3 * lanes)
        grads[:, columns] = ref[...]
        for j in range(3):
            place = (3 * h + j) * lanes
            weights[:, place : place + lanes] = w_ref[j, :, h * lanes : (h + 1) * lanes]
    total = dot(grads[...], weights[...], 1, 1).astype(BF)
    for half in range(2):
        for out, there in ((keep_ref, half == core), (send_ref, half != core)):

            @pl.when(there)
            def _(half=half, out=out):
                for part in range(2):
                    place = 2 * half + part
                    rows = pl.ds(pl.multiple_of((part ^ flip) * BLOCK, BLOCK), BLOCK)
                    out[rows, :] = total[place * BLOCK : (place + 1) * BLOCK]


def input_back_kernel(idx, keep_ref, recv_ref, gh_ref, xa, xb, params, oa, ob):
    gain = params[14:15, :]
    for slot, (x_ref, out) in enumerate(((xa, oa), (xb, ob))):
        tile = slice(slot * BLOCK, (slot + 1) * BLOCK)
        x = x_ref[:BLOCK, :].astype(F32)
        factor = norm_scale(x)
        scaled = (keep_ref[tile, :].astype(F32) + recv_ref[tile, :].astype(F32)) * gain
        mean = jnp.mean(scaled * x, axis=-1, keepdims=True)
        out[...] = (
            gh_ref[tile, :] + factor * scaled - x * (factor * factor * factor * mean)
        ).astype(BF)


def across(values):
    return lax.ppermute(values, "dp", [(0, 1), (1, 0)])


def over(values, k):
    return lax.ppermute(values, "experts", [(i, i ^ k) for i in range(RING)])


def exchange(values, axis):
    return lax.all_to_all(values, axis, 0, 0, tiled=True)


def after(values, *others):
    return lax.optimization_barrier((values, others))[0]


def handed_to_all(values, axis):
    return exchange(jnp.broadcast_to(values[None], (RING, *values.shape)), axis)


def chip_local(
    inputs, cotangent, qkv_weight, out_weight, norm_gains, route_weight, const_gate, const_vec,
    w_gate, w_up, w_down, prev_logits, routes, segments,
):
    e, z, core = lax.axis_index("experts"), lax.axis_index("context"), lax.axis_index("dp")
    flip = z // 2
    idx = jnp.stack([e, z, core, flip]).astype(jnp.int32)
    odd = lax.rem(z, 2)
    rows, model = inputs.shape[2], inputs.shape[3]
    length = rows * RING
    half_model = model // 2
    slots = 2 * (rows * 5 // 16)

    def place(z_index, d, which):
        micro = z_index % 2 if which == 0 else 1 - z_index % 2
        return (2 * micro + d) * 2 + z_index // 2

    routes_of = [
        [(zi * 2 + d, place(zi, d, which)) for zi in range(RING) for d in range(2)]
        for which in range(2)
    ]

    def leave(values):
        return [
            lax.ppermute(
                lax.dynamic_index_in_dim(values, odd if which == 0 else 1 - odd, 0, False),
                ("context", "dp"),
                routes_of[which],
            )
            for which in range(2)
        ]

    def go_home(values, which):
        return lax.ppermute(values, ("context", "dp"), [(b, a) for a, b in routes_of[which]])

    def at_home(*got):
        return jnp.where(odd == 0, jnp.stack(got), jnp.stack(got[::-1]))

    def columns_of(values, side):
        return lax.dynamic_slice_in_dim(values, side * half_model, half_model, values.ndim - 1)

    def in_order(mine, theirs, axis):
        pair = jnp.stack([mine, theirs], axis=axis), jnp.stack([theirs, mine], axis=axis)
        return jnp.where(core == 0, *pair)

    vectors = split3(jnp.concatenate([const_vec, norm_gains], axis=0).T)
    columns = jnp.concatenate(
        [route_weight, const_gate, *(part.astype(BF) for part in vectors)], axis=1
    )
    columns = jnp.pad(columns, ((0, 0), (0, 128 - columns.shape[1])))
    matrix = lax.dynamic_index_in_dim(qkv_weight, jnp.minimum(e, 2), 0, False)
    matrix = jnp.where(e == 3, out_weight, matrix)
    ring = handed_to_all(jnp.concatenate([matrix, columns], axis=1), "context")
    logit_parts = jnp.concatenate(split3(jnp.swapaxes(prev_logits[:, 0], 1, 2)), axis=2)
    ids = jnp.concatenate([jnp.swapaxes(routes[:, 0], 1, 2), segments], axis=1).astype(F32)
    ids = jnp.pad(ids, ((0, 0), (0, 5), (0, 2 * rows)))
    xa, xb = leave(
        jnp.concatenate([inputs[:, 0], logit_parts.astype(BF), ids.astype(BF)], axis=1)
    )
    ring, xa, xb = lax.optimization_barrier((ring, xa, xb))

    def my_part(side):
        return jnp.concatenate([columns_of(ring[:, :, :model], side), ring[:, :, model:]], axis=2)

    shared = in_order(my_part(core), across(my_part(1 - core)), 1)
    shared = shared.reshape(model, half_model + 128)
    columns = shared[:, half_model:]
    w_all = handed_to_all(shared[:, :half_model], "experts")
    theirs = across(jnp.stack([xa, xb]))

    stacked = jnp.stack([w_gate[0], w_up[0], w_down[0]])
    expert_w = lax.all_gather(after(stacked, ring), "context", axis=0)
    ca, cb = leave(after(cotangent[:, 0], shared))

    cosine, sine = (jnp.asarray(t) for t in rope_tables(length))
    q, k, v, normed_in, params, seg_row, seg_col = kernel_call(
        project_kernel,
        idx,
        [xa, xb, theirs, columns, w_all, cosine, sine],
        [((length, half_model), BF)] * 3
        + [((length, model), BF)]
        + [((16, model), F32), ((8, length), F32), ((length, 128), F32)],
        flops=2 * length * model * 3 * half_model,
        share=100,
        scratch=[pltpu.VMEM((length, model), BF)],
    )
    pairs = half_model // (2 * HEAD_DIM)
    lanes = 2 * HEAD_DIM
    by_pair = pl.BlockSpec((length, lanes), lambda h: (0, h))
    half_by_pair = pl.BlockSpec((length // 2, lanes), lambda h: (0, h))
    all_of = pl.BlockSpec(memory_space=pltpu.VMEM)
    lse_spec = pl.BlockSpec((1, 8, length), lambda h: (h, 0, 0))
    keep, send, lse = kernel_call(
        attend_kernel,
        idx,
        [q, k, v, seg_row, seg_col],
        [((length // 2, half_model), BF)] * 2 + [((pairs, 8, length), F32)],
        flops=4 * length * length * half_model,
        share=100,
        grid=(pairs,),
        in_specs=[by_pair] * 3 + [all_of] * 2,
        out_specs=[half_by_pair] * 2 + [lse_spec],
    )
    ca, cb = after((ca, cb), keep)
    (g_slots,) = kernel_call(
        grad_slots_kernel,
        idx,
        [xa, xb, ca, cb],
        [((RING, slots, model), BF)],
        flops=2 * RING * slots * 2 * rows * model,
    )
    g_mine = exchange(g_slots, "experts")
    recv = after(across(send), g_slots)

    hidden, ow_all, state, *sent = kernel_call(
        route_kernel,
        idx,
        [keep, recv, xa, xb, params, w_all[3], across(w_all[3])],
        [((2 * rows, model), F32), ((model, model), BF), ((24, 2 * rows), F32)]
        + [((slots + 16, model), BF)] * RING,
        flops=2 * 2 * rows * model * model + 2 * RING * slots * 2 * rows * model,
    )
    t_mine = [sent[0]] + [over(after(sent[k], g_mine), k) for k in range(1, RING)]
    g_theirs = across(g_mine)
    t_theirs = [across(t) for t in t_mine]

    count = 8 * slots
    chunk = w_gate.shape[2]
    hidden_units = RING * chunk
    lefts, acts, entry_keep, entry_send = kernel_call(
        expert_kernel,
        idx,
        [g_mine, g_theirs, expert_w, *t_mine, *t_theirs],
        [((2, count, model), BF), ((3, count, hidden_units), BF)]
        + [((RING, slots + 16, model), BF)] * 2,
        flops=10 * count * model * hidden_units,
        grid=(RING,),
        in_specs=[all_of] * 2
        + [pl.BlockSpec((1, 3, model, chunk), lambda j: (j, 0, 0, 0))]
        + [all_of] * 8,
        out_specs=[all_of, pl.BlockSpec((3, count, chunk), lambda j: (0, 0, j))] + [all_of] * 2,
        scratch=[
            pltpu.VMEM((count, model), BF),
            pltpu.VMEM((count, 128), F32),
            pltpu.VMEM((count, 3 * chunk), F32),
            pltpu.VMEM((count, 2 * chunk), BF),
            pltpu.VMEM((model, 2 * chunk), BF),
            pltpu.VMEM((count, model), F32),
            pltpu.VMEM((count, 128), F32),
        ],
    )

    def both_cores(kept, received):
        return (kept.astype(F32) + received.astype(F32)).astype(BF)

    entry_sum = both_cores(entry_keep, across(entry_send))
    entry_back = exchange(entry_sum, "experts")
    (far_grads,) = kernel_call(
        expert_grads_kernel,
        idx,
        [after(lefts, entry_sum), acts],
        [((RING, 3, model, chunk), BF)],
        flops=6 * count * model * hidden_units,
        grid=(3,),
        in_specs=[
            pl.BlockSpec((1, count, model), lambda j: (j // 2, 0, 0)),
            pl.BlockSpec((1, count, hidden_units), lambda j: (j, 0, 0)),
        ],
        out_specs=[pl.BlockSpec((RING, 1, model, chunk), lambda j: (0, j, 0, 0))],
    )
    out_keep, out_send = kernel_call(
        expert_out_kernel,
        idx,
        [after(acts, far_grads), expert_w],
        [((RING, slots, model), BF)] * 2,
        flops=2 * count * model * hidden_units,
        grid=(1,),
        in_specs=[
            pl.BlockSpec((1, count, hidden_units), lambda j: (2, 0, 0)),
            pl.BlockSpec((RING, 1, model, chunk), lambda j: (0, 2, 0, 0)),
        ],
        out_specs=[all_of] * 2,
        scratch=[pltpu.VMEM((model, hidden_units), BF)],
    )
    entry_back, out_send, far_grads = lax.optimization_barrier(
        (entry_back, out_send, far_grads)
    )
    expert_grads = lax.psum_scatter(far_grads, "context", scatter_dimension=0)

    grad_hidden, grad_low, ga_own, ga_send, logit_rows, small_grad = kernel_call(
        hidden_back_kernel,
        idx,
        [hidden, state, xa, xb, ca, cb, params, ow_all, entry_back],
        [((2 * rows, model), F32), ((2 * rows, model), BF)]
        + [((2 * rows, half_model), BF)] * 2
        + [((8, 2 * rows), F32), ((16, model), F32)],
        flops=2 * 2 * rows * model * model + 2 * RING * slots * 2 * rows * model,
    )
    ga_other = across(ga_send)
    out_sum = both_cores(out_keep, after(across(out_send), ga_send))
    out_back = exchange(out_sum, "experts")
    og_own, og_send = kernel_call(
        out_grad_kernel,
        idx,
        [keep, recv, grad_low],
        [((model, half_model), BF)] * 2,
        flops=2 * 2 * rows * model * model,
    )
    og_other = across(og_send)
    q = after(q, out_sum)
    shared_parts, pair_grads = [], []
    for h in range(pairs):
        at = lambda n, h=h: pl.BlockSpec((n, lanes), lambda i: (0, h))
        extra = 16 if h == 0 else 0
        grads, part = kernel_call(
            functools.partial(pair_back_kernel, h == 0),
            idx,
            [q, k, v, ga_own, ga_other, seg_row, seg_col, lse, cosine, sine, normed_in]
            + [og_own, og_other]
            + ([small_grad] if h == 0 else []),
            [((length, 3 * lanes), BF), ((RING, RING, model // RING + extra, lanes), BF)],
            flops=10 * length * length * lanes + 6 * length * model * lanes,
            grid=(1,),
            in_specs=[at(length)] * 3
            + [at(length // 2)] * 2
            + [all_of] * 2
            + [pl.BlockSpec((1, 8, length), lambda i, h=h: (h, 0, 0))]
            + [all_of] * 3
            + [at(model)] * 2
            + ([all_of] if h == 0 else []),
            out_specs=[all_of] * 2,
            scratch=[pltpu.VMEM((length, lanes), F32)] * 2,
        )
        pair_grads.append(grads)
        shared_parts.append(exchange(part, "experts"))
        if h == 0:
            q = after(q, out_back)
        if h == 1:
            q = after(q, shared_parts[0])
        if h == 2:
            w_all = after(w_all, shared_parts[1])
    depth = model // RING
    gn_keep, gn_send = kernel_call(
        normed_back_kernel,
        idx,
        [*pair_grads, w_all],
        [((2 * rows, model), BF)] * 2,
        flops=2 * length * model * 3 * half_model,
        scratch=[pltpu.VMEM((length, 3 * half_model), BF), pltpu.VMEM((model, 3 * half_model), BF)],
    )

    ia, ib = kernel_call(
        input_back_kernel,
        idx,
        [gn_keep, across(gn_send), grad_hidden, xa, xb, params],
        [((rows, model), BF)] * 2,
        flops=0,
    )
    oa, ob = kernel_call(
        output_kernel,
        idx,
        [after(hidden, ia), state, xa, xb, params, out_back, logit_rows],
        [((rows + 16, model), BF)] * 2,
        flops=4 * RING * slots * 2 * rows * model,
    )
    home = at_home(go_home(oa, 0), go_home(ob, 1))
    output = home[:, None, :rows]
    logit_grad = home[:, rows : rows + 8].astype(F32).reshape(2, 8, 3, rows).sum(axis=2)
    logit_grad = jnp.swapaxes(logit_grad, 1, 2)[:, None]
    shared_parts[2] = after(shared_parts[2], ia, oa)
    sums = [part.astype(F32).sum(axis=0).astype(BF) for part in shared_parts]
    parts = jnp.concatenate([part[:, :depth] for part in sums], axis=2)
    rest = jnp.pad(sums[0][:, depth:], ((0, 0), (0, 0), (0, half_model - lanes)))
    parts = jnp.concatenate([parts, rest], axis=1)
    ia, ib = go_home(ia, 0), go_home(ib, 1)
    input_grad = at_home(ia, ib).astype(F32)[:, None]
    parts = after(exchange(parts, "context"), ia, ib).astype(F32).sum(axis=0)
    shard = depth // 2
    rest = parts[depth:]
    given = jnp.concatenate(
        [lax.dynamic_slice_in_dim(parts, (1 - core) * shard, shard, 0), rest], axis=0
    )
    taken = across(given.astype(BF)).astype(F32)
    grads = in_order(lax.dynamic_slice_in_dim(parts, core * shard, shard, 0), taken[:shard], 1)
    rest = jnp.pad(rest + taken[shard:], ((0, 0), (0, half_model)))
    grads = jnp.concatenate([grads.reshape(shard, model), rest], axis=0).astype(BF)
    expert_grads = [expert_grads[i].astype(F32)[None] for i in range(3)]
    grads, expert_grads = lax.optimization_barrier((grads, expert_grads))
    grads = handed_to_all(grads, "experts").astype(F32)
    small_grad = lax.dynamic_index_in_dim(grads, core, 0, False)[shard:, :shard]
    qkv_grad = grads[:3, :shard]
    gain_first = (qkv_grad * qkv_weight.astype(F32)).sum(axis=(0, 2)) / norm_gains[0]
    return (
        output,
        input_grad,
        logit_grad,
        qkv_grad,
        grads[3, :shard],
        jnp.stack([gain_first, small_grad[14]]),
        small_grad[:8].T,
        small_grad[8:12].T,
        small_grad[12:14],
        *expert_grads,
    )


def whole_sequence_fits(mesh):
    return (mesh.shape["experts"], mesh.shape["context"], mesh.shape["dp"]) == (4, 4, 2)


def solution(mesh):
    local = chip_local if whole_sequence_fits(mesh) else general_local
    in_specs = (
        P(None, ("experts", "dp"), "context", None),
        P(None, ("experts", "dp"), "context", None),
        P(None, ("context", "dp"), None),
        P(("context", "dp"), None),
        P(None, ("context", "dp")),
        P(("context", "dp"), None),
        P(("context", "dp"), None),
        P(None, ("context", "dp")),
        P("experts", None, ("context", "dp")),
        P("experts", None, ("context", "dp")),
        P("experts", None, ("context", "dp")),
        P(None, ("experts", "dp"), "context", None),
        P(None, ("experts", "dp"), "context", None),
        P(None, ("experts", "dp"), "context"),
    )
    out_specs = (
        P(None, ("experts", "dp"), "context", None),
        P(None, ("experts", "dp"), "context", None),
        P(None, ("experts", "dp"), "context", None),
        P(None, ("context", "dp"), None),
        P(("context", "dp"), None),
        P(None, ("context", "dp")),
        P(("context", "dp"), None),
        P(("context", "dp"), None),
        P(None, ("context", "dp")),
        P("experts", None, ("context", "dp")),
        P("experts", None, ("context", "dp")),
        P("experts", None, ("context", "dp")),
    )
    return jax.shard_map(local, mesh=mesh, in_specs=in_specs, out_specs=out_specs, check_vma=False)
```

```python
import functools
import functools
import math

import jax
import jax.numpy as jnp
import numpy as np
from jax import lax
from jax.experimental import pallas as pl
from jax.experimental.pallas import tpu as pltpu
from jax.sharding import PartitionSpec as P

HEAD_DIM = 64
FF = 2048


EPSILON = 1e-05
MASKED = -1e30


def rotate(values, positions, direction):
    half_dim = values.shape[-1] // 2
    inverse = 10000.0 ** (-jnp.arange(half_dim, dtype=jnp.float32) / half_dim)
    angles = positions.astype(jnp.float32)[:, None] * inverse[None, :]
    cosine = jnp.cos(angles)[:, None, :]
    sine_part = jnp.sin(angles)[:, None, :]
    first_half = values[..., :half_dim]
    second = values[..., half_dim:]
    return jnp.concatenate(
        [
            first_half * cosine - direction * second * sine_part,
            second * cosine + direction * first_half * sine_part,
        ],
        axis=-1,
    )


def softmax_last(logits):
    shifted = jnp.exp(logits - jnp.max(logits, axis=-1, keepdims=True))
    return shifted / jnp.sum(shifted, axis=-1, keepdims=True)


def norm_scale(values):
    return lax.rsqrt(jnp.mean(values * values, axis=-1, keepdims=True) + EPSILON)


def norm_back(grad_in, values, factor, gain_vec):
    scaled = grad_in * gain_vec
    grad_gain = jnp.sum(grad_in * values * factor, axis=0)
    grad_values = factor * scaled - values * factor * factor * factor * jnp.mean(
        scaled * values, axis=-1, keepdims=True
    )
    return (grad_values, grad_gain)


def masked_scores(
    queries, key_rows, query_segments, key_segments, query_positions, key_positions, score_scale
):
    scores = (
        jnp.einsum("qhd,khd->hqk", queries, key_rows, preferred_element_type=jnp.float32)
        * score_scale
    )
    allowed = (query_segments[:, None] == key_segments[None, :]) & (
        key_positions[None, :] <= query_positions[:, None]
    )
    return (jnp.where(allowed[None], scores, MASKED), allowed)


def general_local(
    inputs,
    cotangent,
    qkv_weight,
    out_weight,
    norm_gains,
    route_weight,
    const_gate,
    const_vec,
    w_gate,
    w_up,
    w_down,
    prev_logits,
    routes,
    segments,
):
    micro_count = inputs.shape[0]
    row_count = inputs.shape[2]
    model_width = inputs.shape[3]
    head_count = model_width // HEAD_DIM
    score_scale = HEAD_DIM ** (-0.5)
    local_experts = w_gate.shape[0]
    experts = local_experts * lax.axis_size("experts")
    capacity = row_count * 5 // 16
    routed = prev_logits.shape[3]
    assigned = 2 * row_count
    head_shape = (row_count, head_count, HEAD_DIM)
    positions = lax.axis_index("context") * row_count + jnp.arange(row_count, dtype=jnp.int32)
    grad_qkv = jnp.zeros((3, model_width, model_width), jnp.float32)
    grad_out = jnp.zeros((model_width, model_width), jnp.float32)
    gain_first = jnp.zeros((model_width,), jnp.float32)
    gain_second = jnp.zeros((model_width,), jnp.float32)
    grad_vec = jnp.zeros((2, model_width), jnp.float32)
    grad_route = jnp.zeros((model_width, routed), jnp.float32)
    grad_mixer = jnp.zeros((model_width, 4), jnp.float32)
    grad_gate = jnp.zeros((local_experts, model_width, FF), jnp.float32)
    grad_up = jnp.zeros((local_experts, model_width, FF), jnp.float32)
    grad_down = jnp.zeros((local_experts, model_width, FF), jnp.float32)
    output_rows = []
    input_rows = []
    logit_rows = []
    for batch_index in range(micro_count):
        qkv_full, out_full, gains, vectors, route_full, mixer_full = (
            lax.all_gather(qkv_weight, ("context", "dp"), axis=1, tiled=True),
            lax.all_gather(out_weight, ("context", "dp"), axis=0, tiled=True),
            lax.all_gather(
                norm_gains.astype(jnp.bfloat16), ("context", "dp"), axis=1, tiled=True
            ).astype(norm_gains.dtype),
            lax.all_gather(
                const_vec.astype(jnp.bfloat16), ("context", "dp"), axis=1, tiled=True
            ).astype(const_vec.dtype),
            lax.all_gather(route_weight, ("context", "dp"), axis=0, tiled=True),
            lax.all_gather(const_gate, ("context", "dp"), axis=0, tiled=True),
        )
        gate_full, up_full, down_full = (
            lax.all_gather(w_gate, ("context", "dp"), axis=2, tiled=True),
            lax.all_gather(w_up, ("context", "dp"), axis=2, tiled=True),
            lax.all_gather(w_down, ("context", "dp"), axis=2, tiled=True),
        )
        token_rows = inputs[batch_index, 0].astype(jnp.float32)
        seg_rows = segments[batch_index, 0]
        route_rows = routes[batch_index, 0]
        grad_rows = cotangent[batch_index, 0].astype(jnp.float32)
        scale_first = norm_scale(token_rows)
        normed_in = (token_rows * scale_first * gains[0]).astype(jnp.bfloat16)
        projected = jnp.einsum(
            "qd,cde->cqe", normed_in, qkv_full, preferred_element_type=jnp.float32
        )
        queries = rotate(projected[0].reshape(head_shape), positions, 1.0).astype(jnp.bfloat16)
        rotated_keys = rotate(projected[1].reshape(head_shape), positions, 1.0).astype(jnp.bfloat16)
        values = projected[2].reshape(head_shape).astype(jnp.bfloat16)
        row_peak = jnp.full((head_count, row_count), MASKED, jnp.float32)
        key_block = lax.all_gather(rotated_keys, "context", axis=0, tiled=True)
        value_block = lax.all_gather(values, "context", axis=0, tiled=True)
        segment_block = lax.all_gather(seg_rows, "context", axis=0, tiled=True)
        key_positions = jnp.arange(key_block.shape[0], dtype=jnp.int32)
        scores, allowed = masked_scores(
            queries, key_block, seg_rows, segment_block, positions, key_positions, score_scale
        )
        new_peak = jnp.maximum(row_peak, jnp.max(scores, axis=-1))
        expo = jnp.where(allowed[None], jnp.exp(scores - new_peak[:, :, None]), 0.0)
        weighted = jnp.einsum(
            "hqk,khd->hqd",
            expo.astype(jnp.bfloat16),
            value_block,
            preferred_element_type=jnp.float32,
        )
        row_peak, row_total, weighted = (new_peak, jnp.sum(expo, axis=-1), weighted)
        log_total = row_peak + jnp.log(row_total)
        attn_heads = jnp.transpose(weighted / row_total[:, :, None], (1, 0, 2))
        attended = attn_heads.reshape(row_count, model_width).astype(jnp.bfloat16)
        hidden = token_rows + jnp.dot(attended, out_full, preferred_element_type=jnp.float32)
        scale_second = norm_scale(hidden)
        normed = hidden * scale_second * gains[1]
        normed_low = normed.astype(jnp.bfloat16)
        logits = (
            jnp.dot(normed_low, route_full, preferred_element_type=jnp.float32)
            + prev_logits[batch_index, 0]
        )
        probabilities = softmax_last(logits)
        gate_values = jnp.take_along_axis(probabilities, route_rows, axis=-1)
        route_ids = route_rows.reshape(-1)
        routed_ffn = route_ids < experts
        onehot = (route_ids[:, None] == jnp.arange(experts, dtype=jnp.int32)[None, :]).astype(
            jnp.int32
        )
        slot_index = jnp.sum((jnp.cumsum(onehot, axis=0) - onehot) * onehot, axis=-1)
        slot_table = (
            jnp.full((experts, capacity), assigned, jnp.int32)
            .at[jnp.where(routed_ffn, route_ids, experts), slot_index]
            .set(jnp.arange(assigned, dtype=jnp.int32), mode="drop")
        )
        token_of = jnp.where(slot_table < assigned, slot_table // 2, row_count)
        pad_rows = jnp.concatenate([normed_low, jnp.zeros((1, model_width), jnp.bfloat16)], axis=0)
        received = lax.all_to_all(
            pad_rows[token_of], "experts", split_axis=0, concat_axis=1, tiled=True
        )
        gate_act = jnp.einsum(
            "erd,edf->erf", received, gate_full, preferred_element_type=jnp.float32
        )
        up_act = jnp.einsum("erd,edf->erf", received, up_full, preferred_element_type=jnp.float32)
        sigma = jax.nn.sigmoid(gate_act)
        silu_act = gate_act * sigma
        inner_low = (silu_act * up_act).astype(jnp.bfloat16)
        expert_low = jnp.einsum(
            "erf,edf->erd", inner_low, down_full, preferred_element_type=jnp.float32
        ).astype(jnp.bfloat16)
        returned = lax.all_to_all(
            expert_low, "experts", split_axis=1, concat_axis=0, tiled=True
        ).reshape(experts * capacity, model_width)
        pick_index = jnp.where(routed_ffn, route_ids * capacity + slot_index, 0)
        expert_out = jnp.where(
            routed_ffn[:, None], returned[pick_index].astype(jnp.float32), 0.0
        ).reshape(row_count, 2, model_width)
        const_mix = softmax_last(
            jnp.dot(normed_low, mixer_full, preferred_element_type=jnp.float32).reshape(
                row_count, 2, 2
            )
        )
        const_out = (
            const_mix[:, :, 0:1] * normed[:, None, :] + const_mix[:, :, 1:2] * vectors[None, :, :]
        )
        copy_mask = (route_rows == experts + 1).astype(jnp.float32)
        const_pick = (
            route_rows[:, :, None] == experts + 2 + jnp.arange(2, dtype=jnp.int32)[None, None, :]
        ).astype(jnp.float32)
        branch = (
            expert_out
            + copy_mask[:, :, None] * normed[:, None, :]
            + jnp.einsum("qjc,qcd->qjd", const_pick, const_out, precision=lax.Precision.HIGHEST)
        )
        output_rows.append(
            (hidden + jnp.sum(gate_values[:, :, None] * branch, axis=1)).astype(jnp.bfloat16)
        )
        grad_branch = gate_values[:, :, None] * grad_rows[:, None, :]
        grad_gates = jnp.sum(grad_rows[:, None, :] * branch, axis=-1)
        grad_probs = jnp.sum(
            (route_rows[:, :, None] == jnp.arange(routed, dtype=jnp.int32)[None, None, :]).astype(
                jnp.float32
            )
            * grad_gates[:, :, None],
            axis=1,
        )
        grad_logits = probabilities * (
            grad_probs - jnp.sum(probabilities * grad_probs, axis=-1, keepdims=True)
        )
        logit_rows.append(grad_logits)
        normed_wide = normed_low.astype(jnp.float32)
        grad_route = grad_route + jnp.dot(
            normed_wide.T, grad_logits, precision=lax.Precision.HIGHEST
        )
        grad_normed = jnp.dot(
            grad_logits, route_full.astype(jnp.float32).T, precision=lax.Precision.HIGHEST
        )
        grad_normed = grad_normed + jnp.sum(copy_mask[:, :, None] * grad_branch, axis=1)
        grad_const = jnp.einsum(
            "qjc,qjd->qcd", const_pick, grad_branch, precision=lax.Precision.HIGHEST
        )
        grad_mix = jnp.stack(
            [
                jnp.sum(grad_const * normed[:, None, :], axis=-1),
                jnp.sum(grad_const * vectors[None, :, :], axis=-1),
            ],
            axis=-1,
        )
        grad_mix_logits = (
            const_mix * (grad_mix - jnp.sum(const_mix * grad_mix, axis=-1, keepdims=True))
        ).reshape(row_count, 4)
        grad_mixer = grad_mixer + jnp.dot(
            normed_wide.T, grad_mix_logits, precision=lax.Precision.HIGHEST
        )
        grad_normed = grad_normed + jnp.dot(
            grad_mix_logits, mixer_full.astype(jnp.float32).T, precision=lax.Precision.HIGHEST
        )
        grad_normed = grad_normed + jnp.sum(const_mix[:, :, 0:1] * grad_const, axis=1)
        grad_vec = grad_vec + jnp.sum(const_mix[:, :, 1:2] * grad_const, axis=0)
        grad_slots = jnp.where(
            routed_ffn[:, None], grad_branch.reshape(assigned, model_width), 0.0
        ).astype(jnp.bfloat16)
        grad_pad = jnp.concatenate([grad_slots, jnp.zeros((1, model_width), jnp.bfloat16)], axis=0)
        grad_received = lax.all_to_all(
            grad_pad[slot_table], "experts", split_axis=0, concat_axis=1, tiled=True
        )
        grad_inner = jnp.einsum(
            "erd,edf->erf", grad_received, down_full, preferred_element_type=jnp.float32
        )
        grad_down = grad_down + jnp.einsum(
            "erd,erf->edf", grad_received, inner_low, preferred_element_type=jnp.float32
        )
        grad_gate_low = (grad_inner * up_act * sigma * (1.0 + gate_act * (1.0 - sigma))).astype(
            jnp.bfloat16
        )
        grad_up_low = (grad_inner * silu_act).astype(jnp.bfloat16)
        grad_gate = grad_gate + jnp.einsum(
            "erd,erf->edf", received, grad_gate_low, preferred_element_type=jnp.float32
        )
        grad_up = grad_up + jnp.einsum(
            "erd,erf->edf", received, grad_up_low, preferred_element_type=jnp.float32
        )
        grad_entry = (
            jnp.einsum("erf,edf->erd", grad_gate_low, gate_full, preferred_element_type=jnp.float32)
            + jnp.einsum("erf,edf->erd", grad_up_low, up_full, preferred_element_type=jnp.float32)
        ).astype(jnp.bfloat16)
        grad_back = lax.all_to_all(
            grad_entry, "experts", split_axis=1, concat_axis=0, tiled=True
        ).reshape(experts * capacity, model_width)
        grad_normed = grad_normed + jnp.sum(
            jnp.where(routed_ffn[:, None], grad_back[pick_index].astype(jnp.float32), 0.0).reshape(
                row_count, 2, model_width
            ),
            axis=1,
        )
        grad_hidden_norm, gain_term = norm_back(grad_normed, hidden, scale_second, gains[1])
        gain_second = gain_second + gain_term
        grad_hidden = grad_rows + grad_hidden_norm
        grad_attn_low = grad_hidden.astype(jnp.bfloat16)
        grad_out = grad_out + jnp.dot(attended.T, grad_attn_low, preferred_element_type=jnp.float32)
        grad_attended = (
            jnp.dot(grad_attn_low, out_full.T, preferred_element_type=jnp.float32)
            .astype(jnp.bfloat16)
            .reshape(head_shape)
        )
        delta = jnp.sum(grad_attended.astype(jnp.float32) * attn_heads, axis=-1).T
        zero_heads = jnp.zeros(head_shape, jnp.float32)
        key_all, value_all, segment_all = (
            lax.all_gather(rotated_keys, "context", axis=0, tiled=True),
            lax.all_gather(values, "context", axis=0, tiled=True),
            lax.all_gather(seg_rows, "context", axis=0, tiled=True),
        )
        total_keys = key_all.shape[0]
        group_count = math.gcd(total_keys // row_count, max(1, 512 // row_count))
        block_rows = row_count * group_count
        block_count = total_keys // block_rows

        def back_block(grad_query, block_parts):
            key_block, value_block, segment_block, block_start = block_parts
            key_positions = block_start + jnp.arange(block_rows, dtype=jnp.int32)
            scores, allowed = masked_scores(
                queries, key_block, seg_rows, segment_block, positions, key_positions, score_scale
            )
            probability = jnp.where(allowed[None], jnp.exp(scores - log_total[:, :, None]), 0.0)
            grad_prob = jnp.einsum(
                "qhd,khd->hqk", grad_attended, value_block, preferred_element_type=jnp.float32
            )
            grad_score = (probability * (grad_prob - delta[:, :, None])).astype(jnp.bfloat16)
            grad_query = (
                grad_query
                + jnp.einsum(
                    "hqk,khd->qhd", grad_score, key_block, preferred_element_type=jnp.float32
                )
                * score_scale
            )
            grad_key = (
                jnp.einsum("hqk,qhd->khd", grad_score, queries, preferred_element_type=jnp.float32)
                * score_scale
            )
            grad_value = jnp.einsum(
                "hqk,qhd->khd",
                probability.astype(jnp.bfloat16),
                grad_attended,
                preferred_element_type=jnp.float32,
            )
            return (grad_query, (grad_key, grad_value))

        block_starts = jnp.arange(block_count, dtype=jnp.int32) * block_rows
        grad_query, (key_terms, value_terms) = lax.scan(
            back_block,
            zero_heads,
            (
                key_all.reshape(block_count, block_rows, head_count, HEAD_DIM),
                value_all.reshape(block_count, block_rows, head_count, HEAD_DIM),
                segment_all.reshape(block_count, block_rows),
                block_starts,
            ),
        )
        grad_key, grad_value = (
            lax.psum_scatter(
                key_terms.reshape(total_keys, head_count, HEAD_DIM).astype(jnp.bfloat16),
                "context",
                scatter_dimension=0,
                tiled=True,
            ).astype(jnp.float32),
            lax.psum_scatter(
                value_terms.reshape(total_keys, head_count, HEAD_DIM).astype(jnp.bfloat16),
                "context",
                scatter_dimension=0,
                tiled=True,
            ).astype(jnp.float32),
        )
        grad_projected = jnp.stack(
            [
                rotate(grad_query, positions, -1.0).reshape(row_count, model_width),
                rotate(grad_key, positions, -1.0).reshape(row_count, model_width),
                grad_value.reshape(row_count, model_width),
            ]
        ).astype(jnp.bfloat16)
        grad_qkv = grad_qkv + jnp.einsum(
            "qd,cqe->cde", normed_in, grad_projected, preferred_element_type=jnp.float32
        )
        grad_normed_in = jnp.einsum(
            "cqe,cde->qd", grad_projected, qkv_full, preferred_element_type=jnp.float32
        )
        grad_token_norm, gain_term = norm_back(grad_normed_in, token_rows, scale_first, gains[0])
        gain_first = gain_first + gain_term
        input_rows.append(grad_hidden + grad_token_norm)
    grad_gain = jnp.stack([gain_first, gain_second])
    (
        grad_qkv,
        grad_out,
        grad_gain,
        grad_vec,
        grad_route,
        grad_mixer,
        grad_gate,
        grad_up,
        grad_down,
    ) = (
        lax.psum_scatter(
            grad_qkv.astype(jnp.bfloat16), ("context", "dp"), scatter_dimension=1, tiled=True
        ).astype(jnp.float32),
        lax.psum_scatter(
            grad_out.astype(jnp.bfloat16), ("context", "dp"), scatter_dimension=0, tiled=True
        ).astype(jnp.float32),
        lax.psum_scatter(
            grad_gain.astype(jnp.bfloat16), ("context", "dp"), scatter_dimension=1, tiled=True
        ).astype(jnp.float32),
        lax.psum_scatter(
            grad_vec.astype(jnp.bfloat16), ("context", "dp"), scatter_dimension=1, tiled=True
        ).astype(jnp.float32),
        lax.psum_scatter(
            grad_route.astype(jnp.bfloat16), ("context", "dp"), scatter_dimension=0, tiled=True
        ).astype(jnp.float32),
        lax.psum_scatter(
            grad_mixer.astype(jnp.bfloat16), ("context", "dp"), scatter_dimension=0, tiled=True
        ).astype(jnp.float32),
        lax.psum_scatter(
            grad_gate.astype(jnp.bfloat16), ("context", "dp"), scatter_dimension=2, tiled=True
        ).astype(jnp.float32),
        lax.psum_scatter(
            grad_up.astype(jnp.bfloat16), ("context", "dp"), scatter_dimension=2, tiled=True
        ).astype(jnp.float32),
        lax.psum_scatter(
            grad_down.astype(jnp.bfloat16), ("context", "dp"), scatter_dimension=2, tiled=True
        ).astype(jnp.float32),
    )
    grad_qkv, grad_out, grad_gain, grad_vec, grad_route, grad_mixer = (
        lax.psum(grad_qkv.astype(jnp.bfloat16), "experts").astype(jnp.float32),
        lax.psum(grad_out.astype(jnp.bfloat16), "experts").astype(jnp.float32),
        lax.psum(grad_gain.astype(jnp.bfloat16), "experts").astype(jnp.float32),
        lax.psum(grad_vec.astype(jnp.bfloat16), "experts").astype(jnp.float32),
        lax.psum(grad_route.astype(jnp.bfloat16), "experts").astype(jnp.float32),
        lax.psum(grad_mixer.astype(jnp.bfloat16), "experts").astype(jnp.float32),
    )
    output = jnp.stack(output_rows)[:, None]
    input_grad = jnp.stack(input_rows)[:, None]
    logit_grad = jnp.stack(logit_rows)[:, None]
    return (
        output,
        input_grad,
        logit_grad,
        grad_qkv,
        grad_out,
        grad_gain,
        grad_route,
        grad_mixer,
        grad_vec,
        grad_gate,
        grad_up,
        grad_down,
    )


BF = jnp.bfloat16
F32 = jnp.float32
BLOCK = 256
RING = 4
VMEM_BYTES = 60 * 2**20


def dot(left, right, left_dim, right_dim):
    return lax.dot_general(
        left, right, (((left_dim,), (right_dim,)), ((), ())), preferred_element_type=F32
    )


def iota(shape, dim):
    return lax.broadcasted_iota(jnp.int32, shape, dim)


def split3(values):
    high = values.astype(BF).astype(F32)
    rest = values - high
    middle = rest.astype(BF).astype(F32)
    return (high, middle, rest - middle)


def split2(values):
    high = values.astype(BF)
    return (high, (values - high.astype(F32)).astype(BF))


def rows_of(parts, count):
    width = parts[0].shape[1]
    index = iota((count, width), 0)
    total = jnp.zeros((count, width), F32)
    for place, part in enumerate(parts):
        total = jnp.where(index == place, jnp.broadcast_to(part, (count, width)), total)
    return total


def column_of(row, width=128):
    stacked = rows_of(split3(row), 16).astype(BF)
    return dot(stacked, jnp.ones((16, width), BF), 0, 0)


def wide(column, copies):
    return jnp.concatenate([column] * copies, axis=1)


def kernel_call(
    body, idx, args, outs, flops, grid=None, in_specs=None, out_specs=None, scratch=(), share=1
):
    moved = sum(a.size * a.dtype.itemsize for a in args)
    moved += sum(math.prod(s) * jnp.dtype(d).itemsize for s, d in outs)
    whole = pl.BlockSpec(memory_space=pltpu.VMEM)
    extra = {} if grid is None else {"grid": grid}
    return pl.pallas_call(
        body,
        out_shape=[jax.ShapeDtypeStruct(s, d) for s, d in outs],
        in_specs=[pl.BlockSpec(memory_space=pltpu.SMEM)]
        + (in_specs if in_specs is not None else [whole] * len(args)),
        out_specs=out_specs if out_specs is not None else [whole] * len(outs),
        scratch_shapes=list(scratch),
        compiler_params=pltpu.CompilerParams(vmem_limit_bytes=VMEM_BYTES),
        cost_estimate=pl.CostEstimate(
            flops=flops // share, bytes_accessed=moved // share, transcendentals=0
        ),
        **extra,
    )(idx, *args)


def rope_tables(length):
    half = HEAD_DIM // 2
    inverse = (10000.0 ** (-np.arange(half, dtype=np.float32) / half)).astype(np.float32)
    angles = (np.arange(length, dtype=np.float32)[:, None] * inverse[None, :]).astype(np.float64)
    cosine, sine = np.cos(angles), np.sin(angles)
    cosine = np.concatenate([cosine] * 4, axis=1).astype(np.float32)
    sine = np.concatenate([-sine, sine] * 2, axis=1).astype(np.float32)
    return cosine, sine


def turn(values, cosine, sine, direction):
    width = values.shape[1]
    copies = width // cosine.shape[1]
    ahead = pltpu.roll(values, width - HEAD_DIM // 2, 1)
    behind = pltpu.roll(values, HEAD_DIM // 2, 1)
    first = (iota(values.shape, 1) & (HEAD_DIM - 1)) < HEAD_DIM // 2
    partner = jnp.where(first, ahead, behind)
    return values * wide(cosine, copies) + direction * (partner * wide(sine, copies))


def project_kernel(idx, xa, xb, theirs, columns, w_ref, cosine, sine, *outs):
    q_ref, k_ref, v_ref, normed_ref, params_ref, seg_row, seg_col, x_ref = outs
    core, flip = idx[2], idx[3]
    row, column = iota((16, 128), 0), iota((16, 128), 1)
    spread = (row == column) | ((row >= 12) & ((column == row + 4) | (column == row + 8)))
    params_ref[...] = dot(jnp.where(spread, 1.0, 0.0).astype(BF), columns[...], 1, 1)
    sources = (
        (xa, core, 0),
        (xb, core, 1),
        (theirs.at[0], 1 - core, 0),
        (theirs.at[1], 1 - core, 1),
    )
    for ref, half, slot in sources:
        block = 2 * half + (flip if slot == 0 else 1 - flip)
        rows = pl.ds(pl.multiple_of(block * BLOCK, BLOCK), BLOCK)
        x_ref[rows, :] = ref[:BLOCK, :]
        segment = ref[ref.shape[0] - 16 :, :BLOCK].astype(F32)[10:11]
        seg_row[:, rows] = jnp.broadcast_to(segment, (8, BLOCK))
        seg_col[rows, :] = column_of(segment)
    gain = params_ref[14:15, :]
    tiles = [slice(i * BLOCK, (i + 1) * BLOCK) for i in range(x_ref.shape[0] // BLOCK)]
    for rows in tiles:
        x = x_ref[rows, :].astype(F32)
        normed_ref[rows, :] = (x * norm_scale(x) * gain).astype(BF)
    queries, keys, values = (dot(normed_ref[...], w_ref[j], 1, 0) for j in range(3))
    for rows in tiles:
        turned = turn(queries[rows], cosine[rows, :], sine[rows, :], 1.0)
        q_ref[rows, :] = (turned * HEAD_DIM**-0.5).astype(BF)
        k_ref[rows, :] = turn(keys[rows], cosine[rows, :], sine[rows, :], 1.0).astype(BF)
        v_ref[rows, :] = values[rows].astype(BF)


def mask_of(seg_row, seg_col, i):
    n = (i + 1) * BLOCK
    mine = seg_row[:1, i * BLOCK : n]
    key_index, query_index = iota((BLOCK, BLOCK), 0), iota((BLOCK, BLOCK), 1)
    last = (seg_col[i * BLOCK : n, :1] == mine) & (key_index <= query_index)
    bias = jnp.where(last, 0.0, MASKED)
    if i > 0:
        before = jnp.where(seg_col[: i * BLOCK, :1] == mine, 0.0, MASKED)
        bias = jnp.concatenate([before, bias], axis=0)
    return bias


def both_heads(values, low_lanes):
    return jnp.concatenate(
        [jnp.where(low_lanes, values, 0), jnp.where(low_lanes, 0, values)], axis=0
    )


def attend_kernel(idx, q_ref, k_ref, v_ref, seg_row, seg_col, keep_ref, send_ref, lse_ref):
    core, flip = idx[2], idx[3]
    low_lanes = iota((BLOCK, 2 * HEAD_DIM), 1) < HEAD_DIM
    results = []
    for i in range(q_ref.shape[0] // BLOCK):
        n = (i + 1) * BLOCK
        queries = q_ref[i * BLOCK : n, :]
        keys, values = k_ref[:n, :], v_ref[:n, :]
        bias = mask_of(seg_row, seg_col, i)
        both = both_heads(queries, low_lanes)
        scores = dot(keys, both, 1, 1) + wide(bias, 2)
        peak = jnp.max(scores, axis=0, keepdims=True)
        weights = jnp.exp(scores - peak)
        total = jnp.sum(weights, axis=0, keepdims=True)
        out = dot(values, weights.astype(BF), 0, 0)
        lse = peak + jnp.log(total)
        out = out / total
        out = jnp.concatenate([out[:HEAD_DIM, :BLOCK], out[HEAD_DIM:, BLOCK:]], axis=0)
        lse_ref[0, 0:1, i * BLOCK : n] = lse[:, :BLOCK]
        lse_ref[0, 1:2, i * BLOCK : n] = lse[:, BLOCK:]
        half, slot = i // 2, (i % 2) ^ flip
        results.append((half, slot, out.T.astype(BF)))
    for half, slot, attended in results:
        rows = pl.ds(pl.multiple_of(slot * BLOCK, BLOCK), BLOCK)

        @pl.when(half == core)
        def _(attended=attended, rows=rows):
            keep_ref[rows, :] = attended

        @pl.when(half != core)
        def _(attended=attended, rows=rows):
            send_ref[rows, :] = attended


def pair_back_kernel(
    first, idx, q_ref, k_ref, v_ref, own_ref, other_ref, seg_row, seg_col, lse_ref, cosine, sine,
    normed_ref, og_ref, og_recv, *refs,
):
    if first:
        small_ref, grads_ref, shared, key_sum, value_sum = refs
    else:
        grads_ref, shared, key_sum, value_sum = refs
    core, flip = idx[2], idx[3]
    lanes = 2 * HEAD_DIM
    low_lanes = iota((BLOCK, lanes), 1) < HEAD_DIM
    key_sum[...] = jnp.zeros(key_sum.shape, F32)
    value_sum[...] = jnp.zeros(value_sum.shape, F32)
    for i in range(q_ref.shape[0] // BLOCK):
        n = (i + 1) * BLOCK
        keys, values = k_ref[:n, :], v_ref[:n, :]
        half, slot = i // 2, (i % 2) ^ flip
        rows = pl.ds(pl.multiple_of(slot * BLOCK, BLOCK), BLOCK)
        grads = jnp.where(half == core, own_ref[rows, :], other_ref[rows, :])
        queries = both_heads(q_ref[i * BLOCK : n, :], low_lanes)
        grads = both_heads(grads, low_lanes)
        bias = mask_of(seg_row, seg_col, i)
        lse = jnp.concatenate([lse_ref[0, 0:1, i * BLOCK : n], lse_ref[0, 1:2, i * BLOCK : n]], 1)
        weights = jnp.exp(dot(keys, queries, 1, 1) + wide(bias, 2) - lse)
        grad_weights = dot(values, grads, 1, 1)
        delta = jnp.sum(weights * grad_weights, axis=0, keepdims=True)
        grad_scores = (weights * (grad_weights - delta)).astype(BF)
        key_sum[:n, :] += dot(grad_scores, queries, 1, 0)
        value_sum[:n, :] += dot(weights.astype(BF), grads, 1, 0)
        grad_query = dot(grad_scores, keys, 0, 0)
        grad_query = jnp.where(low_lanes, grad_query[:BLOCK], grad_query[BLOCK:]) * HEAD_DIM**-0.5
        tile = slice(i * BLOCK, n)
        turned = turn(grad_query, cosine[tile, :], sine[tile, :], -1.0)
        grads_ref[tile, :lanes] = turned.astype(BF)
    for i in range(q_ref.shape[0] // BLOCK):
        tile = slice(i * BLOCK, (i + 1) * BLOCK)
        turned = turn(key_sum[tile, :], cosine[tile, :], sine[tile, :], -1.0)
        grads_ref[tile, lanes : 2 * lanes] = turned.astype(BF)
        grads_ref[tile, 2 * lanes :] = value_sum[tile, :].astype(BF)
    model = normed_ref.shape[1]
    depth = model // RING
    weight_grads = dot(normed_ref[...], grads_ref[...], 0, 0)
    out_grads = og_ref[...].astype(F32) + og_recv[...].astype(F32)
    for z in range(RING):
        rows = slice(z * depth, (z + 1) * depth)
        for j in range(3):
            piece = weight_grads[rows, j * lanes : (j + 1) * lanes]
            shared[j, z, :depth, :] = piece.astype(BF)
        shared[3, z, :depth, :] = out_grads[rows].astype(BF)
        if first:
            shard = depth // 2
            for j in range(2):
                lane = iota((model, lanes), 1)
                pick = iota((model, lanes), 0) == lane + (z * depth + j * shard)
                pick = jnp.where(pick & (lane < shard), 1.0, 0.0).astype(BF)
                picked = dot(small_ref[...].astype(BF), pick, 1, 0)
                shared[j, z, depth:, :] = picked.astype(BF)
            for j in range(2, RING):
                shared[j, z, depth:, :] = jnp.zeros((16, lanes), BF)


def routed_rows(small, routed):
    index = iota((routed, small.shape[1]), 0).astype(F32)
    return jnp.where((small[8:9, :] == index) | (small[9:10, :] == index), 1.0, 0.0)


def ranks_of(named):
    tokens = named.shape[1]
    before, here = iota((tokens, tokens), 0), iota((tokens, tokens), 1)
    earlier = (before < here) & (before // BLOCK == here // BLOCK)
    stacked = jnp.concatenate([named, jnp.zeros_like(named)], axis=0).astype(BF)
    return dot(stacked, jnp.where(earlier, 1.0, 0.0).astype(BF), 1, 0)[: named.shape[0]]


def pick_row(values, index):
    return jnp.sum(jnp.where(iota(values.shape, 0) == index, values, 0.0), axis=0, keepdims=True)


def slots_of(named, rank, expert, capacity):
    tokens = named.shape[1]
    place = pick_row(rank, expert)
    place = place + jnp.where(iota((1, tokens), 1) >= BLOCK, float(capacity), 0.0)
    slot = iota((2 * capacity, tokens), 0).astype(F32)
    taken = (slot == place) & (pick_row(named, expert) > 0.5)
    return jnp.where(taken, 1.0, 0.0).astype(BF)


def pair_of(first, second):
    return jnp.concatenate([first[:BLOCK, :], second[:BLOCK, :]], axis=0)


def small_of(xa, xb):
    blocks = []
    for packed in (xa, xb):
        values = packed[BLOCK:, :].astype(F32)
        width = values.shape[1] // 3
        logits = values[:8, :width] + values[:8, width : 2 * width] + values[:8, 2 * width :]
        blocks.append(jnp.concatenate([logits, values[8:, :width]], axis=0))
    return jnp.concatenate(blocks, axis=1)


def grad_slots_kernel(idx, xa, xb, ca, cb, out):
    named = routed_rows(small_of(xa, xb), 8)
    rank = ranks_of(named)
    grads = pair_of(ca, cb)
    for expert in range(out.shape[0]):
        taken = slots_of(named, rank, expert, out.shape[1] // 2)
        out[expert] = dot(taken, grads, 1, 0).astype(BF)


def route_kernel(idx, keep, recv, xa, xb, params, mine, theirs, *refs):
    (hidden_ref, ow_ref, state_ref), outs = refs[:3], refs[3:]
    core = idx[2]
    width = keep.shape[1]
    own = pl.ds(pl.multiple_of(core * width, 128), width)
    other = pl.ds(pl.multiple_of((1 - core) * width, 128), width)
    ow_ref[:, own] = mine[...]
    ow_ref[:, other] = theirs[...]
    hidden = (
        pair_of(xa, xb).astype(F32)
        + dot(keep[...], ow_ref[own, :], 1, 0)
        + dot(recv[...], ow_ref[other, :], 1, 0)
    )
    hidden_ref[...] = hidden
    normed = (hidden * norm_scale(hidden) * params[15:16, :]).astype(BF)
    small = small_of(xa, xb)
    logits = dot(params[...].astype(BF), normed, 1, 1)
    named = routed_rows(small, 8)
    rank = ranks_of(named)
    shifted = logits[:8] + small[:8]
    shifted = jnp.exp(shifted - jnp.max(shifted, axis=0, keepdims=True))
    probabilities = shifted / jnp.sum(shifted, axis=0, keepdims=True)
    mixed = []
    for c in range(2):
        first, second = logits[8 + 2 * c : 9 + 2 * c], logits[9 + 2 * c : 10 + 2 * c]
        peak = jnp.maximum(first, second)
        first, second = jnp.exp(first - peak), jnp.exp(second - peak)
        mixed += [first / (first + second), second / (first + second)]
    state_ref[0:8, :] = probabilities
    state_ref[8:16, :] = rows_of(mixed, 8)
    state_ref[16:24, :] = rank
    slots = outs[0].shape[0] - 16
    for k, out in enumerate(outs):
        expert = idx[0] ^ k
        taken = slots_of(named, rank, expert, slots // 2)
        out[:slots, :] = dot(taken, normed, 1, 0).astype(BF)
        gates = rows_of(split3(pick_row(probabilities, expert)), 16).astype(BF)
        out[slots:, :] = jnp.zeros((16, out.shape[1]), BF)
        out[slots:, :slots] = dot(gates, taken, 1, 1).astype(BF)


def expert_kernel(idx, g_own, g_other, weights, *refs):
    pieces, refs = refs[:8], refs[8:]
    lefts, acts, keep, send = refs[:4]
    g_all, scale_all, products, joined, joined_w, entry_sum, dot_sum = refs[4:]
    core = idx[2]
    j = pl.program_id(0)
    slots = g_own.shape[1]
    count, model = g_all.shape
    lanes = dot_sum.shape[1]
    chunk = weights.shape[3]

    @pl.when(j == 0)
    def _():
        for p in range(8):
            grads = (g_own if p < RING else g_other)[idx[0] ^ (p % RING)]
            rows = slice(p * slots, (p + 1) * slots)
            lefts[0, rows, :] = pieces[p][:slots, :]
            scale = dot(pieces[p][slots:, :slots], jnp.ones((16, lanes), BF), 0, 0)
            scale_all[rows, :] = scale
            g_all[rows, :] = grads
            scaled = grads.astype(F32) * wide(scale, model // lanes)
            lefts[1, rows, :] = scaled.astype(BF)
        dot_sum[...] = jnp.zeros(dot_sum.shape, F32)
        entry_sum[...] = jnp.zeros(entry_sum.shape, F32)

    joined_w[:, :chunk] = weights[0, 0]
    joined_w[:, chunk:] = weights[0, 1]
    products[:, : 2 * chunk] = dot(lefts[0], joined_w[...], 1, 0)
    products[:, 2 * chunk :] = dot(g_all[...], weights[0, 2], 1, 0)
    tile = 64
    for i in range(count // tile):
        rows = slice(i * tile, (i + 1) * tile)
        gate, up, back = (products[rows, p * chunk : (p + 1) * chunk] for p in range(3))
        sigma = 0.5 * jnp.tanh(0.5 * gate) + 0.5
        silu = gate * sigma
        inner = silu * up
        acts[2, rows, :] = inner.astype(BF)
        product = inner * back
        dot_sum[rows, :] += product[:, :lanes] + product[:, lanes:]
        back = back * wide(scale_all[rows, :], chunk // lanes)
        grad_gate = (back * up * (sigma + silu - silu * sigma)).astype(BF)
        grad_up = (back * silu).astype(BF)
        acts[0, rows, :] = grad_gate
        acts[1, rows, :] = grad_up
        joined[rows, :chunk] = grad_gate
        joined[rows, chunk:] = grad_up
    entry_sum[...] += dot(joined[...], joined_w[...], 1, 1)

    @pl.when(j == pl.num_programs(0) - 1)
    def _():
        ones = jnp.ones((16, lanes), BF)
        index = iota((16, slots), 0)
        for p in range(8):
            rows = slice(p * slots, (p + 1) * slots)
            high, low = split2(dot_sum[rows, :])
            high, middle, rest = split3(dot(ones, high, 1, 1) + dot(ones, low, 1, 1))
            packed = jnp.where(
                index == 4 * core,
                high,
                jnp.where(
                    index == 4 * core + 1, middle, jnp.where(index == 4 * core + 2, rest, 0.0)
                ),
            )
            out = (keep if p < RING else send).at[idx[0] ^ (p % RING)]
            out[:slots, :] = entry_sum[rows, :].astype(BF)
            out[slots:, :] = jnp.zeros((16, model), BF)
            out[slots:, :slots] = packed.astype(BF)


def expert_out_kernel(idx, inner_ref, weights, keep, send, down):
    slots = keep.shape[1]
    chunk = weights.shape[3]
    for k in range(RING):
        down[:, k * chunk : (k + 1) * chunk] = weights[k, 0]
    out = dot(inner_ref[0], down[...], 1, 1).astype(BF)
    for p in range(8):
        place = idx[0] ^ (p % RING)
        (keep if p < RING else send)[place] = out[p * slots : (p + 1) * slots]


def expert_grads_kernel(idx, left, right, out):
    chunk = out.shape[3]
    grad = dot(left[0], right[0], 0, 0).astype(BF)
    for k in range(out.shape[0]):
        out[k, 0] = grad[:, k * chunk : (k + 1) * chunk]


def slot_table(small, state, capacity):
    named = routed_rows(small, 8)
    rank = state[16:24, :]
    return [slots_of(named, rank, expert, capacity) for expert in range(RING)], named


def branch_weights(state, named):
    gates = state[0:8, :] * named
    consts = [gates[6 + c : 7 + c] for c in range(2)]
    normed_weight = gates[5:6]
    for c in range(2):
        normed_weight = normed_weight + consts[c] * state[8 + 2 * c : 9 + 2 * c, :]
    vector_weights = [consts[c] * state[9 + 2 * c : 10 + 2 * c, :] for c in range(2)]
    return consts, normed_weight, vector_weights


def output_kernel(idx, hidden_ref, state_ref, xa, xb, params, returned, logits_ref, oa, ob):
    state = state_ref[...]
    tables, named = slot_table(small_of(xa, xb), state, returned.shape[1] // 2)
    hidden = hidden_ref[...]
    normed = hidden * norm_scale(hidden) * params[15:16, :]
    _, normed_weight, vector_weights = branch_weights(state, named)
    output = hidden + wide(column_of(normed_weight), normed.shape[1] // 128) * normed
    vector_rows = rows_of(split3(params[12:13, :])[:2] * 2 + split3(params[13:14, :])[:2] * 2, 16)
    first, second = split3(vector_weights[0])[:2], split3(vector_weights[1])[:2]
    weight_rows = rows_of(
        (first[0], first[0], first[1], first[1], second[0], second[0], second[1], second[1]), 16
    )
    output += dot(weight_rows.astype(BF), vector_rows.astype(BF), 0, 0)
    for k in range(RING):
        gate = state[k : k + 1, :]
        high, low, _ = split3(gate)
        table = tables[k].astype(F32)
        output += dot((table * high).astype(BF), returned[k], 0, 0)
        output += dot((table * low).astype(BF), returned[k], 0, 0)
    for slot, out in enumerate((oa, ob)):
        out[:BLOCK, :] = output[slot * BLOCK : (slot + 1) * BLOCK].astype(BF)
        parts = split3(logits_ref[:, slot * BLOCK : (slot + 1) * BLOCK])
        parts = jnp.concatenate(parts, axis=1)
        out[BLOCK:, :] = jnp.concatenate([parts, jnp.zeros_like(parts)], axis=0).astype(BF)


def hidden_back_kernel(
    idx, hidden_ref, state_ref, xa, xb, ca, cb, params, ow_ref, returned, *outs
):
    gh_ref, low_ref, own_ref, send_ref, logits_ref, small_ref = outs
    core = idx[2]
    state = state_ref[...]
    slots = returned.shape[1] - 16
    tables, named = slot_table(small_of(xa, xb), state, slots // 2)
    probabilities = state[0:8, :]
    hidden = hidden_ref[...]
    factor = norm_scale(hidden)
    scaled_hidden = hidden * factor
    normed = scaled_hidden * params[15:16, :]
    normed_low = normed.astype(BF)
    grads_low = pair_of(ca, cb)
    grads = grads_low.astype(F32)
    ones = jnp.ones((16, hidden.shape[1]), BF)
    high, low = split2(grads * normed)
    on_normed = (dot(ones, high, 1, 1) + dot(ones, low, 1, 1))[0:1]
    first, second = split3(params[12:13, :])[:2], split3(params[13:14, :])[:2]
    on_vectors = dot(rows_of(first + second, 16).astype(BF), grads_low, 1, 1)
    on_vector = (on_vectors[0:1] + on_vectors[1:2], on_vectors[2:3] + on_vectors[3:4])
    consts, normed_weight, vector_weights = branch_weights(state, named)
    index = iota(probabilities.shape, 0)
    grad_probs = jnp.where(index == 5, on_normed, 0.0)
    mix_rows = []
    for c in range(2):
        mix_first, mix_second = state[8 + 2 * c : 9 + 2 * c, :], state[9 + 2 * c : 10 + 2 * c, :]
        dot_c = mix_first * on_normed + mix_second * on_vector[c]
        grad_probs = jnp.where(index == 6 + c, dot_c, grad_probs)
        grad_first, grad_second = consts[c] * on_normed, consts[c] * on_vector[c]
        mean = mix_first * grad_first + mix_second * grad_second
        mix_rows += [mix_first * (grad_first - mean), mix_second * (grad_second - mean)]
    back = jnp.zeros(hidden.shape, F32)
    for k in range(RING):
        packed = returned[k, slots:, :slots]
        found = jnp.sum(dot(packed, tables[k], 1, 0), axis=0, keepdims=True)
        grad_probs = jnp.where(index == k, found, grad_probs)
        back += dot(tables[k], returned[k, :slots, :], 0, 0)
    grad_probs = grad_probs * named
    grad_logits = probabilities * (
        grad_probs - jnp.sum(probabilities * grad_probs, axis=0, keepdims=True)
    )
    logits_ref[...] = grad_logits
    router_rows = jnp.concatenate([grad_logits, rows_of(mix_rows, 8)], axis=0)
    rows_high, rows_low = split2(router_rows)
    weights_low = params[...].astype(BF)
    grad_normed = (
        back
        + dot(rows_high, weights_low, 0, 0)
        + dot(rows_low, weights_low, 0, 0)
        + wide(column_of(normed_weight), hidden.shape[1] // 128) * grads
    )
    router_grad = dot(rows_high, normed_low, 1, 0) + dot(rows_low, normed_low, 1, 0)
    first, second = split3(vector_weights[0])[:2], split3(vector_weights[1])[:2]
    vector_grad = dot(rows_of(first + second, 16).astype(BF), grads_low, 1, 0)
    gain_grad = jnp.sum(grad_normed * scaled_hidden, axis=0, keepdims=True)
    small_ref[...] = jnp.where(
        iota(router_grad.shape, 0) < 12,
        router_grad,
        rows_of(
            [jnp.zeros_like(gain_grad)] * 12
            + [vector_grad[0:1] + vector_grad[1:2], vector_grad[2:3] + vector_grad[3:4], gain_grad],
            16,
        ),
    )
    scaled = grad_normed * params[15:16, :]
    mean = jnp.mean(scaled * hidden, axis=-1, keepdims=True)
    grad_hidden = grads + factor * scaled - hidden * (factor * factor * factor * mean)
    gh_ref[...] = grad_hidden
    grad_low = grad_hidden.astype(BF)
    low_ref[...] = grad_low
    width = own_ref.shape[1]
    own_rows = pl.ds(pl.multiple_of(core * width, 16), width)
    other_rows = pl.ds(pl.multiple_of((1 - core) * width, 16), width)
    own_ref[...] = dot(grad_low, ow_ref[own_rows, :], 1, 1).astype(BF)
    send_ref[...] = dot(grad_low, ow_ref[other_rows, :], 1, 1).astype(BF)


def out_grad_kernel(idx, keep, recv, low_ref, own_ref, send_ref):
    core = idx[2]
    width = keep.shape[1]
    own = pl.ds(pl.multiple_of(core * width, 128), width)
    other = pl.ds(pl.multiple_of((1 - core) * width, 128), width)
    for out, columns in ((own_ref, own), (send_ref, other)):
        grads = low_ref[:, columns]
        out[own, :] = dot(keep[...], grads, 0, 0).astype(BF)
        out[other, :] = dot(recv[...], grads, 0, 0).astype(BF)


def normed_back_kernel(idx, *refs):
    pair_grads, w_ref, keep_ref, send_ref, grads, weights = refs[:3], *refs[3:]
    core, flip = idx[2], idx[3]
    lanes = 2 * HEAD_DIM
    for h, ref in enumerate(pair_grads):
        columns = slice(h * 3 * lanes, (h + 1) * 3 * lanes)
        grads[:, columns] = ref[...]
        for j in range(3):
            place = (3 * h + j) * lanes
            weights[:, place : place + lanes] = w_ref[j, :, h * lanes : (h + 1) * lanes]
    total = dot(grads[...], weights[...], 1, 1).astype(BF)
    for half in range(2):
        for out, there in ((keep_ref, half == core), (send_ref, half != core)):

            @pl.when(there)
            def _(half=half, out=out):
                for part in range(2):
                    place = 2 * half + part
                    rows = pl.ds(pl.multiple_of((part ^ flip) * BLOCK, BLOCK), BLOCK)
                    out[rows, :] = total[place * BLOCK : (place + 1) * BLOCK]


def input_back_kernel(idx, keep_ref, recv_ref, gh_ref, xa, xb, params, oa, ob):
    gain = params[14:15, :]
    for slot, (x_ref, out) in enumerate(((xa, oa), (xb, ob))):
        tile = slice(slot * BLOCK, (slot + 1) * BLOCK)
        x = x_ref[:BLOCK, :].astype(F32)
        factor = norm_scale(x)
        scaled = (keep_ref[tile, :].astype(F32) + recv_ref[tile, :].astype(F32)) * gain
        mean = jnp.mean(scaled * x, axis=-1, keepdims=True)
        out[...] = (
            gh_ref[tile, :] + factor * scaled - x * (factor * factor * factor * mean)
        ).astype(BF)


def across(values):
    return lax.ppermute(values, "dp", [(0, 1), (1, 0)])


def over(values, k):
    return lax.ppermute(values, "experts", [(i, i ^ k) for i in range(RING)])


def exchange(values, axis):
    return lax.all_to_all(values, axis, 0, 0, tiled=True)


def after(values, *others):
    return lax.optimization_barrier((values, others))[0]


def handed_to_all(values, axis):
    return exchange(jnp.broadcast_to(values[None], (RING, *values.shape)), axis)


def chip_local(
    inputs, cotangent, qkv_weight, out_weight, norm_gains, route_weight, const_gate, const_vec,
    w_gate, w_up, w_down, prev_logits, routes, segments,
):
    e, z, core = lax.axis_index("experts"), lax.axis_index("context"), lax.axis_index("dp")
    flip = z // 2
    idx = jnp.stack([e, z, core, flip]).astype(jnp.int32)
    odd = lax.rem(z, 2)
    rows, model = inputs.shape[2], inputs.shape[3]
    length = rows * RING
    half_model = model // 2
    slots = 2 * (rows * 5 // 16)

    def place(z_index, d, which):
        micro = z_index % 2 if which == 0 else 1 - z_index % 2
        return (2 * micro + d) * 2 + z_index // 2

    routes_of = [
        [(zi * 2 + d, place(zi, d, which)) for zi in range(RING) for d in range(2)]
        for which in range(2)
    ]

    def leave(values):
        return [
            lax.ppermute(
                lax.dynamic_index_in_dim(values, odd if which == 0 else 1 - odd, 0, False),
                ("context", "dp"),
                routes_of[which],
            )
            for which in range(2)
        ]

    def go_home(values, which):
        return lax.ppermute(values, ("context", "dp"), [(b, a) for a, b in routes_of[which]])

    def at_home(*got):
        return jnp.where(odd == 0, jnp.stack(got), jnp.stack(got[::-1]))

    def columns_of(values, side):
        return lax.dynamic_slice_in_dim(values, side * half_model, half_model, values.ndim - 1)

    def in_order(mine, theirs, axis):
        pair = jnp.stack([mine, theirs], axis=axis), jnp.stack([theirs, mine], axis=axis)
        return jnp.where(core == 0, *pair)

    vectors = split3(jnp.concatenate([const_vec, norm_gains], axis=0).T)
    columns = jnp.concatenate(
        [route_weight, const_gate, *(part.astype(BF) for part in vectors)], axis=1
    )
    columns = jnp.pad(columns, ((0, 0), (0, 128 - columns.shape[1])))
    matrix = lax.dynamic_index_in_dim(qkv_weight, jnp.minimum(e, 2), 0, False)
    matrix = jnp.where(e == 3, out_weight, matrix)
    ring = handed_to_all(jnp.concatenate([matrix, columns], axis=1), "context")
    logit_parts = jnp.concatenate(split3(jnp.swapaxes(prev_logits[:, 0], 1, 2)), axis=2)
    ids = jnp.concatenate([jnp.swapaxes(routes[:, 0], 1, 2), segments], axis=1).astype(F32)
    ids = jnp.pad(ids, ((0, 0), (0, 5), (0, 2 * rows)))
    xa, xb = leave(
        jnp.concatenate([inputs[:, 0], logit_parts.astype(BF), ids.astype(BF)], axis=1)
    )
    ring, xa, xb = lax.optimization_barrier((ring, xa, xb))

    def my_part(side):
        return jnp.concatenate([columns_of(ring[:, :, :model], side), ring[:, :, model:]], axis=2)

    shared = in_order(my_part(core), across(my_part(1 - core)), 1)
    shared = shared.reshape(model, half_model + 128)
    columns = shared[:, half_model:]
    w_all = handed_to_all(shared[:, :half_model], "experts")
    theirs = across(jnp.stack([xa, xb]))

    stacked = jnp.stack([w_gate[0], w_up[0], w_down[0]])
    expert_w = lax.all_gather(after(stacked, ring), "context", axis=0)
    ca, cb = leave(after(cotangent[:, 0], shared))

    cosine, sine = (jnp.asarray(t) for t in rope_tables(length))
    q, k, v, normed_in, params, seg_row, seg_col = kernel_call(
        project_kernel,
        idx,
        [xa, xb, theirs, columns, w_all, cosine, sine],
        [((length, half_model), BF)] * 3
        + [((length, model), BF)]
        + [((16, model), F32), ((8, length), F32), ((length, 128), F32)],
        flops=2 * length * model * 3 * half_model,
        share=100,
        scratch=[pltpu.VMEM((length, model), BF)],
    )
    pairs = half_model // (2 * HEAD_DIM)
    lanes = 2 * HEAD_DIM
    by_pair = pl.BlockSpec((length, lanes), lambda h: (0, h))
    half_by_pair = pl.BlockSpec((length // 2, lanes), lambda h: (0, h))
    all_of = pl.BlockSpec(memory_space=pltpu.VMEM)
    lse_spec = pl.BlockSpec((1, 8, length), lambda h: (h, 0, 0))
    keep, send, lse = kernel_call(
        attend_kernel,
        idx,
        [q, k, v, seg_row, seg_col],
        [((length // 2, half_model), BF)] * 2 + [((pairs, 8, length), F32)],
        flops=4 * length * length * half_model,
        share=100,
        grid=(pairs,),
        in_specs=[by_pair] * 3 + [all_of] * 2,
        out_specs=[half_by_pair] * 2 + [lse_spec],
    )
    ca, cb = after((ca, cb), keep)
    (g_slots,) = kernel_call(
        grad_slots_kernel,
        idx,
        [xa, xb, ca, cb],
        [((RING, slots, model), BF)],
        flops=2 * RING * slots * 2 * rows * model,
    )
    g_mine = exchange(g_slots, "experts")
    recv = after(across(send), g_slots)

    hidden, ow_all, state, *sent = kernel_call(
        route_kernel,
        idx,
        [keep, recv, xa, xb, params, w_all[3], across(w_all[3])],
        [((2 * rows, model), F32), ((model, model), BF), ((24, 2 * rows), F32)]
        + [((slots + 16, model), BF)] * RING,
        flops=2 * 2 * rows * model * model + 2 * RING * slots * 2 * rows * model,
    )
    t_mine = [sent[0]] + [over(after(sent[k], g_mine), k) for k in range(1, RING)]
    g_theirs = across(g_mine)
    t_theirs = [across(t) for t in t_mine]

    count = 8 * slots
    chunk = w_gate.shape[2]
    hidden_units = RING * chunk
    lefts, acts, entry_keep, entry_send = kernel_call(
        expert_kernel,
        idx,
        [g_mine, g_theirs, expert_w, *t_mine, *t_theirs],
        [((2, count, model), BF), ((3, count, hidden_units), BF)]
        + [((RING, slots + 16, model), BF)] * 2,
        flops=10 * count * model * hidden_units,
        grid=(RING,),
        in_specs=[all_of] * 2
        + [pl.BlockSpec((1, 3, model, chunk), lambda j: (j, 0, 0, 0))]
        + [all_of] * 8,
        out_specs=[all_of, pl.BlockSpec((3, count, chunk), lambda j: (0, 0, j))] + [all_of] * 2,
        scratch=[
            pltpu.VMEM((count, model), BF),
            pltpu.VMEM((count, 128), F32),
            pltpu.VMEM((count, 3 * chunk), F32),
            pltpu.VMEM((count, 2 * chunk), BF),
            pltpu.VMEM((model, 2 * chunk), BF),
            pltpu.VMEM((count, model), F32),
            pltpu.VMEM((count, 128), F32),
        ],
    )

    def both_cores(kept, received):
        return (kept.astype(F32) + received.astype(F32)).astype(BF)

    entry_sum = both_cores(entry_keep, across(entry_send))
    entry_back = exchange(entry_sum, "experts")
    (far_grads,) = kernel_call(
        expert_grads_kernel,
        idx,
        [after(lefts, entry_sum), acts],
        [((RING, 3, model, chunk), BF)],
        flops=6 * count * model * hidden_units,
        grid=(3,),
        in_specs=[
            pl.BlockSpec((1, count, model), lambda j: (j // 2, 0, 0)),
            pl.BlockSpec((1, count, hidden_units), lambda j: (j, 0, 0)),
        ],
        out_specs=[pl.BlockSpec((RING, 1, model, chunk), lambda j: (0, j, 0, 0))],
    )
    out_keep, out_send = kernel_call(
        expert_out_kernel,
        idx,
        [after(acts, far_grads), expert_w],
        [((RING, slots, model), BF)] * 2,
        flops=2 * count * model * hidden_units,
        grid=(1,),
        in_specs=[
            pl.BlockSpec((1, count, hidden_units), lambda j: (2, 0, 0)),
            pl.BlockSpec((RING, 1, model, chunk), lambda j: (0, 2, 0, 0)),
        ],
        out_specs=[all_of] * 2,
        scratch=[pltpu.VMEM((model, hidden_units), BF)],
    )
    entry_back, out_send, far_grads = lax.optimization_barrier(
        (entry_back, out_send, far_grads)
    )
    expert_grads = lax.psum_scatter(far_grads, "context", scatter_dimension=0)

    grad_hidden, grad_low, ga_own, ga_send, logit_rows, small_grad = kernel_call(
        hidden_back_kernel,
        idx,
        [hidden, state, xa, xb, ca, cb, params, ow_all, entry_back],
        [((2 * rows, model), F32), ((2 * rows, model), BF)]
        + [((2 * rows, half_model), BF)] * 2
        + [((8, 2 * rows), F32), ((16, model), F32)],
        flops=2 * 2 * rows * model * model + 2 * RING * slots * 2 * rows * model,
    )
    ga_other = across(ga_send)
    out_sum = both_cores(out_keep, after(across(out_send), ga_send))
    out_back = exchange(out_sum, "experts")
    og_own, og_send = kernel_call(
        out_grad_kernel,
        idx,
        [keep, recv, grad_low],
        [((model, half_model), BF)] * 2,
        flops=2 * 2 * rows * model * model,
    )
    og_other = across(og_send)
    q = after(q, out_sum)
    shared_parts, pair_grads = [], []
    for h in range(pairs):
        at = lambda n, h=h: pl.BlockSpec((n, lanes), lambda i: (0, h))
        extra = 16 if h == 0 else 0
        grads, part = kernel_call(
            functools.partial(pair_back_kernel, h == 0),
            idx,
            [q, k, v, ga_own, ga_other, seg_row, seg_col, lse, cosine, sine, normed_in]
            + [og_own, og_other]
            + ([small_grad] if h == 0 else []),
            [((length, 3 * lanes), BF), ((RING, RING, model // RING + extra, lanes), BF)],
            flops=10 * length * length * lanes + 6 * length * model * lanes,
            grid=(1,),
            in_specs=[at(length)] * 3
            + [at(length // 2)] * 2
            + [all_of] * 2
            + [pl.BlockSpec((1, 8, length), lambda i, h=h: (h, 0, 0))]
            + [all_of] * 3
            + [at(model)] * 2
            + ([all_of] if h == 0 else []),
            out_specs=[all_of] * 2,
            scratch=[pltpu.VMEM((length, lanes), F32)] * 2,
        )
        pair_grads.append(grads)
        shared_parts.append(exchange(part, "experts"))
        if h == 0:
            q = after(q, out_back)
        if h == 1:
            q = after(q, shared_parts[0])
        if h == 2:
            w_all = after(w_all, shared_parts[1])
    depth = model // RING
    gn_keep, gn_send = kernel_call(
        normed_back_kernel,
        idx,
        [*pair_grads, w_all],
        [((2 * rows, model), BF)] * 2,
        flops=2 * length * model * 3 * half_model,
        scratch=[pltpu.VMEM((length, 3 * half_model), BF), pltpu.VMEM((model, 3 * half_model), BF)],
    )

    ia, ib = kernel_call(
        input_back_kernel,
        idx,
        [gn_keep, across(gn_send), grad_hidden, xa, xb, params],
        [((rows, model), BF)] * 2,
        flops=0,
    )
    oa, ob = kernel_call(
        output_kernel,
        idx,
        [after(hidden, ia), state, xa, xb, params, out_back, logit_rows],
        [((rows + 16, model), BF)] * 2,
        flops=4 * RING * slots * 2 * rows * model,
    )
    shared_parts[2] = after(shared_parts[2], ia, oa)
    sums = [part.astype(F32).sum(axis=0).astype(BF) for part in shared_parts]
    parts = jnp.concatenate([part[:, :depth] for part in sums], axis=2)
    rest = jnp.pad(sums[0][:, depth:], ((0, 0), (0, 0), (0, half_model - lanes)))
    parts = jnp.concatenate([parts, rest], axis=1)
    parts, ia, ib, oa, ob = lax.optimization_barrier((exchange(parts, "context"), ia, ib, oa, ob))
    ia, ib = go_home(ia, 0), go_home(ib, 1)
    homeward = (go_home(oa, 0), go_home(ob, 1))
    parts = parts.astype(F32).sum(axis=0)
    shard = depth // 2
    rest = parts[depth:]
    given = jnp.concatenate(
        [lax.dynamic_slice_in_dim(parts, (1 - core) * shard, shard, 0), rest], axis=0
    )
    taken = across(given.astype(BF)).astype(F32)
    grads = in_order(lax.dynamic_slice_in_dim(parts, core * shard, shard, 0), taken[:shard], 1)
    rest = jnp.pad(rest + taken[shard:], ((0, 0), (0, half_model)))
    grads = jnp.concatenate([grads.reshape(shard, model), rest], axis=0).astype(BF)
    expert_grads = [expert_grads[i].astype(F32)[None] for i in range(3)]
    grads, expert_grads = lax.optimization_barrier((grads, expert_grads))
    grads = handed_to_all(grads, "experts").astype(F32)
    small_grad = lax.dynamic_index_in_dim(grads, core, 0, False)[shard:, :shard]
    qkv_grad = grads[:3, :shard]
    gain_first = (qkv_grad * qkv_weight.astype(F32)).sum(axis=(0, 2)) / norm_gains[0]
    shared_grads = (
        qkv_grad,
        grads[3, :shard],
        jnp.stack([gain_first, small_grad[14]]),
        small_grad[:8].T,
        small_grad[8:12].T,
        small_grad[12:14],
    )
    homeward, shared_grads = lax.optimization_barrier((homeward, shared_grads))
    home = at_home(*homeward)
    output = home[:, None, :rows]
    logit_grad = home[:, rows : rows + 8].astype(F32).reshape(2, 8, 3, rows).sum(axis=2)
    logit_grad = jnp.swapaxes(logit_grad, 1, 2)[:, None]
    input_grad = at_home(ia, ib).astype(F32)[:, None]
    return (output, input_grad, logit_grad, *shared_grads, *expert_grads)


def whole_sequence_fits(mesh):
    return (mesh.shape["experts"], mesh.shape["context"], mesh.shape["dp"]) == (4, 4, 2)


def solution(mesh):
    local = chip_local if whole_sequence_fits(mesh) else general_local
    in_specs = (
        P(None, ("experts", "dp"), "context", None),
        P(None, ("experts", "dp"), "context", None),
        P(None, ("context", "dp"), None),
        P(("context", "dp"), None),
        P(None, ("context", "dp")),
        P(("context", "dp"), None),
        P(("context", "dp"), None),
        P(None, ("context", "dp")),
        P("experts", None, ("context", "dp")),
        P("experts", None, ("context", "dp")),
        P("experts", None, ("context", "dp")),
        P(None, ("experts", "dp"), "context", None),
        P(None, ("experts", "dp"), "context", None),
        P(None, ("experts", "dp"), "context"),
    )
    out_specs = (
        P(None, ("experts", "dp"), "context", None),
        P(None, ("experts", "dp"), "context", None),
        P(None, ("experts", "dp"), "context", None),
        P(None, ("context", "dp"), None),
        P(("context", "dp"), None),
        P(None, ("context", "dp")),
        P(("context", "dp"), None),
        P(("context", "dp"), None),
        P(None, ("context", "dp")),
        P("experts", None, ("context", "dp")),
        P("experts", None, ("context", "dp")),
        P("experts", None, ("context", "dp")),
    )
    return jax.shard_map(local, mesh=mesh, in_specs=in_specs, out_specs=out_specs, check_vma=False)
```
